128 devices in a mesh: blk: 16 (over z, y_lo, core), mp: 8 (over x, y_hi).
Axes of the slice: x: 4, y: 4 (y_hi: 2, y_lo: 2; y = y_hi * 2 + y_lo), z: 4, core: 2. Of those that a mesh axis runs over, the one named last changes fastest.
Arguments:
- img_feat: bfloat16 [16384, 6144], P('blk', 'mp'), may hold values from -60 to 60
- txt_feat: bfloat16 [16384, 4096], P('blk', 'mp'), may hold values from -60 to 60
- img_weight: bfloat16 [6144, 1024], P('mp'), may hold values from -0.5 to 2
- txt_weight: bfloat16 [4096, 1024], P('mp'), may hold values from -0.5 to 2
- natural_exponent_multiplier: float32 [1], replicated, may hold values from 2.3 to 3
- bias: float32 [1], replicated, may hold values from -3 to -1
Outputs:
- img_feat_grad: bfloat16 [16384, 6144], P('blk', 'mp')
- txt_feat_grad: bfloat16 [16384, 4096], P('blk', 'mp')
- img_weight_grad: float32 [6144, 1024], P('mp', 'blk')
- txt_weight_grad: float32 [4096, 1024], P('mp', 'blk')
The draws below stay inside these ranges and needn't reach their ends.
All inputs are finite; a program needn't handle non-finite values.
Results may differ from the reference program's by a relative error of at most 0.019.
Values may be sent and summed in bfloat16 or wider, within the bound.
No kernel may reach another device: no remote copies, remote signals or barrier semaphores. Data moves between devices by JAX's collectives and lax.ppermute only.
A program may use at most 128 MiB of HBM per device.

```python
import math
import jax
import jax.numpy as jnp
from jax import lax

DI = 6144
DT = 4096
E = 1024
GRP = 1024
BATCH = 16384
N_BLK = 16


def shared_latent(key):
    key = jax.random.fold_in(key, 101)
    own_key, load_key, line_key = jax.random.split(key, 3)
    own_part = jnp.clip(jax.random.normal(own_key, (BATCH, E), jnp.float32), -4.0, 4.0)
    row_loads = jnp.clip(jax.random.normal(load_key, (BATCH, 2), jnp.float32), -3.0, 3.0)
    directions = jnp.clip(jax.random.normal(line_key, (2, E), jnp.float32), -3.0, 3.0)
    common_part = row_loads[:, 0:1] * directions[0:1, :] + row_loads[:, 1:2] * directions[1:2, :]
    return own_part * math.sqrt(0.5) + common_part * 0.5


def tower_rows(latent, noise_part, row_scales, width):
    columns = jnp.arange(width, dtype=jnp.int32) % E
    mixed = noise_part + latent[:, columns]
    return jnp.clip(mixed * row_scales, -60.0, 60.0).astype(jnp.bfloat16)


def comb_weight(key, row_count):
    noise_part = jnp.clip(jax.random.normal(key, (row_count, E), jnp.float32), -4.0, 4.0) * row_count ** (-0.5)
    row_ids = jnp.arange(row_count, dtype=jnp.int32)[:, None] % E
    col_ids = jnp.arange(E, dtype=jnp.int32)[None, :]
    comb_part = jnp.where(row_ids == col_ids, 1.5 * E / row_count, 0.0).astype(jnp.float32)
    return (noise_part + comb_part).astype(jnp.bfloat16)


def draw_img_feat(key, part):
    latent = shared_latent(key)
    key = jax.random.fold_in(key, 11)
    base_key, scale_key = jax.random.split(key)
    noise_part = jnp.clip(jax.random.normal(base_key, (BATCH, DI), jnp.float32), -3.0, 3.0)
    spread = math.log(10.0)
    row_scales = jnp.exp(jax.random.uniform(scale_key, (BATCH, 1), jnp.float32, 0.0, spread))
    return tower_rows(latent, noise_part, row_scales, DI)


def draw_txt_feat(key, part):
    latent = shared_latent(key)
    key = jax.random.fold_in(key, 23)
    base_key, scale_key = jax.random.split(key)
    noise_part = jnp.clip(jax.random.normal(base_key, (BATCH, DT), jnp.float32), -3.0, 3.0)
    spread = math.log(10.0)
    row_scales = jnp.exp(jax.random.uniform(scale_key, (BATCH, 1), jnp.float32, 0.0, spread))
    return tower_rows(latent, noise_part, row_scales, DT)


def draw_img_weight(key, part):
    key = jax.random.fold_in(key, 37)
    return comb_weight(key, DI)


def draw_txt_weight(key, part):
    key = jax.random.fold_in(key, 41)
    return comb_weight(key, DT)


def setup_inputs(seed: int = 0) -> dict:
    splits = jax.random.split(jax.random.key(seed), 7)
    img_feat = draw_img_feat(jax.random.fold_in(splits[6], 71), 0)
    txt_feat = draw_txt_feat(jax.random.fold_in(splits[6], 71), 0)
    img_weight = draw_img_weight(jax.random.fold_in(splits[6], 71), 0)
    txt_weight = draw_txt_weight(jax.random.fold_in(splits[6], 71), 0)
    natural_exponent_multiplier = jnp.clip(jax.random.uniform(splits[4], (1,), jnp.float32, 2.3, 3.0), 2.3, 3.0)
    bias = jnp.clip(jax.random.uniform(splits[5], (1,), jnp.float32, -3.0, -1.0), -3.0, -1.0)
    return dict(img_feat=img_feat, txt_feat=txt_feat, img_weight=img_weight, txt_weight=txt_weight, natural_exponent_multiplier=natural_exponent_multiplier, bias=bias)


EPS = 1e-06

def unit_rows(embedded):
    inverse = lax.rsqrt(lax.optimization_barrier(jnp.sum(embedded * embedded, axis=1, keepdims=True)) + EPS)
    return (embedded * inverse, inverse)

def norm_back(unit_grad, unit_full, inverse):
    return inverse * (unit_grad - unit_full * lax.optimization_barrier(jnp.sum(unit_full * unit_grad, axis=1, keepdims=True)))

def cross_contributions(picture_sample_group, caption_submatrix, matching_targets, sharpness_multiplier, additive_offset):
    cosine_affinities = lax.dot_general(caption_submatrix, picture_sample_group, (((1,), (1,)), ((), ())), preferred_element_type=jnp.float32)
    matching_affinities = sharpness_multiplier * cosine_affinities + additive_offset
    derivative_multiplier = (-matching_targets * jax.nn.sigmoid(-matching_targets * matching_affinities) * sharpness_multiplier).astype(jnp.bfloat16)
    picture_portion = lax.dot_general(derivative_multiplier, caption_submatrix, (((0,), (0,)), ((), ())), preferred_element_type=jnp.float32)
    caption_portion = jnp.dot(derivative_multiplier, picture_sample_group, preferred_element_type=jnp.float32)
    return (picture_portion, caption_portion)

def reference(img_feat, txt_feat, img_weight, txt_weight, natural_exponent_multiplier, bias):
    sharpness_multiplier = jnp.exp(natural_exponent_multiplier[0])
    additive_offset = bias[0]
    img_emb = jnp.dot(img_feat, img_weight, preferred_element_type=jnp.float32)
    txt_emb = jnp.dot(txt_feat, txt_weight, preferred_element_type=jnp.float32)
    img_unit, img_inv = unit_rows(img_emb)
    txt_unit, txt_inv = unit_rows(txt_emb)
    picture_sample_group = img_unit.astype(jnp.bfloat16)
    text_blocks = txt_unit.astype(jnp.bfloat16).reshape(N_BLK, GRP, E)
    image_ids = jnp.arange(BATCH, dtype=jnp.int32)[None, :]

    def visit_block(running, inputs):
        caption_submatrix, block_index = inputs
        text_ids = block_index * GRP + jnp.arange(GRP, dtype=jnp.int32)[:, None]
        matching_targets = jnp.where(text_ids == image_ids, 1.0, -1.0).astype(jnp.float32)
        picture_portion, caption_portion = cross_contributions(picture_sample_group, caption_submatrix, matching_targets, sharpness_multiplier, additive_offset)
        return (running + picture_portion, caption_portion)
    img_ugrad, txt_pieces = lax.scan(visit_block, jnp.zeros((BATCH, E), jnp.float32), (text_blocks, jnp.arange(N_BLK, dtype=jnp.int32)))
    txt_ugrad = txt_pieces.reshape(BATCH, E)
    img_egrad = norm_back(img_ugrad, img_unit, img_inv).astype(jnp.bfloat16)
    txt_egrad = norm_back(txt_ugrad, txt_unit, txt_inv).astype(jnp.bfloat16)
    img_feat_grad = lax.dot_general(img_egrad, img_weight, (((1,), (1,)), ((), ())), preferred_element_type=jnp.float32).astype(jnp.bfloat16)
    txt_feat_grad = lax.dot_general(txt_egrad, txt_weight, (((1,), (1,)), ((), ())), preferred_element_type=jnp.float32).astype(jnp.bfloat16)
    img_weight_grad = lax.dot_general(img_feat, img_egrad, (((0,), (0,)), ((), ())), preferred_element_type=jnp.float32)
    txt_weight_grad = lax.dot_general(txt_feat, txt_egrad, (((0,), (0,)), ((), ())), preferred_element_type=jnp.float32)
    return (img_feat_grad, txt_feat_grad, img_weight_grad, txt_weight_grad)
```

```python
import jax
import jax.numpy as jnp
from jax import lax
from jax.experimental import pallas as pl
from jax.experimental.pallas import tpu as pltpu
from jax.sharding import PartitionSpec as P

EPS = 1e-06
BF16 = jnp.bfloat16
F32 = jnp.float32
VMEM_LIMIT = 48 * 1024 * 1024


def swap(value, axis, offset):
    count = lax.axis_size(axis)
    return lax.ppermute(value, axis, [(i, i ^ offset) for i in range(count)])


def shape(*dims, dtype=BF16):
    return jax.ShapeDtypeStruct(dims, dtype)


def call(name, body, outs, ins, flops=0, grid_spec=None, scratch=()):
    if grid_spec is None:
        layout = dict(scratch_shapes=list(scratch))
    else:
        layout = dict(grid_spec=grid_spec)
    moved = sum(a.size * a.dtype.itemsize for a in list(ins) + list(outs))
    return pl.pallas_call(
        body,
        out_shape=outs,
        compiler_params=pltpu.CompilerParams(vmem_limit_bytes=VMEM_LIMIT),
        cost_estimate=pl.CostEstimate(flops=flops, bytes_accessed=moved, transcendentals=0),
        name=name,
        **layout,
    )(*ins)


def wide(ref, block=None):
    return (ref[...] if block is None else ref[block]).astype(F32)


def embed(name, feat, weight, column, blocks, tile=256):
    rows, width = feat.shape
    columns = weight.shape[1]
    own = rows // blocks

    def body(column_ref, feat_ref, weight_ref, p01, p23, p67, p4, p5, product):
        product[...] = jnp.dot(feat_ref[...], weight_ref[...], preferred_element_type=F32).astype(BF16)

        def part(k):
            return product[pl.ds(pl.multiple_of((column_ref[0] ^ k) * own, own), own)]

        for k in range(2):
            p01[k] = part(k)
            p23[k] = part(2 + k)
            p67[k] = part(6 + k)
        p4[...] = part(4)
        p5[...] = part(5)

    pair = pl.BlockSpec((2, own, tile), lambda i, c: (0, 0, i))
    single = pl.BlockSpec((own, tile), lambda i, c: (0, i))
    grid_spec = pltpu.PrefetchScalarGridSpec(
        num_scalar_prefetch=1,
        grid=(columns // tile,),
        in_specs=[
            pl.BlockSpec((rows, width), lambda i, c: (0, 0)),
            pl.BlockSpec((width, tile), lambda i, c: (0, i)),
        ],
        out_specs=[pair, pair, pair, single, single],
        scratch_shapes=[pltpu.VMEM((rows, tile), BF16)],
    )
    outs = [shape(2, own, columns)] * 3 + [shape(own, columns)] * 2
    return call(name, body, outs, (column, feat, weight), 2 * rows * width * columns, grid_spec)


def relay_add(p23, p67, r4, r5, out23, out67):
    out23[0] = (wide(p23, 0) + wide(r4)).astype(BF16)
    out23[1] = p23[1]
    out67[0] = p67[0]
    out67[1] = (wide(p67, 1) + wide(r5)).astype(BF16)


def unit_of(embedded):
    inverse = lax.rsqrt(jnp.sum(embedded * embedded, axis=1, keepdims=True) + EPS)
    return embedded * inverse, inverse


def norm_back(unit_grad, embedded):
    unit, inverse = unit_of(embedded)
    return inverse * (unit_grad - unit * jnp.sum(unit * unit_grad, axis=1, keepdims=True))


def flat(ref):
    return ref[...].reshape(-1, ref.shape[-1])


def rows_of(*refs):
    return jnp.concatenate([flat(ref) for ref in refs], axis=0)


def factors(scale, bias, txt, img):
    affinity = lax.dot_general(txt, img, (((1,), (1,)), ((), ())), preferred_element_type=F32)
    logits = scale * affinity + bias
    return logits, (scale / (1.0 + jnp.exp(-logits))).astype(BF16)


def product(first, second):
    return jnp.dot(first, second, preferred_element_type=F32)


def pair_call(name, body, outs, scale, bias, arrays, flops):
    smem = pl.BlockSpec(memory_space=pltpu.SMEM)
    vmem = pl.BlockSpec(memory_space=pltpu.VMEM)
    moved = sum(a.size * a.dtype.itemsize for a in list(arrays) + outs)
    return pl.pallas_call(
        body,
        in_specs=[smem, smem] + [vmem] * len(arrays),
        out_shape=outs,
        compiler_params=pltpu.CompilerParams(vmem_limit_bytes=VMEM_LIMIT),
        cost_estimate=pl.CostEstimate(flops=flops, bytes_accessed=moved, transcendentals=0),
        name=name,
    )(scale, bias, *arrays)


def pairs_near(scale, bias, even, odd, near):
    own, width = even.shape[-2:]
    texts, images = 12 * own, 6 * own

    def body(scale_ref, bias_ref, even, odd, u01, u23, u67, out, flipped):
        scale, bias = scale_ref[0], bias_ref[0]
        for t, txt_ref in enumerate((even, odd)):
            rows = slice(t * 6 * own, (t + 1) * 6 * own)
            for i, img_ref in enumerate((u01, u23, u67)):
                columns = slice(i * 2 * own, (i + 1) * 2 * own)
                logits, factor = factors(scale, bias, flat(txt_ref), flat(img_ref))
                if t == 0 and i == 0:
                    row = lax.broadcasted_iota(jnp.int32, logits.shape, 0)
                    column = lax.broadcasted_iota(jnp.int32, logits.shape, 1)
                    pull = (-scale / (1.0 + jnp.exp(logits))).astype(BF16)
                    factor = jnp.where((row == column) & (row < own), pull, factor)
                out[rows, columns] = factor
                flipped[columns, rows] = factor.T

    outs = [shape(texts, images), shape(images, texts)]
    return pair_call("pairs_near", body, outs, scale, bias, (even, odd, *near), 2 * texts * images * width)


def pairs_far(scale, bias, even, odd, far, near, u4, u5):
    own, width = u4.shape
    texts, images = 12 * own, 6 * own

    def body(scale_ref, bias_ref, even, odd, a8, a10, a9, a11, u01, u23, u67, u4, u5, near_far, far_near, far_flip, far_far, g4, g5):
        scale, bias = scale_ref[0], bias_ref[0]
        far_images = rows_of(u4, u5)
        far_texts = rows_of(a8, a10, a9, a11)
        total = jnp.zeros((2 * own, width), F32)
        for t, txt_ref in enumerate((even, odd)):
            factor = factors(scale, bias, flat(txt_ref), far_images)[1]
            near_far[t * 6 * own : (t + 1) * 6 * own] = factor
            total = total + product(factor.T, flat(txt_ref))
        factor = factors(scale, bias, far_texts, far_images)[1]
        far_far[...] = factor
        total = total + product(factor.T, far_texts)
        g4[...] = total[:own].astype(BF16)
        g5[...] = total[own:].astype(BF16)
        for i, img_ref in enumerate((u01, u23, u67)):
            columns = slice(i * 2 * own, (i + 1) * 2 * own)
            factor = factors(scale, bias, far_texts, flat(img_ref))[1]
            far_near[:, columns] = factor
            far_flip[columns] = factor.T

    outs = [
        shape(texts, 2 * own),
        shape(4 * own, images),
        shape(images, 4 * own),
        shape(4 * own, 2 * own),
        shape(own, width),
        shape(own, width),
    ]
    flops = 2 * width * own * own * (16 * 2 * 2 + 4 * 6)
    return pair_call("pairs_far", body, outs, scale, bias, (even, odd, *far, *near, u4, u5), flops)


def text_grads(out, start, far_start, near_near, near_far, far_near, far_far, image_refs, own):
    width = out.shape[-1]
    near_rows = jnp.concatenate(
        [near_near[start : start + 6 * own], near_far[start : start + 6 * own]], axis=1
    )
    far_rows = jnp.concatenate(
        [far_near[far_start : far_start + 2 * own], far_far[far_start : far_start + 2 * own]], axis=1
    )
    all_rows = jnp.concatenate([near_rows, far_rows], axis=0)
    for at in range(0, width, 256):
        images = jnp.concatenate(
            [ref[:, :, at : at + 256].reshape(-1, 256) for ref in image_refs[:3]]
            + [ref[:, at : at + 256] for ref in image_refs[3:]],
            axis=0,
        )
        out[:, :, at : at + 256] = product(all_rows, images).astype(BF16).reshape(8, own, 256)


def pairs_odd(scale, bias, near_near, near_far, far_near, far_far, images):
    own, width = images[-1].shape

    def body(scale_ref, bias_ref, near_near, near_far, far_near, far_far, u01, u23, u67, u4, u5, out):
        text_grads(out, 6 * own, 2 * own, near_near, near_far, far_near, far_far, (u01, u23, u67, u4, u5), own)

    flops = 2 * 8 * 8 * own * own * width
    arrays = (near_near, near_far, far_near, far_far, *images)
    return pair_call("pairs_odd", body, [shape(8, own, width)], scale, bias, arrays, flops)[0]


def pairs_rest(scale, bias, near_near, near_far, far_near, far_far, images, near_flip, far_flip, even, odd, far):
    own, width = images[-1].shape

    def body(*refs):
        near_near, near_far, far_near, far_far = refs[2:6]
        image_refs, (near_flip, far_flip, even, odd), far = refs[6:11], refs[11:15], refs[15:19]
        g01, g23, g67, out = refs[19:]
        text_grads(out, 0, 0, near_near, near_far, far_near, far_far, image_refs, own)
        for at in range(0, width, 256):
            columns = slice(at, at + 256)
            texts = [ref[:, :, columns].reshape(-1, 256) for ref in (even, odd)]
            far_texts = jnp.concatenate([ref[:, columns] for ref in far], axis=0)
            total = product(near_flip[:, : 6 * own], texts[0])
            total = total + product(near_flip[:, 6 * own :], texts[1])
            total = total + product(far_flip[...], far_texts)
            total = total.astype(BF16).reshape(3, 2, own, 256)
            g01[:, :, columns] = total[0]
            g23[:, :, columns] = total[1]
            g67[:, :, columns] = total[2]

    flops = 2 * own * own * width * (8 * 8 + 6 * 16)
    arrays = (near_near, near_far, far_near, far_far, *images, near_flip, far_flip, even, odd, *far)
    outs = [shape(2, own, width)] * 3 + [shape(8, own, width)]
    return pair_call("pairs_rest", body, outs, scale, bias, arrays, flops)


def in_index_order(e01, e23, e67, e4, e5):
    return [e01.at[0], e01.at[1], e23.at[0], e23.at[1], e4, e5, e67.at[0], e67.at[1]]


def weight_part(name, column, place, pieces, feat):
    own, width = pieces[-1].shape
    rows, features = feat.shape
    strip = width // 16
    tile = 256

    def body(column_ref, place_ref, e01, e23, e67, e4, e5, feat_ref, same, other, flipped, moved, result):
        @pl.when(pl.program_id(0) == 0)
        def _():
            for k, block in enumerate(in_index_order(e01, e23, e67, e4, e5)):
                flipped[:, k * own : (k + 1) * own] = block[...].T

        for k in range(rows // own):
            start = pl.multiple_of((column_ref[0] ^ k) * own, own)
            moved[k * own : (k + 1) * own] = feat_ref[pl.ds(start, own)]
        result[...] = product(flipped[...], moved[...]).astype(BF16)
        core = place_ref[0] & 1
        for j in range(8):
            mine = pl.multiple_of((2 * j + core) * strip, strip)
            theirs = pl.multiple_of((2 * j + 1 - core) * strip, strip)
            same[j] = result[pl.ds(mine, strip)]
            other[j] = result[pl.ds(theirs, strip)]

    def whole(array):
        zeros = (0,) * array.ndim
        return pl.BlockSpec(array.shape, lambda i, c, p: zeros)

    strips = pl.BlockSpec((8, strip, tile), lambda i, c, p: (0, 0, i))
    grid_spec = pltpu.PrefetchScalarGridSpec(
        num_scalar_prefetch=2,
        grid=(features // tile,),
        in_specs=[whole(piece) for piece in pieces] + [pl.BlockSpec((rows, tile), lambda i, c, p: (0, i))],
        out_specs=[strips, strips],
        scratch_shapes=[
            pltpu.VMEM((width, rows), BF16),
            pltpu.VMEM((rows, tile), BF16),
            pltpu.VMEM((width, tile), BF16),
        ],
    )
    outs = [shape(8, strip, features)] * 2
    return call(name, body, outs, (column, place, *pieces, feat), 2 * rows * width * features, grid_spec)


def feature_grad(name, column, pieces, weight):
    own, width = pieces[-1].shape
    features = weight.shape[0]
    rows = 8 * own
    tile = 256

    def body(column_ref, e01, e23, e67, e4, e5, weight_ref, out):
        egrad = rows_of(e01, e23, e4, e5, e67)
        result = lax.dot_general(
            egrad, weight_ref[...], (((1,), (1,)), ((), ())), preferred_element_type=F32
        ).astype(BF16)
        for k in range(rows // own):
            start = pl.multiple_of((column_ref[0] ^ k) * own, own)
            out[pl.ds(start, own)] = result[k * own : (k + 1) * own]

    def whole(array):
        zeros = (0,) * array.ndim
        return pl.BlockSpec(array.shape, lambda i, c: zeros)

    grid_spec = pltpu.PrefetchScalarGridSpec(
        num_scalar_prefetch=1,
        grid=(features // tile,),
        in_specs=[whole(piece) for piece in pieces] + [pl.BlockSpec((tile, width), lambda i, c: (i, 0))],
        out_specs=[pl.BlockSpec((rows, tile), lambda i, c: (0, i))],
    )
    outs = shape(rows, features)
    moved = (column, *pieces, weight)
    return call(name, body, [outs], moved, 2 * rows * width * features, grid_spec)[0]


def sum_weight(same, other):
    def body(same_ref, got_ref, out):
        out[...] = (wide(same_ref) + wide(got_ref)).astype(BF16)

    got = swap(other, "blk", 1)
    (chip,) = call("weight_chip", body, [shape(*same.shape)], (same, got))
    groups = [list(range(core, 16, 2)) for core in range(2)]
    parts = lax.all_to_all(chip, "blk", 0, 0, axis_index_groups=groups, tiled=True)
    return jnp.sum(parts.astype(F32), axis=0).T


def local(img_feat, txt_feat, img_weight, txt_weight, natural_exponent_multiplier, bias):
    scale = jnp.exp(natural_exponent_multiplier)
    blocks = lax.axis_size("mp")
    column = lax.axis_index("mp").astype(jnp.int32)[None]
    place = lax.axis_index("blk").astype(jnp.int32)[None]
    own = img_feat.shape[0] // blocks
    width = img_weight.shape[1]
    one, two = (own, width), (2, own, width)

    t01, t23, t67, t4, t5 = embed("embed_text", txt_feat, txt_weight, column, blocks)
    t4, t5 = swap(t4, "mp", 6), swap(t5, "mp", 2)
    i01, i23, i67, i4, i5 = embed("embed_image", img_feat, img_weight, column, blocks)
    t23, t67 = call("relay_text", relay_add, [shape(*two)] * 2, (t23, t67, t4, t5))
    t23, t67 = swap(t23, "mp", 2), swap(t67, "mp", 6)
    i4, i5 = swap(i4, "mp", 6), swap(i5, "mp", 2)

    def second(t01, t23, t67, i23, i67, i4, i5, t0_out, t1_out, i23_out, i67_out):
        t0_out[...] = wide(t01, 0) + wide(t23, 0) + wide(t67, 0)
        t1_out[...] = (wide(t01, 1) + wide(t23, 1) + wide(t67, 1)).astype(BF16)
        relay_add(i23, i67, i4, i5, i23_out, i67_out)

    t0, t1, i23, i67 = call(
        "sums_second",
        second,
        [shape(*one, dtype=F32), shape(*one), shape(*two), shape(*two)],
        (t01, t23, t67, i23, i67, i4, i5),
    )
    t1 = swap(t1, "mp", 1)
    i23, i67 = swap(i23, "mp", 2), swap(i67, "mp", 6)

    def third(t0, t1, i01, i23, i67, text_out, unit_out, i01_out):
        embedded = t0[...] + wide(t1)
        text_out[...] = embedded
        unit_out[...] = unit_of(embedded)[0].astype(BF16)
        for k in range(2):
            i01_out[k] = (wide(i01, k) + wide(i23, k) + wide(i67, k)).astype(BF16)

    txt_emb, a0, i01 = call(
        "sums_third",
        third,
        [shape(*one, dtype=F32), shape(*one), shape(*two)],
        (t0, t1, i01, i23, i67),
    )
    a2 = swap(a0, "blk", 2)
    got01 = swap(i01, "mp", 1)

    def fourth(a0, a2, i01, got01, a02_out, emb_out, unit_out):
        a02_out[0] = a0[...]
        a02_out[1] = a2[...]
        for k in range(2):
            embedded = wide(i01, k) + wide(got01, 1 - k)
            emb_out[k] = embedded
            unit_out[k] = unit_of(embedded)[0].astype(BF16)

    a02, img_emb, u01 = call(
        "sums_fourth",
        fourth,
        [shape(*two), shape(*two, dtype=F32), shape(*two)],
        (a0, a2, i01, got01),
    )

    a46, a1214 = swap(a02, "blk", 4), swap(a02, "blk", 12)
    u23, u67 = swap(u01, "mp", 2), swap(u01, "mp", 6)

    def joined(a02, a46, a1214, u23, u67, even_out, a4_out, a14_out, u2_out, u7_out):
        even_out[0:2] = a02[...]
        even_out[2:4] = a46[...]
        even_out[4:6] = a1214[...]
        a4_out[...] = a46[0]
        a14_out[...] = a1214[1]
        u2_out[...] = u23[0]
        u7_out[...] = u67[1]

    even, a8, a10, u4, u5 = call(
        "join", joined, [shape(6, *one)] + [shape(*one)] * 4, (a02, a46, a1214, u23, u67)
    )
    odd = swap(even, "blk", 1)
    a8, a10 = swap(a8, "blk", 12), swap(a10, "blk", 4)
    u4, u5 = swap(u4, "mp", 6), swap(u5, "mp", 2)
    a9, a11 = swap(a8, "blk", 1), swap(a10, "blk", 1)
    near, far, images = (u01, u23, u67), (a8, a10, a9, a11), (u01, u23, u67, u4, u5)
    near_near, near_flip = pairs_near(scale, bias, even, odd, near)
    near_far, far_near, far_flip, far_far, g4, g5 = pairs_far(scale, bias, even, odd, far, near, u4, u5)
    g4, g5 = swap(g4, "mp", 6), swap(g5, "mp", 2)
    factor_parts = (near_near, near_far, far_near, far_far)
    odd_sum = pairs_odd(scale, bias, *factor_parts, images)
    odd_got = swap(odd_sum, "blk", 1)
    g01, g23, g67, even_sum = pairs_rest(
        scale, bias, *factor_parts, images, near_flip, far_flip, even, odd, far
    )

    def fifth(even, got, g23, g67, g4, g5, p8, p10, g23_out, g67_out):
        p8[...] = (wide(even, 6) + wide(got, 6)).astype(BF16)
        p10[...] = (wide(even, 7) + wide(got, 7)).astype(BF16)
        relay_add(g23, g67, g4, g5, g23_out, g67_out)

    p8, p10, g23, g67 = call(
        "sums_fifth",
        fifth,
        [shape(*one), shape(*one), shape(*two), shape(*two)],
        (even_sum, odd_got, g23, g67, g4, g5),
    )
    g23, g67 = swap(g23, "mp", 2), swap(g67, "mp", 6)
    p8, p10 = swap(p8, "blk", 12), swap(p10, "blk", 4)

    def sixth(even, got, p8, p10, g01, g23, g67, p02, p46, p1214, g01_out):
        for k in range(2):
            p02[k] = (wide(even, k) + wide(got, k)).astype(BF16)
            g01_out[k] = (wide(g01, k) + wide(g23, k) + wide(g67, k)).astype(BF16)
        p46[0] = (wide(even, 2) + wide(got, 2) + wide(p8)).astype(BF16)
        p46[1] = (wide(even, 3) + wide(got, 3)).astype(BF16)
        p1214[0] = (wide(even, 4) + wide(got, 4)).astype(BF16)
        p1214[1] = (wide(even, 5) + wide(got, 5) + wide(p10)).astype(BF16)

    p02, p46, p1214, g01 = call(
        "sums_sixth", sixth, [shape(*two)] * 4, (even_sum, odd_got, p8, p10, g01, g23, g67)
    )
    g01_got = swap(g01, "mp", 1)
    p46, p1214 = swap(p46, "blk", 4), swap(p1214, "blk", 12)

    def seventh(p02, p46, p1214, g01, g01_got, img_emb, p0_out, p2_out, e01_out):
        p0_out[...] = wide(p02, 0) + wide(p46, 0) + wide(p1214, 0)
        p2_out[...] = (wide(p02, 1) + wide(p46, 1) + wide(p1214, 1)).astype(BF16)
        for k in range(2):
            unit_grad = wide(g01, k) + wide(g01_got, 1 - k)
            e01_out[k] = norm_back(unit_grad, img_emb[k]).astype(BF16)

    p0, p2, e01 = call(
        "sums_seventh",
        seventh,
        [shape(*one, dtype=F32), shape(*one), shape(*two)],
        (p02, p46, p1214, g01, g01_got, img_emb),
    )
    p2 = swap(p2, "blk", 2)
    e23, e67 = swap(e01, "mp", 2), swap(e01, "mp", 6)

    def eighth(p0, p2, txt_emb, out):
        out[...] = norm_back(p0[...] + wide(p2), txt_emb[...]).astype(BF16)

    (d0,) = call("sums_eighth", eighth, [shape(*one)], (p0, p2, txt_emb))
    d1 = swap(d0, "mp", 1)

    def ninth(d0, d1, e23, e67, d01_out, e2_out, e7_out):
        d01_out[0] = d0[...]
        d01_out[1] = d1[...]
        e2_out[...] = e23[0]
        e7_out[...] = e67[1]

    d01, e4, e5 = call("join_ninth", ninth, [shape(*two), shape(*one), shape(*one)], (d0, d1, e23, e67))
    e4, e5 = swap(e4, "mp", 6), swap(e5, "mp", 2)
    d23, d67 = swap(d01, "mp", 2), swap(d01, "mp", 6)
    e_all = (e01, e23, e67, e4, e5)
    img_weight_grad = sum_weight(*weight_part("weight_image", column, place, e_all, img_feat))
    d4, d5 = swap(d23[0], "mp", 6), swap(d67[1], "mp", 2)
    d_all = (d01, d23, d67, d4, d5)
    txt_weight_grad = sum_weight(*weight_part("weight_text", column, place, d_all, txt_feat))
    return (
        feature_grad("feature_image", column, e_all, img_weight),
        feature_grad("feature_text", column, d_all, txt_weight),
        img_weight_grad,
        txt_weight_grad,
    )


def solution(mesh):
    return jax.shard_map(
        local,
        mesh=mesh,
        in_specs=(P("blk", "mp"), P("blk", "mp"), P("mp", None), P("mp", None), P(), P()),
        out_specs=(P("blk", "mp"), P("blk", "mp"), P("mp", "blk"), P("mp", "blk")),
        check_vma=False,
    )
```

```python
import jax
import jax.numpy as jnp
from jax import lax
from jax.experimental import pallas as pl
from jax.experimental.pallas import tpu as pltpu
from jax.sharding import PartitionSpec as P

EPS = 1e-06
BF16 = jnp.bfloat16
F32 = jnp.float32
MIB = 1024 * 1024
ORDER_COST = 12 * 10**9
NEAR_FAR = (0, 1, 2, 3, 6, 7, 4, 5)


def swap(value, axis, offset):
    count = lax.axis_size(axis)
    return lax.ppermute(value, axis, [(i, i ^ offset) for i in range(count)])


def shape(*dims, dtype=BF16):
    return jax.ShapeDtypeStruct(dims, dtype)


def call(name, body, outs, ins, flops=0, limit=10, after=None, in_specs=None, scratch=()):
    ins, specs = list(ins), in_specs or [pl.BlockSpec(memory_space=pltpu.VMEM)] * len(ins)
    run = body
    if after is not None:
        after = list(after) if isinstance(after, tuple) else [after]
        ins, specs = after + ins, [pl.BlockSpec(memory_space=pltpu.VMEM)] * len(after) + list(specs)

        def run(*refs):
            body(*refs[len(after) :])

    moved = sum(a.size * a.dtype.itemsize for a in ins + list(outs))
    return pl.pallas_call(
        run,
        out_shape=outs,
        in_specs=specs,
        scratch_shapes=list(scratch),
        compiler_params=pltpu.CompilerParams(vmem_limit_bytes=limit * MIB),
        cost_estimate=pl.CostEstimate(flops=flops, bytes_accessed=moved, transcendentals=0),
        name=name,
    )(*ins)


def tiles(count, size, body):
    def step(index, carry):
        body(pl.ds(pl.multiple_of(index * size, size), size))
        return carry

    lax.fori_loop(0, count, step, 0)


def wide(ref, block=None):
    return (ref[...] if block is None else ref[block]).astype(F32)


def embed(name, feat, weight, column, blocks, tile=256):
    rows, width = feat.shape
    columns = weight.shape[1]
    own = rows // blocks

    def body(column_ref, feat_ref, weight_ref, p01, p23, p67, p4, p5, result):
        def part(k):
            return result[pl.ds(pl.multiple_of((column_ref[0] ^ k) * own, own), own)]

        def columns_at(here):
            result[...] = product(feat_ref[...], weight_ref[:, here]).astype(BF16)
            for k in range(2):
                p01[k, :, here] = part(k)
                p23[k, :, here] = part(2 + k)
                p67[k, :, here] = part(6 + k)
            p4[:, here] = part(4)
            p5[:, here] = part(5)

        tiles(columns // tile, tile, columns_at)

    outs = [shape(2, own, columns)] * 3 + [shape(own, columns)] * 2
    specs = [pl.BlockSpec(memory_space=pltpu.SMEM)] + [pl.BlockSpec(memory_space=pltpu.VMEM)] * 2
    scratch = [pltpu.VMEM((rows, tile), BF16)]
    return call(name, body, outs, (column, feat, weight), 2 * rows * width * columns, 16, None, specs, scratch)


def relay_add(p23, p67, r4, r5, out23, out67):
    out23[0] = (wide(p23, 0) + wide(r4)).astype(BF16)
    out23[1] = p23[1]
    out67[0] = p67[0]
    out67[1] = (wide(p67, 1) + wide(r5)).astype(BF16)


def relay_split(p23, p67, r4, r5, a23, a67, b23, b67):
    half = r4.shape[0] // 2
    for h, (out23, out67) in enumerate(((a23, a67), (b23, b67))):
        rows = slice(h * half, (h + 1) * half)
        out23[0] = (p23[0, rows].astype(F32) + wide(r4, rows)).astype(BF16)
        out23[1] = p23[1, rows]
        out67[0] = p67[0, rows]
        out67[1] = (p67[1, rows].astype(F32) + wide(r5, rows)).astype(BF16)


def add_half(h):
    def body(p01, r23, r67, out):
        half = out.shape[1]
        for k in range(2):
            own = p01[k, h * half : (h + 1) * half].astype(F32)
            out[k] = (own + wide(r23, k) + wide(r67, k)).astype(BF16)

    return body


def norm_half(p01, got01, emb_out, unit_out):
    for k in range(2):
        embedded = wide(p01, k) + wide(got01, 1 - k)
        emb_out[k] = embedded
        unit_out[k] = unit_of(embedded)[0].astype(BF16)


def back_half(g01, got01, emb, out):
    for k in range(2):
        out[k] = norm_back(wide(g01, k) + wide(got01, 1 - k), emb[k]).astype(BF16)


def cut(near, other, first_out, last_out):
    first_out[...] = near[0]
    last_out[...] = other[1]


def stack(first, second, out):
    out[0] = first[...]
    out[1] = second[...]


def grouped(refs, halves):
    return [refs[i * halves : (i + 1) * halves] for i in range(5)]


def block(group, k=None):
    parts = [ref[...] if k is None else ref[k] for ref in group]
    return parts[0] if len(parts) == 1 else jnp.concatenate(parts, axis=0)


def near_far_order(groups):
    g01, g23, g67, g4, g5 = groups
    pairs = [block(g, k) for g in (g01, g23, g67) for k in range(2)]
    return pairs + [block(g4), block(g5)]


def unit_of(embedded):
    inverse = lax.rsqrt(jnp.sum(embedded * embedded, axis=1, keepdims=True) + EPS)
    return embedded * inverse, inverse


def norm_back(unit_grad, embedded):
    unit, inverse = unit_of(embedded)
    return inverse * (unit_grad - unit * jnp.sum(unit * unit_grad, axis=1, keepdims=True))


def flat(ref):
    return ref[...].reshape(-1, ref.shape[-1])


def factors(scale, bias, txt, img):
    affinity = lax.dot_general(txt, img, (((1,), (1,)), ((), ())), preferred_element_type=F32)
    logits = scale * affinity + bias
    return logits, (scale / (1.0 + jnp.exp(-logits))).astype(BF16)


def product(first, second):
    return jnp.dot(first, second, preferred_element_type=F32)


def pair_call(name, body, outs, scale, bias, arrays, flops, limit, scratch=()):
    smem = pl.BlockSpec(memory_space=pltpu.SMEM)
    vmem = pl.BlockSpec(memory_space=pltpu.VMEM)
    moved = sum(a.size * a.dtype.itemsize for a in list(arrays) + outs)
    return pl.pallas_call(
        body,
        in_specs=[smem, smem] + [vmem] * len(arrays),
        out_shape=outs,
        scratch_shapes=list(scratch),
        compiler_params=pltpu.CompilerParams(vmem_limit_bytes=limit * MIB),
        cost_estimate=pl.CostEstimate(flops=flops, bytes_accessed=moved, transcendentals=0),
        name=name,
    )(scale, bias, *arrays)


def image_rows(image_refs, image_all):
    own = image_all.shape[0] // 8
    for k, part in enumerate(near_far_order(grouped(image_refs, 2))):
        image_all[k * own : (k + 1) * own] = part


def factor_rows(scale, bias, texts, image_all, factor_all, flipped):
    def images_at(here):
        factor = factors(scale, bias, flat(texts), image_all[here])[1]
        factor_all[:, here] = factor
        flipped[here] = factor.T

    tiles(image_all.shape[0] // 256, 256, images_at)


def match(scale, bias, texts, image_all, factor_all, flipped):
    own = texts.shape[1]
    logits = factors(scale, bias, texts[0], image_all[:own])[0]
    row = lax.broadcasted_iota(jnp.int32, logits.shape, 0)
    column = lax.broadcasted_iota(jnp.int32, logits.shape, 1)
    pull = (-scale / (1.0 + jnp.exp(logits))).astype(BF16)
    factor = jnp.where(row == column, pull, factor_all[:own, :own])
    factor_all[:own, :own] = factor
    flipped[:own, :own] = factor.T


def text_grads(factor_all, image_all, out):
    def columns_at(here):
        grads = product(factor_all[...], image_all[:, here]).astype(BF16)
        out[:, :, here] = grads.reshape(*out.shape[:2], 256)

    tiles(out.shape[-1] // 256, 256, columns_at)


def pairs_even(scale, bias, texts, images):
    count, own, width = texts.shape
    rows = count * own

    def body(scale_ref, bias_ref, texts, *refs):
        image_refs, (factor_all, flipped, image_all) = refs[:10], refs[10:]
        image_rows(image_refs, image_all)
        scale, bias = scale_ref[0], bias_ref[0]
        factor_rows(scale, bias, texts, image_all, factor_all, flipped)
        match(scale, bias, texts, image_all, factor_all, flipped)

    outs = [shape(rows, rows), shape(rows, rows), shape(rows, width)]
    return pair_call("pairs_even", body, outs, scale, bias, (texts, *images), 2 * rows * rows * width, 24)


def pairs_odd(scale, bias, texts, image_all, after):
    count, own, width = texts.shape
    rows = count * own

    def body(scale_ref, bias_ref, texts, image_all, _, flipped, out, factor_all):
        factor_rows(scale_ref[0], bias_ref[0], texts, image_all, factor_all, flipped)
        text_grads(factor_all, image_all, out)

    outs = [shape(rows, rows), shape(count, own, width)]
    scratch = [pltpu.VMEM((rows, rows), BF16)]
    arrays = (texts, image_all, after)
    return pair_call("pairs_odd", body, outs, scale, bias, arrays, 4 * rows * rows * width, 24, scratch)


def pairs_image(name, flips, texts, start, stop, outs, after=None):
    own, width = texts[0].shape[-2:]

    def body(flip_even, flip_odd, even, odd, *out_refs):
        def columns_at(here):
            factor = jnp.concatenate([flip_even[start:stop], flip_odd[start:stop]], axis=1)
            rows = jnp.concatenate([ref[:, :, here].reshape(-1, 256) for ref in (even, odd)], axis=0)
            total = product(factor, rows).astype(BF16)
            place = 0
            for ref in out_refs:
                size = ref.size // width
                ref[..., here] = total[place : place + size].reshape(*ref.shape[:-1], 256)
                place += size

        tiles(width // 256, 256, columns_at)

    flops = 2 * (stop - start) * 16 * own * width
    return call(name, body, outs, (*flips, *texts), flops, 24, after)


def weight_part(name, column, place, pieces, feat, after):
    halves, width = len(pieces) // 5, pieces[-1].shape[-1]
    rows, features = feat.shape
    own = rows // 8
    strip = width // 16
    tile = 256

    def body(column_ref, place_ref, *refs):
        feat_ref, same, other, flipped, moved, result = refs[5 * halves :]
        for n, part in enumerate(near_far_order(grouped(refs, halves))):
            k = NEAR_FAR[n]
            flipped[:, k * own : (k + 1) * own] = part.T
        def features_at(here):
            for k in range(rows // own):
                start = pl.multiple_of((column_ref[0] ^ k) * own, own)
                moved[k * own : (k + 1) * own] = feat_ref[pl.ds(start, own), here]
            result[...] = product(flipped[...], moved[...]).astype(BF16)
            for j, k in enumerate((0, 2, 4, 6, 12, 14, 8, 10)):
                mine = pl.multiple_of((place_ref[0] ^ k) * strip, strip)
                theirs = pl.multiple_of((place_ref[0] ^ (k + 1)) * strip, strip)
                same[j, :, here] = result[pl.ds(mine, strip)]
                other[j, :, here] = result[pl.ds(theirs, strip)]

        tiles(features // tile, tile, features_at)

    smem, vmem = pl.BlockSpec(memory_space=pltpu.SMEM), pl.BlockSpec(memory_space=pltpu.VMEM)
    specs = [smem, smem] + [vmem] * (len(pieces) + 1)
    scratch = [
        pltpu.VMEM((width, rows), BF16),
        pltpu.VMEM((rows, tile), BF16),
        pltpu.VMEM((width, tile), BF16),
    ]
    outs = [shape(8, strip, features)] * 2
    flops = 2 * rows * width * features
    return call(name, body, outs, (column, place, *pieces, feat), flops, 16, after, specs, scratch)


def feature_grad(name, column, pieces, weight):
    halves, width = len(pieces) // 5, pieces[-1].shape[-1]
    features = weight.shape[0]
    own = pieces[-1].shape[0] * halves
    rows = 8 * own
    tile = 256

    def body(column_ref, *refs):
        weight_ref, out = refs[5 * halves :]
        def features_at(here):
            egrad = jnp.concatenate(near_far_order(grouped(refs, halves)), axis=0)
            result = lax.dot_general(
                egrad, weight_ref[here], (((1,), (1,)), ((), ())), preferred_element_type=F32
            ).astype(BF16)
            for n, k in enumerate(NEAR_FAR):
                start = pl.multiple_of((column_ref[0] ^ k) * own, own)
                out[pl.ds(start, own), here] = result[n * own : (n + 1) * own]

        tiles(features // tile, tile, features_at)

    smem, vmem = pl.BlockSpec(memory_space=pltpu.SMEM), pl.BlockSpec(memory_space=pltpu.VMEM)
    outs, ins = [shape(rows, features)], (column, *pieces, weight)
    return call(name, body, outs, ins, 2 * rows * width * features, 16, None, [smem] + [vmem] * (len(pieces) + 1))[0]


def chip_weight(name, same, other, after=None):
    strip, features = same.shape[1:]

    def body(same, got, *outs):
        for j, out in enumerate(outs):
            out[...] = (wide(same, slice(2 * j, 2 * j + 2)) + wide(got, slice(2 * j, 2 * j + 2))).astype(BF16)

    outs = [shape(2, strip, features)] * 4
    return call(name, body, outs, (same, swap(other, "blk", 1)), after=after)


def sum_weight(p02, p46, p1214, p810):
    strip, features = p02.shape[1:]

    def along_z(p02, p46, p1214, p810, p0_out, p2_out):
        total = wide(p02) + wide(p46) + wide(p1214) + wide(p810)
        p0_out[...] = total[0]
        p2_out[...] = total[1].astype(BF16)

    def along_y(p0, p2, out):
        out[...] = p0[...] + wide(p2)

    p46, p1214, p810 = swap(p46, "blk", 4), swap(p1214, "blk", 12), swap(p810, "blk", 8)
    outs = [shape(strip, features, dtype=F32), shape(strip, features)]
    p0, p2 = call("weight_z", along_z, outs, (p02, p46, p1214, p810))
    p2 = swap(p2, "blk", 2)
    return call("weight_y", along_y, outs[:1], (p0, p2))[0].T, (p46, p1214)


def local(img_feat, txt_feat, img_weight, txt_weight, natural_exponent_multiplier, bias):
    scale = jnp.exp(natural_exponent_multiplier)
    blocks = lax.axis_size("mp")
    column = lax.axis_index("mp").astype(jnp.int32)[None]
    place = lax.axis_index("blk").astype(jnp.int32)[None]
    own = img_feat.shape[0] // blocks
    width = img_weight.shape[1]
    one, two = (own, width), (2, own, width)

    half = (2, own // 2, width)
    own_half = (own // 2, width)

    t01, t23, t67, t4, t5 = embed("embed_text", txt_feat, txt_weight, column, blocks)
    t4, t5 = swap(t4, "mp", 6), swap(t5, "mp", 2)
    i01, i23, i67, i4, i5 = embed("embed_image", img_feat, img_weight, column, blocks)
    t23, t67 = call("relay_text", relay_add, [shape(*two)] * 2, (t23, t67, t4, t5))
    t23, t67 = swap(t23, "mp", 2), swap(t67, "mp", 6)
    i4, i5 = swap(i4, "mp", 6), swap(i5, "mp", 2)

    def second(t01, t23, t67, t0_out, t1_out):
        t0_out[...] = wide(t01, 0) + wide(t23, 0) + wide(t67, 0)
        t1_out[...] = (wide(t01, 1) + wide(t23, 1) + wide(t67, 1)).astype(BF16)

    t0, t1 = call("sums_second", second, [shape(*one, dtype=F32), shape(*one)], (t01, t23, t67))
    t1_got = swap(t1, "mp", 1)
    sent = call("relay_image", relay_split, [shape(*half)] * 4, (i23, i67, i4, i5), after=t1)
    got = [(swap(sent[2 * h], "mp", 2), swap(sent[2 * h + 1], "mp", 6)) for h in range(2)]

    def third(t0, t1, text_out, unit_out):
        embedded = t0[...] + wide(t1)
        text_out[...] = embedded
        unit_out[...] = unit_of(embedded)[0].astype(BF16)

    txt_emb, a0 = call("sums_third", third, [shape(*one, dtype=F32), shape(*one)], (t0, t1_got), after=sent[0])
    a2 = swap(a0, "blk", 2)
    (x_a,) = call("image_x_a", add_half(0), [shape(*half)], (i01, *got[0]), after=a0)
    y_a = swap(x_a, "mp", 1)
    (a02,) = call("stack_text", stack, [shape(*two)], (a0, a2), after=x_a)
    a46, a1214 = swap(a02, "blk", 4), swap(a02, "blk", 12)
    (x_b,) = call("image_x_b", add_half(1), [shape(*half)], (i01, *got[1]), after=a02)
    y_b = swap(x_b, "mp", 1)
    outs = [shape(*half, dtype=F32), shape(*half)]
    emb_a, u01_a = call("image_unit_a", norm_half, outs, (x_a, y_a), after=x_b)
    u23_a, u67_a = swap(u01_a, "mp", 2), swap(u01_a, "mp", 6)
    emb_b, u01_b = call("image_unit_b", norm_half, outs, (x_b, y_b), after=u01_a)
    u23_b, u67_b = swap(u01_b, "mp", 2), swap(u01_b, "mp", 6)
    outs = [shape(*own_half)] * 2
    u2_a, u7_a = call("cut_image_a", cut, outs, (u23_a, u67_a), after=u01_b)
    u4_a, u5_a = swap(u2_a, "mp", 6), swap(u7_a, "mp", 2)
    a4, a14 = call("cut_text", cut, [shape(*one)] * 2, (a46, a1214), after=u2_a)
    a8, a10 = swap(a4, "blk", 12), swap(a14, "blk", 4)
    u2_b, u7_b = call("cut_image_b", cut, outs, (u23_b, u67_b), after=a4)
    u4_b, u5_b = swap(u2_b, "mp", 6), swap(u7_b, "mp", 2)

    def collect(a02, a46, a1214, a8, a10, out):
        for k, ref in enumerate((a02, a46, a1214)):
            out[2 * k : 2 * k + 2] = ref[...]
        out[6] = a8[...]
        out[7] = a10[...]

    (even,) = call("collect", collect, [shape(8, *one)], (a02, a46, a1214, a8, a10), after=(u4_a, u5_a, u4_b, u5_b))
    odd = swap(even, "blk", 1)
    images = (u01_a, u01_b, u23_a, u23_b, u67_a, u67_b, u4_a, u4_b, u5_a, u5_b)
    factor_even, flip_even, image_all = pairs_even(scale, bias, even, images)
    flip_odd, odd_sum = pairs_odd(scale, bias, odd, image_all, flip_even)
    odd_got = swap(odd_sum, "blk", 1)
    flips, texts = (flip_even, flip_odd), (even, odd)
    g4, g5 = pairs_image("pairs_far_images", flips, texts, 6 * own, 8 * own, [shape(*one)] * 2, odd_sum)
    g4_got, g5_got = swap(g4, "mp", 6), swap(g5, "mp", 2)
    flops = 128 * own * own * width
    (even_sum,) = call("text_grads_even", text_grads, [shape(8, *one)], (factor_even, image_all), flops, 20, g4)

    def fifth(even, got, p8, p10):
        p8[...] = (wide(even, 6) + wide(got, 6)).astype(BF16)
        p10[...] = (wide(even, 7) + wide(got, 7)).astype(BF16)

    p8, p10 = call("sums_fifth", fifth, [shape(*one)] * 2, (even_sum, odd_got))
    g01, g23, g67 = pairs_image("pairs_near_images", flips, texts, 0, 6 * own, [shape(*two)] * 3, p8)
    p8_got, p10_got = swap(p8, "blk", 12), swap(p10, "blk", 4)
    sent = call("relay_image_grads", relay_split, [shape(*half)] * 4, (g23, g67, g4_got, g5_got))
    got = [(swap(sent[2 * h], "mp", 2), swap(sent[2 * h + 1], "mp", 6)) for h in range(2)]

    def sixth(even, got, p8, p10, p02, p46, p1214):
        for k in range(2):
            p02[k] = (wide(even, k) + wide(got, k)).astype(BF16)
        p46[0] = (wide(even, 2) + wide(got, 2) + wide(p8)).astype(BF16)
        p46[1] = (wide(even, 3) + wide(got, 3)).astype(BF16)
        p1214[0] = (wide(even, 4) + wide(got, 4)).astype(BF16)
        p1214[1] = (wide(even, 5) + wide(got, 5) + wide(p10)).astype(BF16)

    outs = [shape(*two)] * 3
    p02, p46, p1214 = call("sums_sixth", sixth, outs, (even_sum, odd_got, p8_got, p10_got), after=sent[0])
    p46, p1214 = swap(p46, "blk", 4), swap(p1214, "blk", 12)
    (x_a,) = call("image_grads_x_a", add_half(0), [shape(*half)], (g01, *got[0]), after=p02)
    y_a = swap(x_a, "mp", 1)
    (x_b,) = call("image_grads_x_b", add_half(1), [shape(*half)], (g01, *got[1]), after=x_a)
    y_b = swap(x_b, "mp", 1)
    (e01_a,) = call("image_back_a", back_half, [shape(*half)], (x_a, y_a, emb_a), after=x_b)
    e23_a, e67_a = swap(e01_a, "mp", 2), swap(e01_a, "mp", 6)

    def seventh(p02, p46, p1214, p0_out, p2_out):
        p0_out[...] = wide(p02, 0) + wide(p46, 0) + wide(p1214, 0)
        p2_out[...] = (wide(p02, 1) + wide(p46, 1) + wide(p1214, 1)).astype(BF16)

    outs = [shape(*one, dtype=F32), shape(*one)]
    p0, p2 = call("sums_seventh", seventh, outs, (p02, p46, p1214), after=e01_a)
    p2_got = swap(p2, "blk", 2)
    (e01_b,) = call("image_back_b", back_half, [shape(*half)], (x_b, y_b, emb_b), after=p2)
    e23_b, e67_b = swap(e01_b, "mp", 2), swap(e01_b, "mp", 6)
    outs = [shape(*own_half)] * 2
    e2_a, e7_a = call("cut_image_grads_a", cut, outs, (e23_a, e67_a), after=e01_b)
    e4_a, e5_a = swap(e2_a, "mp", 6), swap(e7_a, "mp", 2)

    def text_back(p0, p2, txt_emb, out):
        out[...] = norm_back(p0[...] + wide(p2), txt_emb[...]).astype(BF16)

    (d0,) = call("text_back", text_back, [shape(*one)], (p0, p2_got, txt_emb), after=e2_a)
    d1 = swap(d0, "mp", 1)
    e2_b, e7_b = call("cut_image_grads_b", cut, outs, (e23_b, e67_b), after=d0)
    e4_b, e5_b = swap(e2_b, "mp", 6), swap(e7_b, "mp", 2)
    (d01,) = call("stack_text_grads", stack, [shape(*two)], (d0, d1), after=(e4_a, e5_a, e4_b, e5_b))
    d23, d67 = swap(d01, "mp", 2), swap(d01, "mp", 6)

    e_all = (e01_a, e01_b, e23_a, e23_b, e67_a, e67_b, e4_a, e4_b, e5_a, e5_b)
    same, other = weight_part("weight_image", column, place, e_all, img_feat, d01)
    d2, d7 = call("cut_text_grads", cut, [shape(*one)] * 2, (d23, d67), ORDER_COST, after=same)
    d4, d5 = swap(d2, "mp", 6), swap(d7, "mp", 2)
    image_chip = chip_weight("weight_image_chip", same, other, None)
    img_weight_grad, image_got = sum_weight(*image_chip)
    d_all = (d01, d23, d67, d4, d5)
    same, other = weight_part("weight_text", column, place, d_all, txt_feat, image_got)
    txt_weight_grad, _ = sum_weight(*chip_weight("weight_text_chip", same, other))
    return (
        feature_grad("feature_image", column, e_all, img_weight),
        feature_grad("feature_text", column, d_all, txt_weight),
        img_weight_grad,
        txt_weight_grad,
    )


def solution(mesh):
    return jax.shard_map(
        local,
        mesh=mesh,
        in_specs=(P("blk", "mp"), P("blk", "mp"), P("mp", None), P("mp", None), P(), P()),
        out_specs=(P("blk", "mp"), P("blk", "mp"), P("mp", "blk"), P("mp", "blk")),
        check_vma=False,
    )
```

```python
import jax
import jax.numpy as jnp
from jax import lax
from jax.experimental import pallas as pl
from jax.experimental.pallas import tpu as pltpu
from jax.sharding import PartitionSpec as P

EPS = 1e-06
BF16 = jnp.bfloat16
F32 = jnp.float32
MIB = 1024 * 1024
ORDER_COST = 30 * 10**9
NEAR_FAR = (0, 1, 2, 3, 6, 7, 4, 5)


def swap(value, axis, offset):
    count = lax.axis_size(axis)
    return lax.ppermute(value, axis, [(i, i ^ offset) for i in range(count)])


def shape(*dims, dtype=BF16):
    return jax.ShapeDtypeStruct(dims, dtype)


def call(name, body, outs, ins, flops=0, limit=10, after=None, in_specs=None, scratch=()):
    ins, specs = list(ins), in_specs or [pl.BlockSpec(memory_space=pltpu.VMEM)] * len(ins)
    run = body
    if after is not None:
        after = list(after) if isinstance(after, tuple) else [after]
        ins, specs = after + ins, [pl.BlockSpec(memory_space=pltpu.VMEM)] * len(after) + list(specs)

        def run(*refs):
            body(*refs[len(after) :])

    moved = sum(a.size * a.dtype.itemsize for a in ins + list(outs))
    return pl.pallas_call(
        run,
        out_shape=outs,
        in_specs=specs,
        scratch_shapes=list(scratch),
        compiler_params=pltpu.CompilerParams(vmem_limit_bytes=limit * MIB),
        cost_estimate=pl.CostEstimate(flops=flops, bytes_accessed=moved, transcendentals=0),
        name=name,
    )(*ins)


def tiles(count, size, body, unroll=False):
    if unroll:
        for index in range(count):
            body(slice(index * size, (index + 1) * size))
        return

    def step(index, carry):
        body(pl.ds(pl.multiple_of(index * size, size), size))
        return carry

    lax.fori_loop(0, count, step, 0)


def wide(ref, block=None):
    return (ref[...] if block is None else ref[block]).astype(F32)


def embed(name, feat, weight, column, blocks, tile=256):
    rows, width = feat.shape
    columns = weight.shape[1]
    own = rows // blocks

    def body(column_ref, feat_ref, weight_ref, p01, p23, p67, p4, p5, result):
        def part(k):
            return result[pl.ds(pl.multiple_of((column_ref[0] ^ k) * own, own), own)]

        def columns_at(here):
            result[...] = product(feat_ref[...], weight_ref[:, here]).astype(BF16)
            for k in range(2):
                p01[k, :, here] = part(k)
                p23[k, :, here] = part(2 + k)
                p67[k, :, here] = part(6 + k)
            p4[:, here] = part(4)
            p5[:, here] = part(5)

        tiles(columns // tile, tile, columns_at)

    outs = [shape(2, own, columns)] * 3 + [shape(own, columns)] * 2
    specs = [pl.BlockSpec(memory_space=pltpu.SMEM)] + [pl.BlockSpec(memory_space=pltpu.VMEM)] * 2
    scratch = [pltpu.VMEM((rows, tile), BF16)]
    return call(name, body, outs, (column, feat, weight), 2 * rows * width * columns, 16, None, specs, scratch)


def relay_add(p23, p67, r4, r5, out23, out67):
    out23[0] = (wide(p23, 0) + wide(r4)).astype(BF16)
    out23[1] = p23[1]
    out67[0] = p67[0]
    out67[1] = (wide(p67, 1) + wide(r5)).astype(BF16)


def relay_split(p23, p67, r4, r5, a23, a67, b23, b67):
    half = r4.shape[0] // 2
    for h, (out23, out67) in enumerate(((a23, a67), (b23, b67))):
        rows = slice(h * half, (h + 1) * half)
        out23[0] = (p23[0, rows].astype(F32) + wide(r4, rows)).astype(BF16)
        out23[1] = p23[1, rows]
        out67[0] = p67[0, rows]
        out67[1] = (p67[1, rows].astype(F32) + wide(r5, rows)).astype(BF16)


def add_half(h):
    def body(p01, r23, r67, out):
        half = out.shape[1]
        for k in range(2):
            own = p01[k, h * half : (h + 1) * half].astype(F32)
            out[k] = (own + wide(r23, k) + wide(r67, k)).astype(BF16)

    return body


def norm_half(p01, got01, emb_out, unit_out):
    for k in range(2):
        embedded = wide(p01, k) + wide(got01, 1 - k)
        emb_out[k] = embedded
        unit_out[k] = unit_of(embedded)[0].astype(BF16)


def back_half(g01, got01, emb, out):
    for k in range(2):
        out[k] = norm_back(wide(g01, k) + wide(got01, 1 - k), emb[k]).astype(BF16)


def cut(near, other, first_out, last_out):
    first_out[...] = near[0]
    last_out[...] = other[1]


def stack(first, second, out):
    out[0] = first[...]
    out[1] = second[...]


def grouped(refs, halves):
    return [refs[i * halves : (i + 1) * halves] for i in range(5)]


def block(group, k=None):
    parts = [ref[...] if k is None else ref[k] for ref in group]
    return parts[0] if len(parts) == 1 else jnp.concatenate(parts, axis=0)


def near_far_order(groups):
    g01, g23, g67, g4, g5 = groups
    pairs = [block(g, k) for g in (g01, g23, g67) for k in range(2)]
    return pairs + [block(g4), block(g5)]


def unit_of(embedded):
    inverse = lax.rsqrt(jnp.sum(embedded * embedded, axis=1, keepdims=True) + EPS)
    return embedded * inverse, inverse


def norm_back(unit_grad, embedded):
    unit, inverse = unit_of(embedded)
    return inverse * (unit_grad - unit * jnp.sum(unit * unit_grad, axis=1, keepdims=True))


def flat(ref):
    return ref[...].reshape(-1, ref.shape[-1])


def factors(scale, bias, txt, img):
    affinity = lax.dot_general(txt, img, (((1,), (1,)), ((), ())), preferred_element_type=F32)
    logits = scale * affinity + bias
    return logits, (scale / (1.0 + jnp.exp(-logits))).astype(BF16)


def product(first, second):
    return jnp.dot(first, second, preferred_element_type=F32)


def pair_call(name, body, outs, scale, bias, arrays, flops, limit, scratch=()):
    smem = pl.BlockSpec(memory_space=pltpu.SMEM)
    vmem = pl.BlockSpec(memory_space=pltpu.VMEM)
    moved = sum(a.size * a.dtype.itemsize for a in list(arrays) + outs)
    return pl.pallas_call(
        body,
        in_specs=[smem, smem] + [vmem] * len(arrays),
        out_shape=outs,
        scratch_shapes=list(scratch),
        compiler_params=pltpu.CompilerParams(vmem_limit_bytes=limit * MIB),
        cost_estimate=pl.CostEstimate(flops=flops, bytes_accessed=moved, transcendentals=0),
        name=name,
    )(scale, bias, *arrays)


def image_rows(image_refs, image_all):
    own = image_all.shape[0] // 8
    for k, part in enumerate(near_far_order(grouped(image_refs, 2))):
        image_all[k * own : (k + 1) * own] = part


def factor_rows(scale, bias, texts, image_all, factor_all, flipped, tile, unroll):
    def images_at(here):
        factor = factors(scale, bias, flat(texts), image_all[here])[1]
        factor_all[:, here] = factor
        flipped[here] = factor.T

    tiles(image_all.shape[0] // tile, tile, images_at, unroll)


def match(scale, bias, texts, image_all, factor_all, flipped):
    own = texts.shape[1]
    logits = factors(scale, bias, texts[0], image_all[:own])[0]
    row = lax.broadcasted_iota(jnp.int32, logits.shape, 0)
    column = lax.broadcasted_iota(jnp.int32, logits.shape, 1)
    pull = (-scale / (1.0 + jnp.exp(logits))).astype(BF16)
    factor = jnp.where(row == column, pull, factor_all[:own, :own])
    factor_all[:own, :own] = factor
    flipped[:own, :own] = factor.T


def text_grads(factor_all, image_all, out, tile=512, unroll=False):
    def columns_at(here):
        grads = product(factor_all[...], image_all[:, here]).astype(BF16)
        out[:, :, here] = grads.reshape(*out.shape[:2], tile)

    tiles(out.shape[-1] // tile, tile, columns_at, unroll)


def pairs_even(scale, bias, texts, images):
    count, own, width = texts.shape
    rows = count * own

    def body(scale_ref, bias_ref, texts, *refs):
        image_refs, (factor_all, flipped, image_all) = refs[:10], refs[10:]
        image_rows(image_refs, image_all)
        scale, bias = scale_ref[0], bias_ref[0]
        factor_rows(scale, bias, texts, image_all, factor_all, flipped, 512, False)
        match(scale, bias, texts, image_all, factor_all, flipped)

    outs = [shape(rows, rows), shape(rows, rows), shape(rows, width)]
    return pair_call("pairs_even", body, outs, scale, bias, (texts, *images), 2 * rows * rows * width, 24)


def pairs_odd(scale, bias, texts, image_all, after):
    count, own, width = texts.shape
    rows = count * own

    def body(scale_ref, bias_ref, texts, image_all, _, flipped, out, factor_all):
        factor_rows(scale_ref[0], bias_ref[0], texts, image_all, factor_all, flipped, 256, True)
        text_grads(factor_all, image_all, out, 256, True)

    outs = [shape(rows, rows), shape(count, own, width)]
    scratch = [pltpu.VMEM((rows, rows), BF16)]
    arrays = (texts, image_all, after)
    return pair_call("pairs_odd", body, outs, scale, bias, arrays, 4 * rows * rows * width, 24, scratch)


def pairs_image(name, flips, texts, start, stop, outs, after, tile, unroll):
    own, width = texts[0].shape[-2:]

    def body(flip_even, flip_odd, even, odd, *out_refs):
        def columns_at(here):
            factor = jnp.concatenate([flip_even[start:stop], flip_odd[start:stop]], axis=1)
            rows = jnp.concatenate([ref[:, :, here].reshape(-1, tile) for ref in (even, odd)], axis=0)
            total = product(factor, rows).astype(BF16)
            place = 0
            for ref in out_refs:
                size = ref.size // width
                ref[..., here] = total[place : place + size].reshape(*ref.shape[:-1], tile)
                place += size

        tiles(width // tile, tile, columns_at, unroll)

    flops = 2 * (stop - start) * 16 * own * width
    return call(name, body, outs, (*flips, *texts), flops, 24, after)


def weight_part(name, column, place, pieces, feat, after):
    halves, width = len(pieces) // 5, pieces[-1].shape[-1]
    rows, features = feat.shape
    own = rows // 8
    strip = width // 16
    tile = 256

    def body(column_ref, place_ref, *refs):
        feat_ref, same, other, flipped, moved, result = refs[5 * halves :]
        for n, part in enumerate(near_far_order(grouped(refs, halves))):
            k = NEAR_FAR[n]
            flipped[:, k * own : (k + 1) * own] = part.T
        def features_at(here):
            for k in range(rows // own):
                start = pl.multiple_of((column_ref[0] ^ k) * own, own)
                moved[k * own : (k + 1) * own] = feat_ref[pl.ds(start, own), here]
            result[...] = product(flipped[...], moved[...]).astype(BF16)
            for j, k in enumerate((0, 2, 4, 6, 12, 14, 8, 10)):
                mine = pl.multiple_of((place_ref[0] ^ k) * strip, strip)
                theirs = pl.multiple_of((place_ref[0] ^ (k + 1)) * strip, strip)
                same[j, :, here] = result[pl.ds(mine, strip)]
                other[j, :, here] = result[pl.ds(theirs, strip)]

        tiles(features // tile, tile, features_at, True)

    smem, vmem = pl.BlockSpec(memory_space=pltpu.SMEM), pl.BlockSpec(memory_space=pltpu.VMEM)
    specs = [smem, smem] + [vmem] * (len(pieces) + 1)
    scratch = [
        pltpu.VMEM((width, rows), BF16),
        pltpu.VMEM((rows, tile), BF16),
        pltpu.VMEM((width, tile), BF16),
    ]
    outs = [shape(8, strip, features)] * 2
    flops = 2 * rows * width * features
    return call(name, body, outs, (column, place, *pieces, feat), flops, 16, after, specs, scratch)


def feature_grad(name, column, pieces, weight):
    halves, width = len(pieces) // 5, pieces[-1].shape[-1]
    features = weight.shape[0]
    own = pieces[-1].shape[0] * halves
    rows = 8 * own
    tile = 256

    def body(column_ref, *refs):
        weight_ref, out = refs[5 * halves :]
        def features_at(here):
            egrad = jnp.concatenate(near_far_order(grouped(refs, halves)), axis=0)
            result = lax.dot_general(
                egrad, weight_ref[here], (((1,), (1,)), ((), ())), preferred_element_type=F32
            ).astype(BF16)
            for n, k in enumerate(NEAR_FAR):
                start = pl.multiple_of((column_ref[0] ^ k) * own, own)
                out[pl.ds(start, own), here] = result[n * own : (n + 1) * own]

        tiles(features // tile, tile, features_at)

    smem, vmem = pl.BlockSpec(memory_space=pltpu.SMEM), pl.BlockSpec(memory_space=pltpu.VMEM)
    outs, ins = [shape(rows, features)], (column, *pieces, weight)
    return call(name, body, outs, ins, 2 * rows * width * features, 16, None, [smem] + [vmem] * (len(pieces) + 1))[0]


def chip_weight(name, same, other, after=None):
    strip, features = same.shape[1:]

    def body(same, got, *outs):
        for j, out in enumerate(outs):
            out[...] = (wide(same, slice(2 * j, 2 * j + 2)) + wide(got, slice(2 * j, 2 * j + 2))).astype(BF16)

    outs = [shape(2, strip, features)] * 4
    return call(name, body, outs, (same, swap(other, "blk", 1)), after=after)


def sum_weight(p02, p46, p1214, p810):
    strip, features = p02.shape[1:]

    def along_z(p02, p46, p1214, p810, p0_out, p2_out):
        total = wide(p02) + wide(p46) + wide(p1214) + wide(p810)
        p0_out[...] = total[0]
        p2_out[...] = total[1].astype(BF16)

    def along_y(p0, p2, out):
        out[...] = p0[...] + wide(p2)

    p46, p1214, p810 = swap(p46, "blk", 4), swap(p1214, "blk", 12), swap(p810, "blk", 8)
    outs = [shape(strip, features, dtype=F32), shape(strip, features)]
    p0, p2 = call("weight_z", along_z, outs, (p02, p46, p1214, p810))
    p2 = swap(p2, "blk", 2)
    return call("weight_y", along_y, outs[:1], (p0, p2))[0].T


def local(img_feat, txt_feat, img_weight, txt_weight, natural_exponent_multiplier, bias):
    scale = jnp.exp(natural_exponent_multiplier)
    blocks = lax.axis_size("mp")
    column = lax.axis_index("mp").astype(jnp.int32)[None]
    place = lax.axis_index("blk").astype(jnp.int32)[None]
    own = img_feat.shape[0] // blocks
    width = img_weight.shape[1]
    one, two = (own, width), (2, own, width)

    half = (2, own // 2, width)
    own_half = (own // 2, width)

    t01, t23, t67, t4, t5 = embed("embed_text", txt_feat, txt_weight, column, blocks)
    t4, t5 = swap(t4, "mp", 6), swap(t5, "mp", 2)
    i01, i23, i67, i4, i5 = embed("embed_image", img_feat, img_weight, column, blocks)
    t23, t67 = call("relay_text", relay_add, [shape(*two)] * 2, (t23, t67, t4, t5))
    t23, t67 = swap(t23, "mp", 2), swap(t67, "mp", 6)
    i4, i5 = swap(i4, "mp", 6), swap(i5, "mp", 2)

    def second(t01, t23, t67, t0_out, t1_out):
        t0_out[...] = wide(t01, 0) + wide(t23, 0) + wide(t67, 0)
        t1_out[...] = (wide(t01, 1) + wide(t23, 1) + wide(t67, 1)).astype(BF16)

    t0, t1 = call("sums_second", second, [shape(*one, dtype=F32), shape(*one)], (t01, t23, t67))
    t1_got = swap(t1, "mp", 1)
    sent = call("relay_image", relay_split, [shape(*half)] * 4, (i23, i67, i4, i5), after=t1)
    got = [(swap(sent[2 * h], "mp", 2), swap(sent[2 * h + 1], "mp", 6)) for h in range(2)]

    def third(t0, t1, text_out, unit_out):
        embedded = t0[...] + wide(t1)
        text_out[...] = embedded
        unit_out[...] = unit_of(embedded)[0].astype(BF16)

    txt_emb, a0 = call("sums_third", third, [shape(*one, dtype=F32), shape(*one)], (t0, t1_got), after=sent[0])
    a2 = swap(a0, "blk", 2)
    (x_a,) = call("image_x_a", add_half(0), [shape(*half)], (i01, *got[0]), after=a0)
    y_a = swap(x_a, "mp", 1)
    (a02,) = call("stack_text", stack, [shape(*two)], (a0, a2), after=x_a)
    a46, a1214 = swap(a02, "blk", 4), swap(a02, "blk", 12)
    (x_b,) = call("image_x_b", add_half(1), [shape(*half)], (i01, *got[1]), after=a02)
    y_b = swap(x_b, "mp", 1)
    outs = [shape(*half, dtype=F32), shape(*half)]
    emb_a, u01_a = call("image_unit_a", norm_half, outs, (x_a, y_a), after=x_b)
    u23_a, u67_a = swap(u01_a, "mp", 2), swap(u01_a, "mp", 6)
    emb_b, u01_b = call("image_unit_b", norm_half, outs, (x_b, y_b), after=u01_a)
    u23_b, u67_b = swap(u01_b, "mp", 2), swap(u01_b, "mp", 6)
    outs = [shape(*own_half)] * 2
    u2_a, u7_a = call("cut_image_a", cut, outs, (u23_a, u67_a), after=u01_b)
    u4_a, u5_a = swap(u2_a, "mp", 6), swap(u7_a, "mp", 2)
    a4, a14 = call("cut_text", cut, [shape(*one)] * 2, (a46, a1214), after=u2_a)
    a8, a10 = swap(a4, "blk", 12), swap(a14, "blk", 4)
    u2_b, u7_b = call("cut_image_b", cut, outs, (u23_b, u67_b), after=a4)
    u4_b, u5_b = swap(u2_b, "mp", 6), swap(u7_b, "mp", 2)

    def collect(a02, a46, a1214, a8, a10, out):
        for k, ref in enumerate((a02, a46, a1214)):
            out[2 * k : 2 * k + 2] = ref[...]
        out[6] = a8[...]
        out[7] = a10[...]

    (even,) = call("collect", collect, [shape(8, *one)], (a02, a46, a1214, a8, a10), after=(u4_a, u5_a, u4_b, u5_b))
    odd = swap(even, "blk", 1)
    images = (u01_a, u01_b, u23_a, u23_b, u67_a, u67_b, u4_a, u4_b, u5_a, u5_b)
    factor_even, flip_even, image_all = pairs_even(scale, bias, even, images)
    flip_odd, odd_sum = pairs_odd(scale, bias, odd, image_all, flip_even)
    odd_got = swap(odd_sum, "blk", 1)
    flips, texts = (flip_even, flip_odd), (even, odd)
    g4, g5 = pairs_image("pairs_far_images", flips, texts, 6 * own, 8 * own, [shape(*one)] * 2, odd_sum, 256, True)
    g4_got, g5_got = swap(g4, "mp", 6), swap(g5, "mp", 2)
    flops = 128 * own * own * width
    (even_sum,) = call("text_grads_even", text_grads, [shape(8, *one)], (factor_even, image_all), flops, 20, g4)

    def fifth(even, got, p8, p10):
        p8[...] = (wide(even, 6) + wide(got, 6)).astype(BF16)
        p10[...] = (wide(even, 7) + wide(got, 7)).astype(BF16)

    p8, p10 = call("sums_fifth", fifth, [shape(*one)] * 2, (even_sum, odd_got))
    g01, g23, g67 = pairs_image("pairs_near_images", flips, texts, 0, 6 * own, [shape(*two)] * 3, p8, 512, False)
    p8_got, p10_got = swap(p8, "blk", 12), swap(p10, "blk", 4)
    sent = call("relay_image_grads", relay_split, [shape(*half)] * 4, (g23, g67, g4_got, g5_got))
    got = [(swap(sent[2 * h], "mp", 2), swap(sent[2 * h + 1], "mp", 6)) for h in range(2)]

    def sixth(even, got, p8, p10, p02, p46, p1214):
        for k in range(2):
            p02[k] = (wide(even, k) + wide(got, k)).astype(BF16)
        p46[0] = (wide(even, 2) + wide(got, 2) + wide(p8)).astype(BF16)
        p46[1] = (wide(even, 3) + wide(got, 3)).astype(BF16)
        p1214[0] = (wide(even, 4) + wide(got, 4)).astype(BF16)
        p1214[1] = (wide(even, 5) + wide(got, 5) + wide(p10)).astype(BF16)

    outs = [shape(*two)] * 3
    p02, p46, p1214 = call("sums_sixth", sixth, outs, (even_sum, odd_got, p8_got, p10_got), after=sent[0])
    p46, p1214 = swap(p46, "blk", 4), swap(p1214, "blk", 12)
    (x_a,) = call("image_grads_x_a", add_half(0), [shape(*half)], (g01, *got[0]), after=p02)
    y_a = swap(x_a, "mp", 1)
    (x_b,) = call("image_grads_x_b", add_half(1), [shape(*half)], (g01, *got[1]), after=x_a)
    y_b = swap(x_b, "mp", 1)
    (e01_a,) = call("image_back_a", back_half, [shape(*half)], (x_a, y_a, emb_a), after=x_b)
    e23_a, e67_a = swap(e01_a, "mp", 2), swap(e01_a, "mp", 6)

    def seventh(p02, p46, p1214, p0_out, p2_out):
        p0_out[...] = wide(p02, 0) + wide(p46, 0) + wide(p1214, 0)
        p2_out[...] = (wide(p02, 1) + wide(p46, 1) + wide(p1214, 1)).astype(BF16)

    outs = [shape(*one, dtype=F32), shape(*one)]
    p0, p2 = call("sums_seventh", seventh, outs, (p02, p46, p1214), after=e01_a)
    p2_got = swap(p2, "blk", 2)
    (e01_b,) = call("image_back_b", back_half, [shape(*half)], (x_b, y_b, emb_b), after=p2)
    e23_b, e67_b = swap(e01_b, "mp", 2), swap(e01_b, "mp", 6)
    outs = [shape(*own_half)] * 2
    e2_a, e7_a = call("cut_image_grads_a", cut, outs, (e23_a, e67_a), after=e01_b)
    e4_a, e5_a = swap(e2_a, "mp", 6), swap(e7_a, "mp", 2)

    def text_back(p0, p2, txt_emb, out):
        out[...] = norm_back(p0[...] + wide(p2), txt_emb[...]).astype(BF16)

    (d0,) = call("text_back", text_back, [shape(*one)], (p0, p2_got, txt_emb), after=e2_a)
    d1 = swap(d0, "mp", 1)
    e2_b, e7_b = call("cut_image_grads_b", cut, outs, (e23_b, e67_b), after=d0)
    e4_b, e5_b = swap(e2_b, "mp", 6), swap(e7_b, "mp", 2)
    (d01,) = call("stack_text_grads", stack, [shape(*two)], (d0, d1), after=(e4_a, e5_a, e2_b))
    d23, d67 = swap(d01, "mp", 2), swap(d01, "mp", 6)

    e_all = (e01_a, e01_b, e23_a, e23_b, e67_a, e67_b, e4_a, e4_b, e5_a, e5_b)
    d2, d7 = call("cut_text_grads", cut, [shape(*one)] * 2, (d23, d67))
    d4, d5 = swap(d2, "mp", 6), swap(d7, "mp", 2)
    same, other = weight_part("weight_image", column, place, e_all, img_feat, d7)
    image_chip = chip_weight("weight_image_chip", same, other, None)
    img_weight_grad = sum_weight(*image_chip)

    def keep(first, second, first_out, second_out):
        first_out[...] = first[...]
        second_out[...] = second[...]

    d4, d5 = call("keep_text_far", keep, [shape(*one)] * 2, (d4, d5), ORDER_COST)
    d_all = (d01, d23, d67, d4, d5)
    same, other = weight_part("weight_text", column, place, d_all, txt_feat, image_chip[0])
    txt_weight_grad = sum_weight(*chip_weight("weight_text_chip", same, other))
    return (
        feature_grad("feature_image", column, e_all, img_weight),
        feature_grad("feature_text", column, d_all, txt_weight),
        img_weight_grad,
        txt_weight_grad,
    )


def solution(mesh):
    return jax.shard_map(
        local,
        mesh=mesh,
        in_specs=(P("blk", "mp"), P("blk", "mp"), P("mp", None), P("mp", None), P(), P()),
        out_specs=(P("blk", "mp"), P("blk", "mp"), P("mp", "blk"), P("mp", "blk")),
        check_vma=False,
    )
```

```python
import jax
import jax.numpy as jnp
from jax import lax
from jax.experimental import pallas as pl
from jax.experimental.pallas import tpu as pltpu
from jax.sharding import PartitionSpec as P

EPS = 1e-06
BF16 = jnp.bfloat16
F32 = jnp.float32
MIB = 1024 * 1024
ORDER_COST = 12 * 10**9
NEAR_FAR = (0, 1, 2, 3, 6, 7, 4, 5)


def swap(value, axis, offset):
    count = lax.axis_size(axis)
    return lax.ppermute(value, axis, [(i, i ^ offset) for i in range(count)])


def shape(*dims, dtype=BF16):
    return jax.ShapeDtypeStruct(dims, dtype)


def call(name, body, outs, ins, flops=0, limit=10, after=None, in_specs=None, scratch=()):
    ins, specs = list(ins), in_specs or [pl.BlockSpec(memory_space=pltpu.VMEM)] * len(ins)
    run = body
    if after is not None:
        after = list(after) if isinstance(after, tuple) else [after]
        ins, specs = after + ins, [pl.BlockSpec(memory_space=pltpu.VMEM)] * len(after) + list(specs)

        def run(*refs):
            body(*refs[len(after) :])

    moved = sum(a.size * a.dtype.itemsize for a in ins + list(outs))
    return pl.pallas_call(
        run,
        out_shape=outs,
        in_specs=specs,
        scratch_shapes=list(scratch),
        compiler_params=pltpu.CompilerParams(vmem_limit_bytes=limit * MIB),
        cost_estimate=pl.CostEstimate(flops=flops, bytes_accessed=moved, transcendentals=0),
        name=name,
    )(*ins)


def tiles(count, size, body, unroll=False):
    if unroll:
        for index in range(count):
            body(slice(index * size, (index + 1) * size))
        return

    def step(index, carry):
        body(pl.ds(pl.multiple_of(index * size, size), size))
        return carry

    lax.fori_loop(0, count, step, 0)


def wide(ref, block=None):
    return (ref[...] if block is None else ref[block]).astype(F32)


def embed(name, feat, weight, column, blocks, tile=256):
    rows, width = feat.shape
    columns = weight.shape[1]
    own = rows // blocks

    def body(column_ref, feat_ref, weight_ref, p01, p23, p67, p4, p5, result):
        def part(k):
            return result[pl.ds(pl.multiple_of((column_ref[0] ^ k) * own, own), own)]

        def columns_at(here):
            result[...] = product(feat_ref[...], weight_ref[:, here]).astype(BF16)
            for k in range(2):
                p01[k, :, here] = part(k)
                p23[k, :, here] = part(2 + k)
                p67[k, :, here] = part(6 + k)
            p4[:, here] = part(4)
            p5[:, here] = part(5)

        tiles(columns // tile, tile, columns_at)

    outs = [shape(2, own, columns)] * 3 + [shape(own, columns)] * 2
    specs = [pl.BlockSpec(memory_space=pltpu.SMEM)] + [pl.BlockSpec(memory_space=pltpu.VMEM)] * 2
    scratch = [pltpu.VMEM((rows, tile), BF16)]
    return call(name, body, outs, (column, feat, weight), 2 * rows * width * columns, 16, None, specs, scratch)


def relay_add(p23, p67, r4, r5, out23, out67):
    out23[0] = (wide(p23, 0) + wide(r4)).astype(BF16)
    out23[1] = p23[1]
    out67[0] = p67[0]
    out67[1] = (wide(p67, 1) + wide(r5)).astype(BF16)


def relay_split(p23, p67, r4, r5, a23, a67, b23, b67):
    half = r4.shape[0] // 2
    for h, (out23, out67) in enumerate(((a23, a67), (b23, b67))):
        rows = slice(h * half, (h + 1) * half)
        out23[0] = (p23[0, rows].astype(F32) + wide(r4, rows)).astype(BF16)
        out23[1] = p23[1, rows]
        out67[0] = p67[0, rows]
        out67[1] = (p67[1, rows].astype(F32) + wide(r5, rows)).astype(BF16)


def add_half(h):
    def body(p01, r23, r67, out):
        half = out.shape[1]
        for k in range(2):
            own = p01[k, h * half : (h + 1) * half].astype(F32)
            out[k] = (own + wide(r23, k) + wide(r67, k)).astype(BF16)

    return body


def norm_half(p01, got01, emb_out, unit_out):
    for k in range(2):
        embedded = wide(p01, k) + wide(got01, 1 - k)
        emb_out[k] = embedded
        unit_out[k] = unit_of(embedded)[0].astype(BF16)


def back_half(g01, got01, emb, out):
    for k in range(2):
        out[k] = norm_back(wide(g01, k) + wide(got01, 1 - k), emb[k]).astype(BF16)


def cut(near, other, first_out, last_out):
    first_out[...] = near[0]
    last_out[...] = other[1]


def stack(first, second, out):
    out[0] = first[...]
    out[1] = second[...]


def grouped(refs, halves):
    return [refs[i : i + halves] for i in range(0, len(refs), halves)]


def block(group, k=None):
    parts = [ref[...] if k is None else ref[k] for ref in group]
    return parts[0] if len(parts) == 1 else jnp.concatenate(parts, axis=0)


def near_far_order(groups):
    pairs = [block(g, k) for g in groups[:3] for k in range(2)]
    if len(groups) == 4:
        return pairs + [block(groups[3], k) for k in range(2)]
    return pairs + [block(g) for g in groups[3:]]


def unit_of(embedded):
    inverse = lax.rsqrt(jnp.sum(embedded * embedded, axis=1, keepdims=True) + EPS)
    return embedded * inverse, inverse


def norm_back(unit_grad, embedded):
    unit, inverse = unit_of(embedded)
    return inverse * (unit_grad - unit * jnp.sum(unit * unit_grad, axis=1, keepdims=True))


def flat(ref):
    return ref[...].reshape(-1, ref.shape[-1])


def factors(scale, bias, txt, img):
    affinity = lax.dot_general(txt, img, (((1,), (1,)), ((), ())), preferred_element_type=F32)
    logits = scale * affinity + bias
    return logits, (scale / (1.0 + jnp.exp(-logits))).astype(BF16)


def product(first, second):
    return jnp.dot(first, second, preferred_element_type=F32)


def pair_call(name, body, outs, scale, bias, arrays, flops, limit, scratch=()):
    smem = pl.BlockSpec(memory_space=pltpu.SMEM)
    vmem = pl.BlockSpec(memory_space=pltpu.VMEM)
    moved = sum(a.size * a.dtype.itemsize for a in list(arrays) + outs)
    return pl.pallas_call(
        body,
        in_specs=[smem, smem] + [vmem] * len(arrays),
        out_shape=outs,
        scratch_shapes=list(scratch),
        compiler_params=pltpu.CompilerParams(vmem_limit_bytes=limit * MIB),
        cost_estimate=pl.CostEstimate(flops=flops, bytes_accessed=moved, transcendentals=0),
        name=name,
    )(scale, bias, *arrays)


def image_rows(image_refs, image_all):
    own = image_all.shape[0] // 8
    for k, part in enumerate(near_far_order(grouped(image_refs, 2))):
        image_all[k * own : (k + 1) * own] = part


def factor_rows(scale, bias, texts, image_all, factor_all, flipped, tile, unroll):
    def images_at(here):
        factor = factors(scale, bias, flat(texts), image_all[here])[1]
        factor_all[:, here] = factor
        flipped[here] = factor.T

    tiles(image_all.shape[0] // tile, tile, images_at, unroll)


def match(scale, bias, texts, image_all, factor_all, flipped):
    own = texts.shape[1]
    logits = factors(scale, bias, texts[0], image_all[:own])[0]
    row = lax.broadcasted_iota(jnp.int32, logits.shape, 0)
    column = lax.broadcasted_iota(jnp.int32, logits.shape, 1)
    pull = (-scale / (1.0 + jnp.exp(logits))).astype(BF16)
    factor = jnp.where(row == column, pull, factor_all[:own, :own])
    factor_all[:own, :own] = factor
    flipped[:own, :own] = factor.T


def text_grads(factor_all, image_all, out, tile=512, unroll=False):
    def columns_at(here):
        grads = product(factor_all[...], image_all[:, here]).astype(BF16)
        out[:, :, here] = grads.reshape(*out.shape[:2], tile)

    tiles(out.shape[-1] // tile, tile, columns_at, unroll)


def pairs_even(scale, bias, texts, images):
    count, own, width = texts.shape
    rows = count * own

    def body(scale_ref, bias_ref, texts, *refs):
        image_refs, (factor_all, flipped, image_all) = refs[:10], refs[10:]
        image_rows(image_refs, image_all)
        scale, bias = scale_ref[0], bias_ref[0]
        factor_rows(scale, bias, texts, image_all, factor_all, flipped, 512, False)
        match(scale, bias, texts, image_all, factor_all, flipped)

    outs = [shape(rows, rows), shape(rows, rows), shape(rows, width)]
    return pair_call("pairs_even", body, outs, scale, bias, (texts, *images), 2 * rows * rows * width, 24)


def pairs_odd(scale, bias, texts, image_all, after):
    count, own, width = texts.shape
    rows = count * own

    def body(scale_ref, bias_ref, texts, image_all, _, flipped, out, factor_all):
        factor_rows(scale_ref[0], bias_ref[0], texts, image_all, factor_all, flipped, 256, True)
        text_grads(factor_all, image_all, out, 256, True)

    outs = [shape(rows, rows), shape(count, own, width)]
    scratch = [pltpu.VMEM((rows, rows), BF16)]
    arrays = (texts, image_all, after)
    return pair_call("pairs_odd", body, outs, scale, bias, arrays, 4 * rows * rows * width, 24, scratch)


def pairs_image(name, flips, texts, start, stop, outs, after, tile, unroll):
    own, width = texts[0].shape[-2:]

    def body(flip_even, flip_odd, even, odd, *out_refs):
        def columns_at(here):
            factor = jnp.concatenate([flip_even[start:stop], flip_odd[start:stop]], axis=1)
            rows = jnp.concatenate([ref[:, :, here].reshape(-1, tile) for ref in (even, odd)], axis=0)
            total = product(factor, rows).astype(BF16)
            place = 0
            for ref in out_refs:
                size = ref.size // width
                ref[..., here] = total[place : place + size].reshape(*ref.shape[:-1], tile)
                place += size

        tiles(width // tile, tile, columns_at, unroll)

    flops = 2 * (stop - start) * 16 * own * width
    return call(name, body, outs, (*flips, *texts), flops, 24, after)


def weight_part(name, column, place, pieces, halves, feat, after):
    count, width = len(pieces), pieces[-1].shape[-1]
    rows, features = feat.shape
    own = rows // 8
    strip = width // 16
    tile = 256

    def body(column_ref, place_ref, *refs):
        feat_ref, same, other, flipped, moved, result = refs[count:]
        for n, part in enumerate(near_far_order(grouped(refs[:count], halves))):
            k = NEAR_FAR[n]
            flipped[:, k * own : (k + 1) * own] = part.T
        def features_at(here):
            for k in range(rows // own):
                start = pl.multiple_of((column_ref[0] ^ k) * own, own)
                moved[k * own : (k + 1) * own] = feat_ref[pl.ds(start, own), here]
            result[...] = product(flipped[...], moved[...]).astype(BF16)
            for j, k in enumerate((0, 2, 4, 6, 12, 14, 8, 10)):
                mine = pl.multiple_of((place_ref[0] ^ k) * strip, strip)
                theirs = pl.multiple_of((place_ref[0] ^ (k + 1)) * strip, strip)
                same[j, :, here] = result[pl.ds(mine, strip)]
                other[j, :, here] = result[pl.ds(theirs, strip)]

        tiles(features // tile, tile, features_at, True)

    smem, vmem = pl.BlockSpec(memory_space=pltpu.SMEM), pl.BlockSpec(memory_space=pltpu.VMEM)
    specs = [smem, smem] + [vmem] * (len(pieces) + 1)
    scratch = [
        pltpu.VMEM((width, rows), BF16),
        pltpu.VMEM((rows, tile), BF16),
        pltpu.VMEM((width, tile), BF16),
    ]
    outs = [shape(8, strip, features)] * 2
    flops = 2 * rows * width * features
    return call(name, body, outs, (column, place, *pieces, feat), flops, 16, after, specs, scratch)


def feature_grad(name, column, pieces, halves, weight):
    count, width = len(pieces), pieces[-1].shape[-1]
    features = weight.shape[0]
    own = pieces[0].shape[1] * halves
    rows = 8 * own
    tile = 256

    def body(column_ref, *refs):
        weight_ref, out = refs[count:]
        def features_at(here):
            egrad = jnp.concatenate(near_far_order(grouped(refs[:count], halves)), axis=0)
            result = lax.dot_general(
                egrad, weight_ref[here], (((1,), (1,)), ((), ())), preferred_element_type=F32
            ).astype(BF16)
            for n, k in enumerate(NEAR_FAR):
                start = pl.multiple_of((column_ref[0] ^ k) * own, own)
                out[pl.ds(start, own), here] = result[n * own : (n + 1) * own]

        tiles(features // tile, tile, features_at)

    smem, vmem = pl.BlockSpec(memory_space=pltpu.SMEM), pl.BlockSpec(memory_space=pltpu.VMEM)
    outs, ins = [shape(rows, features)], (column, *pieces, weight)
    return call(name, body, outs, ins, 2 * rows * width * features, 16, None, [smem] + [vmem] * (len(pieces) + 1))[0]


def chip_weight(name, same, other, after=None):
    strip, features = same.shape[1:]

    def body(same, got, *outs):
        for j, out in enumerate(outs):
            out[...] = (wide(same, slice(2 * j, 2 * j + 2)) + wide(got, slice(2 * j, 2 * j + 2))).astype(BF16)

    outs = [shape(2, strip, features)] * 4
    return call(name, body, outs, (same, swap(other, "blk", 1)), after=after)


def sum_weight(p02, p46, p1214, p810):
    strip, features = p02.shape[1:]

    def along_z(p02, p46, p1214, p810, p0_out, p2_out):
        total = wide(p02) + wide(p46) + wide(p1214) + wide(p810)
        p0_out[...] = total[0]
        p2_out[...] = total[1].astype(BF16)

    def along_y(p0, p2, out):
        out[...] = p0[...] + wide(p2)

    p46, p1214, p810 = swap(p46, "blk", 4), swap(p1214, "blk", 12), swap(p810, "blk", 8)
    outs = [shape(strip, features, dtype=F32), shape(strip, features)]
    p0, p2 = call("weight_z", along_z, outs, (p02, p46, p1214, p810))
    p2 = swap(p2, "blk", 2)
    return call("weight_y", along_y, outs[:1], (p0, p2))[0].T


def chip_weight_y(name, same, other, after=None):
    strip, features = same.shape[1:]

    def body(same, got, mine, theirs):
        for j in range(4):
            for k, out in enumerate((mine, theirs)):
                out[j] = (wide(same, 2 * j + k) + wide(got, 2 * j + k)).astype(BF16)

    outs = [shape(4, strip, features)] * 2
    return call(name, body, outs, (same, swap(other, "blk", 1)), after=after)


def sum_weight_y(mine, theirs):
    strip, features = mine.shape[1:]
    one = (strip, features)

    def along_y(mine, got, p0, p4, p12, p8):
        p0[...] = wide(mine, 0) + wide(got, 0)
        for j, out in ((1, p4), (2, p12), (3, p8)):
            out[...] = (wide(mine, j) + wide(got, j)).astype(BF16)

    def along_z(p0, p4, p12, p8, out):
        out[...] = p0[...] + wide(p4) + wide(p12) + wide(p8)

    outs = [shape(*one, dtype=F32)] + [shape(*one)] * 3
    p0, p4, p12, p8 = call("weight_image_y", along_y, outs, (mine, swap(theirs, "blk", 2)))
    p4, p12, p8 = swap(p4, "blk", 4), swap(p12, "blk", 12), swap(p8, "blk", 8)
    return call("weight_image_z", along_z, outs[:1], (p0, p4, p12, p8))[0].T


def local(img_feat, txt_feat, img_weight, txt_weight, natural_exponent_multiplier, bias):
    scale = jnp.exp(natural_exponent_multiplier)
    blocks = lax.axis_size("mp")
    column = lax.axis_index("mp").astype(jnp.int32)[None]
    place = lax.axis_index("blk").astype(jnp.int32)[None]
    own = img_feat.shape[0] // blocks
    width = img_weight.shape[1]
    one, two = (own, width), (2, own, width)

    half = (2, own // 2, width)
    own_half = (own // 2, width)

    t01, t23, t67, t4, t5 = embed("embed_text", txt_feat, txt_weight, column, blocks)
    t4, t5 = swap(t4, "mp", 6), swap(t5, "mp", 2)
    i01, i23, i67, i4, i5 = embed("embed_image", img_feat, img_weight, column, blocks)
    t23, t67 = call("relay_text", relay_add, [shape(*two)] * 2, (t23, t67, t4, t5))
    t23, t67 = swap(t23, "mp", 2), swap(t67, "mp", 6)
    i4, i5 = swap(i4, "mp", 6), swap(i5, "mp", 2)

    def second(t01, t23, t67, t0_out, t1_out):
        t0_out[...] = wide(t01, 0) + wide(t23, 0) + wide(t67, 0)
        t1_out[...] = (wide(t01, 1) + wide(t23, 1) + wide(t67, 1)).astype(BF16)

    t0, t1 = call("sums_second", second, [shape(*one, dtype=F32), shape(*one)], (t01, t23, t67))
    t1_got = swap(t1, "mp", 1)
    sent = call("relay_image", relay_split, [shape(*half)] * 4, (i23, i67, i4, i5), after=t1)
    got = [(swap(sent[2 * h], "mp", 2), swap(sent[2 * h + 1], "mp", 6)) for h in range(2)]

    def third(t0, t1, text_out, unit_out):
        embedded = t0[...] + wide(t1)
        text_out[...] = embedded
        unit_out[...] = unit_of(embedded)[0].astype(BF16)

    txt_emb, a0 = call("sums_third", third, [shape(*one, dtype=F32), shape(*one)], (t0, t1_got), after=sent[0])
    a2 = swap(a0, "blk", 2)
    (x_a,) = call("image_x_a", add_half(0), [shape(*half)], (i01, *got[0]), after=a0)
    y_a = swap(x_a, "mp", 1)
    (a02,) = call("stack_text", stack, [shape(*two)], (a0, a2), after=x_a)
    a46, a1214 = swap(a02, "blk", 4), swap(a02, "blk", 12)
    (x_b,) = call("image_x_b", add_half(1), [shape(*half)], (i01, *got[1]), after=a02)
    y_b = swap(x_b, "mp", 1)
    outs = [shape(*half, dtype=F32), shape(*half)]
    emb_a, u01_a = call("image_unit_a", norm_half, outs, (x_a, y_a), after=x_b)
    u23_a, u67_a = swap(u01_a, "mp", 2), swap(u01_a, "mp", 6)
    emb_b, u01_b = call("image_unit_b", norm_half, outs, (x_b, y_b), after=u01_a)
    u23_b, u67_b = swap(u01_b, "mp", 2), swap(u01_b, "mp", 6)
    outs = [shape(*own_half)] * 2
    u2_a, u7_a = call("cut_image_a", cut, outs, (u23_a, u67_a), after=u01_b)
    u4_a, u5_a = swap(u2_a, "mp", 6), swap(u7_a, "mp", 2)
    a4, a14 = call("cut_text", cut, [shape(*one)] * 2, (a46, a1214), after=u2_a)
    a8, a10 = swap(a4, "blk", 12), swap(a14, "blk", 4)
    u2_b, u7_b = call("cut_image_b", cut, outs, (u23_b, u67_b), after=a4)
    u4_b, u5_b = swap(u2_b, "mp", 6), swap(u7_b, "mp", 2)

    def collect(a02, a46, a1214, a8, a10, out):
        for k, ref in enumerate((a02, a46, a1214)):
            out[2 * k : 2 * k + 2] = ref[...]
        out[6] = a8[...]
        out[7] = a10[...]

    (even,) = call("collect", collect, [shape(8, *one)], (a02, a46, a1214, a8, a10), after=(u4_a, u5_a, u4_b, u5_b))
    odd = swap(even, "blk", 1)
    images = (u01_a, u01_b, u23_a, u23_b, u67_a, u67_b, u4_a, u4_b, u5_a, u5_b)
    factor_even, flip_even, image_all = pairs_even(scale, bias, even, images)
    flip_odd, odd_sum = pairs_odd(scale, bias, odd, image_all, flip_even)
    odd_got = swap(odd_sum, "blk", 1)
    flips, texts = (flip_even, flip_odd), (even, odd)
    g4, g5 = pairs_image("pairs_far_images", flips, texts, 6 * own, 8 * own, [shape(*one)] * 2, odd_sum, 256, True)
    g4_got, g5_got = swap(g4, "mp", 6), swap(g5, "mp", 2)
    flops = 128 * own * own * width
    (even_sum,) = call("text_grads_even", text_grads, [shape(8, *one)], (factor_even, image_all), flops, 20, g4)

    def fifth(even, got, p8, p10):
        p8[...] = (wide(even, 6) + wide(got, 6)).astype(BF16)
        p10[...] = (wide(even, 7) + wide(got, 7)).astype(BF16)

    p8, p10 = call("sums_fifth", fifth, [shape(*one)] * 2, (even_sum, odd_got))
    g01, g23, g67 = pairs_image("pairs_near_images", flips, texts, 0, 6 * own, [shape(*two)] * 3, p8, 512, False)
    p8_got, p10_got = swap(p8, "blk", 12), swap(p10, "blk", 4)
    sent = call("relay_image_grads", relay_split, [shape(*half)] * 4, (g23, g67, g4_got, g5_got))
    got = [(swap(sent[2 * h], "mp", 2), swap(sent[2 * h + 1], "mp", 6)) for h in range(2)]

    def sixth(even, got, p8, p10, p02, p46, p1214):
        for k in range(2):
            p02[k] = (wide(even, k) + wide(got, k)).astype(BF16)
        p46[0] = (wide(even, 2) + wide(got, 2) + wide(p8)).astype(BF16)
        p46[1] = (wide(even, 3) + wide(got, 3)).astype(BF16)
        p1214[0] = (wide(even, 4) + wide(got, 4)).astype(BF16)
        p1214[1] = (wide(even, 5) + wide(got, 5) + wide(p10)).astype(BF16)

    outs = [shape(*two)] * 3
    p02, p46, p1214 = call("sums_sixth", sixth, outs, (even_sum, odd_got, p8_got, p10_got), after=sent[0])
    p46, p1214 = swap(p46, "blk", 4), swap(p1214, "blk", 12)
    (x_a,) = call("image_grads_x_a", add_half(0), [shape(*half)], (g01, *got[0]), after=p02)
    y_a = swap(x_a, "mp", 1)
    (x_b,) = call("image_grads_x_b", add_half(1), [shape(*half)], (g01, *got[1]), after=x_a)
    y_b = swap(x_b, "mp", 1)
    (e01_a,) = call("image_back_a", back_half, [shape(*half)], (x_a, y_a, emb_a), after=x_b)
    e23_a, e67_a, e45_a = swap(e01_a, "mp", 2), swap(e01_a, "mp", 6), swap(e01_a, "mp", 4)

    def seventh(p02, p46, p1214, p0_out, p2_out):
        p0_out[...] = wide(p02, 0) + wide(p46, 0) + wide(p1214, 0)
        p2_out[...] = (wide(p02, 1) + wide(p46, 1) + wide(p1214, 1)).astype(BF16)

    outs = [shape(*one, dtype=F32), shape(*one)]
    p0, p2 = call("sums_seventh", seventh, outs, (p02, p46, p1214), after=e01_a)
    p2_got = swap(p2, "blk", 2)
    (e01_b,) = call("image_back_b", back_half, [shape(*half)], (x_b, y_b, emb_b), after=p2)
    e23_b, e67_b, e45_b = swap(e01_b, "mp", 2), swap(e01_b, "mp", 6), swap(e01_b, "mp", 4)

    def text_back(p0, p2, txt_emb, out):
        out[...] = norm_back(p0[...] + wide(p2), txt_emb[...]).astype(BF16)

    (d0,) = call("text_back", text_back, [shape(*one)], (p0, p2_got, txt_emb), after=(e01_b, e23_a, e67_a, e45_a))
    d1 = swap(d0, "mp", 1)
    (d01,) = call("stack_text_grads", stack, [shape(*two)], (d0, d1), after=(e23_b, e67_b, e45_b))
    d23, d67 = swap(d01, "mp", 2), swap(d01, "mp", 6)

    e_all = (e01_a, e01_b, e23_a, e23_b, e67_a, e67_b, e45_a, e45_b)
    same, other = weight_part("weight_image", column, place, e_all, 2, img_feat, d01)
    d2, d7 = call("cut_text_grads", cut, [shape(*one)] * 2, (d23, d67), ORDER_COST, after=same)
    d4, d5 = swap(d2, "mp", 6), swap(d7, "mp", 2)
    image_chip = chip_weight_y("weight_image_chip", same, other)
    img_weight_grad = sum_weight_y(*image_chip)
    d_all = (d01, d23, d67, d4, d5)
    same, other = weight_part("weight_text", column, place, d_all, 1, txt_feat, image_chip[0])
    txt_weight_grad = sum_weight(*chip_weight("weight_text_chip", same, other))
    return (
        feature_grad("feature_image", column, e_all, 2, img_weight),
        feature_grad("feature_text", column, d_all, 1, txt_weight),
        img_weight_grad,
        txt_weight_grad,
    )


def solution(mesh):
    return jax.shard_map(
        local,
        mesh=mesh,
        in_specs=(P("blk", "mp"), P("blk", "mp"), P("mp", None), P("mp", None), P(), P()),
        out_specs=(P("blk", "mp"), P("blk", "mp"), P("mp", "blk"), P("mp", "blk")),
        check_vma=False,
    )
```

```python
import jax
import jax.numpy as jnp
from jax import lax
from jax.experimental import pallas as pl
from jax.experimental.pallas import tpu as pltpu
from jax.sharding import PartitionSpec as P

EPS = 1e-06
BF16 = jnp.bfloat16
F32 = jnp.float32
MIB = 1024 * 1024
ORDER_COST = 10 * 10**9
NEAR_FAR = (0, 1, 2, 3, 6, 7, 4, 5)


def swap(value, axis, offset):
    count = lax.axis_size(axis)
    return lax.ppermute(value, axis, [(i, i ^ offset) for i in range(count)])


def shape(*dims, dtype=BF16):
    return jax.ShapeDtypeStruct(dims, dtype)


def call(name, body, outs, ins, flops=0, limit=10, after=None, in_specs=None, scratch=()):
    ins, specs = list(ins), in_specs or [pl.BlockSpec(memory_space=pltpu.VMEM)] * len(ins)
    run = body
    if after is not None:
        after = list(after) if isinstance(after, tuple) else [after]
        ins, specs = after + ins, [pl.BlockSpec(memory_space=pltpu.VMEM)] * len(after) + list(specs)

        def run(*refs):
            body(*refs[len(after) :])

    moved = sum(a.size * a.dtype.itemsize for a in ins + list(outs))
    return pl.pallas_call(
        run,
        out_shape=outs,
        in_specs=specs,
        scratch_shapes=list(scratch),
        compiler_params=pltpu.CompilerParams(vmem_limit_bytes=limit * MIB),
        cost_estimate=pl.CostEstimate(flops=flops, bytes_accessed=moved, transcendentals=0),
        name=name,
    )(*ins)


def tiles(count, size, body, unroll=False):
    if unroll:
        for index in range(count):
            body(slice(index * size, (index + 1) * size))
        return

    def step(index, carry):
        body(pl.ds(pl.multiple_of(index * size, size), size))
        return carry

    lax.fori_loop(0, count, step, 0)


def wide(ref, block=None):
    return (ref[...] if block is None else ref[block]).astype(F32)


def embed(name, feat, weight, column, blocks, tile=256):
    rows, width = feat.shape
    columns = weight.shape[1]
    own = rows // blocks

    def body(column_ref, feat_ref, weight_ref, p01, p23, p67, p4, p5, result):
        def part(k):
            return result[pl.ds(pl.multiple_of((column_ref[0] ^ k) * own, own), own)]

        def columns_at(here):
            result[...] = product(feat_ref[...], weight_ref[:, here]).astype(BF16)
            for k in range(2):
                p01[k, :, here] = part(k)
                p23[k, :, here] = part(2 + k)
                p67[k, :, here] = part(6 + k)
            p4[:, here] = part(4)
            p5[:, here] = part(5)

        tiles(columns // tile, tile, columns_at)

    outs = [shape(2, own, columns)] * 3 + [shape(own, columns)] * 2
    specs = [pl.BlockSpec(memory_space=pltpu.SMEM)] + [pl.BlockSpec(memory_space=pltpu.VMEM)] * 2
    scratch = [pltpu.VMEM((rows, tile), BF16)]
    return call(name, body, outs, (column, feat, weight), 2 * rows * width * columns, 16, None, specs, scratch)


def relay_add(p23, p67, r4, r5, out23, out67):
    out23[0] = (wide(p23, 0) + wide(r4)).astype(BF16)
    out23[1] = p23[1]
    out67[0] = p67[0]
    out67[1] = (wide(p67, 1) + wide(r5)).astype(BF16)


def relay_split(p23, p67, r4, r5, a23, a67, b23, b67):
    half = r4.shape[0] // 2
    for h, (out23, out67) in enumerate(((a23, a67), (b23, b67))):
        rows = slice(h * half, (h + 1) * half)
        out23[0] = (p23[0, rows].astype(F32) + wide(r4, rows)).astype(BF16)
        out23[1] = p23[1, rows]
        out67[0] = p67[0, rows]
        out67[1] = (p67[1, rows].astype(F32) + wide(r5, rows)).astype(BF16)


def add_half(h):
    def body(p01, r23, r67, out):
        half = out.shape[1]
        for k in range(2):
            own = p01[k, h * half : (h + 1) * half].astype(F32)
            out[k] = (own + wide(r23, k) + wide(r67, k)).astype(BF16)

    return body


def norm_half(p01, got01, emb_out, unit_out):
    for k in range(2):
        embedded = wide(p01, k) + wide(got01, 1 - k)
        emb_out[k] = embedded
        unit_out[k] = unit_of(embedded)[0].astype(BF16)


def back_half(g01, got01, emb, out):
    for k in range(2):
        out[k] = norm_back(wide(g01, k) + wide(got01, 1 - k), emb[k]).astype(BF16)


def cut(near, other, first_out, last_out):
    first_out[...] = near[0]
    last_out[...] = other[1]


def stack(first, second, out):
    out[0] = first[...]
    out[1] = second[...]


def grouped(refs, halves):
    return [refs[i : i + halves] for i in range(0, len(refs), halves)]


def block(group, k=None):
    parts = [ref[...] if k is None else ref[k] for ref in group]
    return parts[0] if len(parts) == 1 else jnp.concatenate(parts, axis=0)


def near_far_order(groups):
    pairs = [block(g, k) for g in groups[:3] for k in range(2)]
    if len(groups) == 4:
        return pairs + [block(groups[3], k) for k in range(2)]
    return pairs + [block(g) for g in groups[3:]]


def unit_of(embedded):
    inverse = lax.rsqrt(jnp.sum(embedded * embedded, axis=1, keepdims=True) + EPS)
    return embedded * inverse, inverse


def norm_back(unit_grad, embedded):
    unit, inverse = unit_of(embedded)
    return inverse * (unit_grad - unit * jnp.sum(unit * unit_grad, axis=1, keepdims=True))


def flat(ref):
    return ref[...].reshape(-1, ref.shape[-1])


def factors(scale, bias, txt, img):
    affinity = lax.dot_general(txt, img, (((1,), (1,)), ((), ())), preferred_element_type=F32)
    logits = scale * affinity + bias
    return logits, (scale / (1.0 + jnp.exp(-logits))).astype(BF16)


def product(first, second):
    return jnp.dot(first, second, preferred_element_type=F32)


def pair_call(name, body, outs, scale, bias, arrays, flops, limit, scratch=()):
    smem = pl.BlockSpec(memory_space=pltpu.SMEM)
    vmem = pl.BlockSpec(memory_space=pltpu.VMEM)
    moved = sum(a.size * a.dtype.itemsize for a in list(arrays) + outs)
    return pl.pallas_call(
        body,
        in_specs=[smem, smem] + [vmem] * len(arrays),
        out_shape=outs,
        scratch_shapes=list(scratch),
        compiler_params=pltpu.CompilerParams(vmem_limit_bytes=limit * MIB),
        cost_estimate=pl.CostEstimate(flops=flops, bytes_accessed=moved, transcendentals=0),
        name=name,
    )(scale, bias, *arrays)


def image_rows(image_refs, image_all):
    own = image_all.shape[0] // 8
    for k, part in enumerate(near_far_order(grouped(image_refs, 2))):
        image_all[k * own : (k + 1) * own] = part


def factor_rows(scale, bias, texts, image_all, factor_all, flipped, tile, unroll):
    def images_at(here):
        factor = factors(scale, bias, flat(texts), image_all[here])[1]
        factor_all[:, here] = factor
        flipped[here] = factor.T

    tiles(image_all.shape[0] // tile, tile, images_at, unroll)


def match(scale, bias, texts, image_all, factor_all, flipped):
    own = texts.shape[1]
    logits = factors(scale, bias, texts[0], image_all[:own])[0]
    row = lax.broadcasted_iota(jnp.int32, logits.shape, 0)
    column = lax.broadcasted_iota(jnp.int32, logits.shape, 1)
    pull = (-scale / (1.0 + jnp.exp(logits))).astype(BF16)
    factor = jnp.where(row == column, pull, factor_all[:own, :own])
    factor_all[:own, :own] = factor
    flipped[:own, :own] = factor.T


def text_grads(factor_all, image_all, out, tile=512, unroll=False):
    def columns_at(here):
        grads = product(factor_all[...], image_all[:, here]).astype(BF16)
        out[:, :, here] = grads.reshape(*out.shape[:2], tile)

    tiles(out.shape[-1] // tile, tile, columns_at, unroll)


def pairs_even(scale, bias, texts, images):
    count, own, width = texts.shape
    rows = count * own

    def body(scale_ref, bias_ref, texts, *refs):
        image_refs, (factor_all, flipped, image_all) = refs[:10], refs[10:]
        image_rows(image_refs, image_all)
        scale, bias = scale_ref[0], bias_ref[0]
        factor_rows(scale, bias, texts, image_all, factor_all, flipped, 512, False)
        match(scale, bias, texts, image_all, factor_all, flipped)

    outs = [shape(rows, rows), shape(rows, rows), shape(rows, width)]
    return pair_call("pairs_even", body, outs, scale, bias, (texts, *images), 2 * rows * rows * width, 24)


def pairs_odd(scale, bias, texts, image_all, after):
    count, own, width = texts.shape
    rows = count * own

    def body(scale_ref, bias_ref, texts, image_all, _, flipped, out, factor_all):
        factor_rows(scale_ref[0], bias_ref[0], texts, image_all, factor_all, flipped, 256, True)
        text_grads(factor_all, image_all, out, 256, True)

    outs = [shape(rows, rows), shape(count, own, width)]
    scratch = [pltpu.VMEM((rows, rows), BF16)]
    arrays = (texts, image_all, after)
    return pair_call("pairs_odd", body, outs, scale, bias, arrays, 4 * rows * rows * width, 24, scratch)


def pairs_image(name, flips, texts, start, stop, outs, after, tile, unroll):
    own, width = texts[0].shape[-2:]

    def body(flip_even, flip_odd, even, odd, *out_refs):
        def columns_at(here):
            factor = jnp.concatenate([flip_even[start:stop], flip_odd[start:stop]], axis=1)
            rows = jnp.concatenate([ref[:, :, here].reshape(-1, tile) for ref in (even, odd)], axis=0)
            total = product(factor, rows).astype(BF16)
            place = 0
            for ref in out_refs:
                size = ref.size // width
                ref[..., here] = total[place : place + size].reshape(*ref.shape[:-1], tile)
                place += size

        tiles(width // tile, tile, columns_at, unroll)

    flops = 2 * (stop - start) * 16 * own * width
    return call(name, body, outs, (*flips, *texts), flops, 24, after)


def weight_part(name, column, place, pieces, halves, feat, after):
    count, width = len(pieces), pieces[-1].shape[-1]
    rows, features = feat.shape
    own = rows // 8
    strip = width // 16
    tile = 256

    def body(column_ref, place_ref, *refs):
        feat_ref, same, other, flipped, moved, result = refs[count:]
        for n, part in enumerate(near_far_order(grouped(refs[:count], halves))):
            k = NEAR_FAR[n]
            flipped[:, k * own : (k + 1) * own] = part.T
        def features_at(here):
            for k in range(rows // own):
                start = pl.multiple_of((column_ref[0] ^ k) * own, own)
                moved[k * own : (k + 1) * own] = feat_ref[pl.ds(start, own), here]
            result[...] = product(flipped[...], moved[...]).astype(BF16)
            for j, k in enumerate((0, 2, 4, 6, 12, 14, 8, 10)):
                mine = pl.multiple_of((place_ref[0] ^ k) * strip, strip)
                theirs = pl.multiple_of((place_ref[0] ^ (k + 1)) * strip, strip)
                same[j, :, here] = result[pl.ds(mine, strip)]
                other[j, :, here] = result[pl.ds(theirs, strip)]

        tiles(features // tile, tile, features_at, True)

    smem, vmem = pl.BlockSpec(memory_space=pltpu.SMEM), pl.BlockSpec(memory_space=pltpu.VMEM)
    specs = [smem, smem] + [vmem] * (len(pieces) + 1)
    scratch = [
        pltpu.VMEM((width, rows), BF16),
        pltpu.VMEM((rows, tile), BF16),
        pltpu.VMEM((width, tile), BF16),
    ]
    outs = [shape(8, strip, features)] * 2
    flops = 2 * rows * width * features
    return call(name, body, outs, (column, place, *pieces, feat), flops, 16, after, specs, scratch)


def feature_grad(name, column, pieces, halves, weight):
    count, width = len(pieces), pieces[-1].shape[-1]
    features = weight.shape[0]
    own = pieces[0].shape[1] * halves
    rows = 8 * own
    tile = 256

    def body(column_ref, *refs):
        weight_ref, out, mark = refs[count:]
        mark[...] = jnp.zeros_like(mark)
        def features_at(here):
            egrad = jnp.concatenate(near_far_order(grouped(refs[:count], halves)), axis=0)
            result = lax.dot_general(
                egrad, weight_ref[here], (((1,), (1,)), ((), ())), preferred_element_type=F32
            ).astype(BF16)
            for n, k in enumerate(NEAR_FAR):
                start = pl.multiple_of((column_ref[0] ^ k) * own, own)
                out[pl.ds(start, own), here] = result[n * own : (n + 1) * own]

        tiles(features // tile, tile, features_at)

    smem, vmem = pl.BlockSpec(memory_space=pltpu.SMEM), pl.BlockSpec(memory_space=pltpu.VMEM)
    outs, ins = [shape(rows, features), shape(16, 128)], (column, *pieces, weight)
    return call(name, body, outs, ins, 2 * rows * width * features, 16, None, [smem] + [vmem] * (len(pieces) + 1))


def chip_weight(name, same, other, after=None):
    strip, features = same.shape[1:]

    def body(same, got, *outs):
        for j, out in enumerate(outs):
            out[...] = (wide(same, slice(2 * j, 2 * j + 2)) + wide(got, slice(2 * j, 2 * j + 2))).astype(BF16)

    outs = [shape(2, strip, features)] * 4
    return call(name, body, outs, (same, swap(other, "blk", 1)), after=after)


def sum_weight(p02, p46, p1214, p810):
    strip, features = p02.shape[1:]

    def along_z(p02, p46, p1214, p810, p0_out, p2_out):
        total = wide(p02) + wide(p46) + wide(p1214) + wide(p810)
        p0_out[...] = total[0]
        p2_out[...] = total[1].astype(BF16)

    def along_y(p0, p2, out):
        out[...] = p0[...] + wide(p2)

    p46, p1214, p810 = swap(p46, "blk", 4), swap(p1214, "blk", 12), swap(p810, "blk", 8)
    outs = [shape(strip, features, dtype=F32), shape(strip, features)]
    p0, p2 = call("weight_z", along_z, outs, (p02, p46, p1214, p810))
    p2 = swap(p2, "blk", 2)
    return call("weight_y", along_y, outs[:1], (p0, p2))[0].T


def chip_weight_y(name, same, other, after=None):
    strip, features = same.shape[1:]

    def body(same, got, mine, theirs):
        for j in range(4):
            for k, out in enumerate((mine, theirs)):
                out[j] = (wide(same, 2 * j + k) + wide(got, 2 * j + k)).astype(BF16)

    outs = [shape(4, strip, features)] * 2
    return call(name, body, outs, (same, swap(other, "blk", 1)), after=after)


def sum_weight_y(mine, theirs):
    strip, features = mine.shape[1:]
    one = (strip, features)

    def along_y(mine, got, p0, p4, p12, p8):
        p0[...] = wide(mine, 0) + wide(got, 0)
        for j, out in ((1, p4), (2, p12), (3, p8)):
            out[...] = (wide(mine, j) + wide(got, j)).astype(BF16)

    def along_z(p0, p4, p12, p8, out):
        out[...] = p0[...] + wide(p4) + wide(p12) + wide(p8)

    outs = [shape(*one, dtype=F32)] + [shape(*one)] * 3
    p0, p4, p12, p8 = call("weight_image_y", along_y, outs, (mine, swap(theirs, "blk", 2)))
    p4, p12, p8 = swap(p4, "blk", 4), swap(p12, "blk", 12), swap(p8, "blk", 8)
    return call("weight_image_z", along_z, outs[:1], (p0, p4, p12, p8))[0].T, p0


def local(img_feat, txt_feat, img_weight, txt_weight, natural_exponent_multiplier, bias):
    scale = jnp.exp(natural_exponent_multiplier)
    blocks = lax.axis_size("mp")
    column = lax.axis_index("mp").astype(jnp.int32)[None]
    place = lax.axis_index("blk").astype(jnp.int32)[None]
    own = img_feat.shape[0] // blocks
    width = img_weight.shape[1]
    one, two = (own, width), (2, own, width)

    half = (2, own // 2, width)
    own_half = (own // 2, width)

    t01, t23, t67, t4, t5 = embed("embed_text", txt_feat, txt_weight, column, blocks)
    t4, t5 = swap(t4, "mp", 6), swap(t5, "mp", 2)
    i01, i23, i67, i4, i5 = embed("embed_image", img_feat, img_weight, column, blocks)
    t23, t67 = call("relay_text", relay_add, [shape(*two)] * 2, (t23, t67, t4, t5))
    t23, t67 = swap(t23, "mp", 2), swap(t67, "mp", 6)
    i4, i5 = swap(i4, "mp", 6), swap(i5, "mp", 2)

    def second(t01, t23, t67, t0_out, t1_out):
        t0_out[...] = wide(t01, 0) + wide(t23, 0) + wide(t67, 0)
        t1_out[...] = (wide(t01, 1) + wide(t23, 1) + wide(t67, 1)).astype(BF16)

    t0, t1 = call("sums_second", second, [shape(*one, dtype=F32), shape(*one)], (t01, t23, t67))
    t1_got = swap(t1, "mp", 1)
    sent = call("relay_image", relay_split, [shape(*half)] * 4, (i23, i67, i4, i5), after=t1)
    got = [(swap(sent[2 * h], "mp", 2), swap(sent[2 * h + 1], "mp", 6)) for h in range(2)]

    def third(t0, t1, text_out, unit_out):
        embedded = t0[...] + wide(t1)
        text_out[...] = embedded
        unit_out[...] = unit_of(embedded)[0].astype(BF16)

    txt_emb, a0 = call("sums_third", third, [shape(*one, dtype=F32), shape(*one)], (t0, t1_got), after=sent[0])
    a2 = swap(a0, "blk", 2)
    (x_a,) = call("image_x_a", add_half(0), [shape(*half)], (i01, *got[0]), after=a0)
    y_a = swap(x_a, "mp", 1)
    (a02,) = call("stack_text", stack, [shape(*two)], (a0, a2), after=x_a)
    a46, a1214 = swap(a02, "blk", 4), swap(a02, "blk", 12)
    (x_b,) = call("image_x_b", add_half(1), [shape(*half)], (i01, *got[1]), after=a02)
    y_b = swap(x_b, "mp", 1)
    outs = [shape(*half, dtype=F32), shape(*half)]
    emb_a, u01_a = call("image_unit_a", norm_half, outs, (x_a, y_a), after=x_b)
    u23_a, u67_a = swap(u01_a, "mp", 2), swap(u01_a, "mp", 6)
    emb_b, u01_b = call("image_unit_b", norm_half, outs, (x_b, y_b), after=u01_a)
    u23_b, u67_b = swap(u01_b, "mp", 2), swap(u01_b, "mp", 6)
    outs = [shape(*own_half)] * 2
    u2_a, u7_a = call("cut_image_a", cut, outs, (u23_a, u67_a), after=u01_b)
    u4_a, u5_a = swap(u2_a, "mp", 6), swap(u7_a, "mp", 2)
    a4, a14 = call("cut_text", cut, [shape(*one)] * 2, (a46, a1214), after=u2_a)
    a8, a10 = swap(a4, "blk", 12), swap(a14, "blk", 4)
    u2_b, u7_b = call("cut_image_b", cut, outs, (u23_b, u67_b), after=a4)
    u4_b, u5_b = swap(u2_b, "mp", 6), swap(u7_b, "mp", 2)

    def collect(a02, a46, a1214, a8, a10, out):
        for k, ref in enumerate((a02, a46, a1214)):
            out[2 * k : 2 * k + 2] = ref[...]
        out[6] = a8[...]
        out[7] = a10[...]

    (even,) = call("collect", collect, [shape(8, *one)], (a02, a46, a1214, a8, a10), after=(u4_a, u5_a, u4_b, u5_b))
    odd = swap(even, "blk", 1)
    images = (u01_a, u01_b, u23_a, u23_b, u67_a, u67_b, u4_a, u4_b, u5_a, u5_b)
    factor_even, flip_even, image_all = pairs_even(scale, bias, even, images)
    flip_odd, odd_sum = pairs_odd(scale, bias, odd, image_all, flip_even)
    odd_got = swap(odd_sum, "blk", 1)
    flips, texts = (flip_even, flip_odd), (even, odd)
    g4, g5 = pairs_image("pairs_far_images", flips, texts, 6 * own, 8 * own, [shape(*one)] * 2, odd_sum, 256, True)
    g4_got, g5_got = swap(g4, "mp", 6), swap(g5, "mp", 2)
    flops = 128 * own * own * width
    (even_sum,) = call("text_grads_even", text_grads, [shape(8, *one)], (factor_even, image_all), flops, 20, g4)

    def fifth(even, got, p8, p10):
        p8[...] = (wide(even, 6) + wide(got, 6)).astype(BF16)
        p10[...] = (wide(even, 7) + wide(got, 7)).astype(BF16)

    p8, p10 = call("sums_fifth", fifth, [shape(*one)] * 2, (even_sum, odd_got))
    g01, g23, g67 = pairs_image("pairs_near_images", flips, texts, 0, 6 * own, [shape(*two)] * 3, p8, 512, False)
    p8_got, p10_got = swap(p8, "blk", 12), swap(p10, "blk", 4)
    sent = call("relay_image_grads", relay_split, [shape(*half)] * 4, (g23, g67, g4_got, g5_got))
    got = [(swap(sent[2 * h], "mp", 2), swap(sent[2 * h + 1], "mp", 6)) for h in range(2)]

    def sixth(even, got, p8, p10, p02, p46, p1214):
        for k in range(2):
            p02[k] = (wide(even, k) + wide(got, k)).astype(BF16)
        p46[0] = (wide(even, 2) + wide(got, 2) + wide(p8)).astype(BF16)
        p46[1] = (wide(even, 3) + wide(got, 3)).astype(BF16)
        p1214[0] = (wide(even, 4) + wide(got, 4)).astype(BF16)
        p1214[1] = (wide(even, 5) + wide(got, 5) + wide(p10)).astype(BF16)

    outs = [shape(*two)] * 3
    p02, p46, p1214 = call("sums_sixth", sixth, outs, (even_sum, odd_got, p8_got, p10_got), after=sent[0])
    p46, p1214 = swap(p46, "blk", 4), swap(p1214, "blk", 12)
    (x_a,) = call("image_grads_x_a", add_half(0), [shape(*half)], (g01, *got[0]), ORDER_COST // 2, after=p02)
    y_a = swap(x_a, "mp", 1)
    (x_b,) = call("image_grads_x_b", add_half(1), [shape(*half)], (g01, *got[1]), after=x_a)
    y_b = swap(x_b, "mp", 1)
    def seventh(p02, p46, p1214, p0_out, p2_out):
        p0_out[...] = wide(p02, 0) + wide(p46, 0) + wide(p1214, 0)
        p2_out[...] = (wide(p02, 1) + wide(p46, 1) + wide(p1214, 1)).astype(BF16)

    outs = [shape(*one, dtype=F32), shape(*one)]
    p0, p2 = call("sums_seventh", seventh, outs, (p02, p46, p1214), after=x_b)
    p2_got = swap(p2, "blk", 2)
    (e01_a,) = call("image_back_a", back_half, [shape(*half)], (x_a, y_a, emb_a), after=p2)
    e23_a, e67_a, e45_a = swap(e01_a, "mp", 2), swap(e01_a, "mp", 6), swap(e01_a, "mp", 4)

    def text_back(p0, p2, txt_emb, out):
        out[...] = norm_back(p0[...] + wide(p2), txt_emb[...]).astype(BF16)

    (d0,) = call("text_back", text_back, [shape(*one)], (p0, p2_got, txt_emb), after=e01_a)
    d1 = swap(d0, "mp", 1)
    (e01_b,) = call("image_back_b", back_half, [shape(*half)], (x_b, y_b, emb_b), after=d0)
    e23_b, e67_b, e45_b = swap(e01_b, "mp", 2), swap(e01_b, "mp", 6), swap(e01_b, "mp", 4)

    (d01,) = call("stack_text_grads", stack, [shape(*two)], (d0, d1), after=(e01_b, e23_a, e67_a, e45_a))
    d23, d67 = swap(d01, "mp", 2), swap(d01, "mp", 6)

    e_all = (e01_a, e01_b, e23_a, e23_b, e67_a, e67_b, e45_a, e45_b)
    same, other = weight_part("weight_image", column, place, e_all, 2, img_feat, d01)
    img_feat_grad, image_done = feature_grad("feature_image", column, e_all, 2, img_weight)
    d2, d7 = call("cut_text_grads", cut, [shape(*one)] * 2, (d23, d67), ORDER_COST, after=(same, image_done))
    d4, d5 = swap(d2, "mp", 6), swap(d7, "mp", 2)
    image_chip = chip_weight_y("weight_image_chip", same, other)
    img_weight_grad, image_y = sum_weight_y(*image_chip)
    d_all = (d01, d23, d67, d4, d5)
    same, other = weight_part("weight_text", column, place, d_all, 1, txt_feat, image_chip[0])
    txt_weight_grad = sum_weight(*chip_weight("weight_text_chip", same, other))
    txt_feat_grad, _ = feature_grad("feature_text", column, d_all, 1, txt_weight)
    return (img_feat_grad, txt_feat_grad, img_weight_grad, txt_weight_grad)


def solution(mesh):
    return jax.shard_map(
        local,
        mesh=mesh,
        in_specs=(P("blk", "mp"), P("blk", "mp"), P("mp", None), P("mp", None), P(), P()),
        out_specs=(P("blk", "mp"), P("blk", "mp"), P("mp", "blk"), P("mp", "blk")),
        check_vma=False,
    )
```

```python
import jax
import jax.numpy as jnp
from jax import lax
from jax.experimental import pallas as pl
from jax.experimental.pallas import tpu as pltpu
from jax.sharding import PartitionSpec as P

EPS = 1e-06
BF16 = jnp.bfloat16
F32 = jnp.float32
MIB = 1024 * 1024
ORDER_COST = 10 * 10**9
NEAR_FAR = (0, 1, 2, 3, 6, 7, 4, 5)


def swap(value, axis, offset):
    count = lax.axis_size(axis)
    return lax.ppermute(value, axis, [(i, i ^ offset) for i in range(count)])


def shape(*dims, dtype=BF16):
    return jax.ShapeDtypeStruct(dims, dtype)


def call(name, body, outs, ins, flops=0, limit=10, after=None, in_specs=None, scratch=()):
    ins, specs = list(ins), in_specs or [pl.BlockSpec(memory_space=pltpu.VMEM)] * len(ins)
    run = body
    if after is not None:
        after = list(after) if isinstance(after, tuple) else [after]
        ins, specs = after + ins, [pl.BlockSpec(memory_space=pltpu.VMEM)] * len(after) + list(specs)

        def run(*refs):
            body(*refs[len(after) :])

    moved = sum(a.size * a.dtype.itemsize for a in ins + list(outs))
    return pl.pallas_call(
        run,
        out_shape=outs,
        in_specs=specs,
        scratch_shapes=list(scratch),
        compiler_params=pltpu.CompilerParams(vmem_limit_bytes=limit * MIB),
        cost_estimate=pl.CostEstimate(flops=flops, bytes_accessed=moved, transcendentals=0),
        name=name,
    )(*ins)


def tiles(count, size, body, unroll=False):
    if unroll:
        for index in range(count):
            body(slice(index * size, (index + 1) * size))
        return

    def step(index, carry):
        body(pl.ds(pl.multiple_of(index * size, size), size))
        return carry

    lax.fori_loop(0, count, step, 0)


def wide(ref, block=None):
    return (ref[...] if block is None else ref[block]).astype(F32)


def embed(name, feat, weight, column, blocks, tile=256):
    rows, width = feat.shape
    columns = weight.shape[1]
    own = rows // blocks

    def body(column_ref, feat_ref, weight_ref, p01, p23, p67, p4, p5, result):
        def part(k):
            return result[pl.ds(pl.multiple_of((column_ref[0] ^ k) * own, own), own)]

        def columns_at(here):
            result[...] = product(feat_ref[...], weight_ref[:, here]).astype(BF16)
            for k in range(2):
                p01[k, :, here] = part(k)
                p23[k, :, here] = part(2 + k)
                p67[k, :, here] = part(6 + k)
            p4[:, here] = part(4)
            p5[:, here] = part(5)

        tiles(columns // tile, tile, columns_at)

    outs = [shape(2, own, columns)] * 3 + [shape(own, columns)] * 2
    specs = [pl.BlockSpec(memory_space=pltpu.SMEM)] + [pl.BlockSpec(memory_space=pltpu.VMEM)] * 2
    scratch = [pltpu.VMEM((rows, tile), BF16)]
    return call(name, body, outs, (column, feat, weight), 2 * rows * width * columns, 16, None, specs, scratch)


def relay_add(p23, p67, r4, r5, out23, out67):
    out23[0] = (wide(p23, 0) + wide(r4)).astype(BF16)
    out23[1] = p23[1]
    out67[0] = p67[0]
    out67[1] = (wide(p67, 1) + wide(r5)).astype(BF16)


def relay_split(p23, p67, r4, r5, a23, a67, b23, b67):
    half = r4.shape[0] // 2
    for h, (out23, out67) in enumerate(((a23, a67), (b23, b67))):
        rows = slice(h * half, (h + 1) * half)
        out23[0] = (p23[0, rows].astype(F32) + wide(r4, rows)).astype(BF16)
        out23[1] = p23[1, rows]
        out67[0] = p67[0, rows]
        out67[1] = (p67[1, rows].astype(F32) + wide(r5, rows)).astype(BF16)


def add_half(h):
    def body(p01, r23, r67, out):
        half = out.shape[1]
        for k in range(2):
            own = p01[k, h * half : (h + 1) * half].astype(F32)
            out[k] = (own + wide(r23, k) + wide(r67, k)).astype(BF16)

    return body


def norm_half(p01, got01, emb_out, unit_out):
    for k in range(2):
        embedded = wide(p01, k) + wide(got01, 1 - k)
        emb_out[k] = embedded
        unit_out[k] = unit_of(embedded)[0].astype(BF16)


def back_half(g01, got01, emb, out):
    for k in range(2):
        out[k] = norm_back(wide(g01, k) + wide(got01, 1 - k), emb[k]).astype(BF16)


def cut(near, other, first_out, last_out):
    first_out[...] = near[0]
    last_out[...] = other[1]


def stack(first, second, out):
    out[0] = first[...]
    out[1] = second[...]


def grouped(refs, halves):
    return [refs[i : i + halves] for i in range(0, len(refs), halves)]


def block(group, k=None):
    parts = [ref[...] if k is None else ref[k] for ref in group]
    return parts[0] if len(parts) == 1 else jnp.concatenate(parts, axis=0)


def near_far_order(groups):
    pairs = [block(g, k) for g in groups[:3] for k in range(2)]
    if len(groups) == 4:
        return pairs + [block(groups[3], k) for k in range(2)]
    return pairs + [block(g) for g in groups[3:]]


def unit_of(embedded):
    inverse = lax.rsqrt(jnp.sum(embedded * embedded, axis=1, keepdims=True) + EPS)
    return embedded * inverse, inverse


def norm_back(unit_grad, embedded):
    unit, inverse = unit_of(embedded)
    return inverse * (unit_grad - unit * jnp.sum(unit * unit_grad, axis=1, keepdims=True))


def flat(ref):
    return ref[...].reshape(-1, ref.shape[-1])


def factors(scale, bias, txt, img):
    affinity = lax.dot_general(txt, img, (((1,), (1,)), ((), ())), preferred_element_type=F32)
    logits = scale * affinity + bias
    return logits, (scale / (1.0 + jnp.exp(-logits))).astype(BF16)


def product(first, second):
    return jnp.dot(first, second, preferred_element_type=F32)


def pair_call(name, body, outs, scale, bias, arrays, flops, limit, scratch=()):
    smem = pl.BlockSpec(memory_space=pltpu.SMEM)
    vmem = pl.BlockSpec(memory_space=pltpu.VMEM)
    moved = sum(a.size * a.dtype.itemsize for a in list(arrays) + outs)
    return pl.pallas_call(
        body,
        in_specs=[smem, smem] + [vmem] * len(arrays),
        out_shape=outs,
        scratch_shapes=list(scratch),
        compiler_params=pltpu.CompilerParams(vmem_limit_bytes=limit * MIB),
        cost_estimate=pl.CostEstimate(flops=flops, bytes_accessed=moved, transcendentals=0),
        name=name,
    )(scale, bias, *arrays)


def image_rows(image_refs, image_all):
    own = image_all.shape[0] // 8
    for k, part in enumerate(near_far_order(grouped(image_refs, 2))):
        image_all[k * own : (k + 1) * own] = part


def factor_rows(scale, bias, texts, image_all, factor_all, flipped, tile, unroll):
    def images_at(here):
        factor = factors(scale, bias, flat(texts), image_all[here])[1]
        factor_all[:, here] = factor
        flipped[here] = factor.T

    tiles(image_all.shape[0] // tile, tile, images_at, unroll)


def match(scale, bias, texts, image_all, factor_all, flipped):
    own = texts.shape[1]
    logits = factors(scale, bias, texts[0], image_all[:own])[0]
    row = lax.broadcasted_iota(jnp.int32, logits.shape, 0)
    column = lax.broadcasted_iota(jnp.int32, logits.shape, 1)
    pull = (-scale / (1.0 + jnp.exp(logits))).astype(BF16)
    factor = jnp.where(row == column, pull, factor_all[:own, :own])
    factor_all[:own, :own] = factor
    flipped[:own, :own] = factor.T


def text_grads(factor_all, image_all, out, tile=512, unroll=False):
    def columns_at(here):
        grads = product(factor_all[...], image_all[:, here]).astype(BF16)
        out[:, :, here] = grads.reshape(*out.shape[:2], tile)

    tiles(out.shape[-1] // tile, tile, columns_at, unroll)


def pairs_even(scale, bias, texts, images):
    count, own, width = texts.shape
    rows = count * own

    def body(scale_ref, bias_ref, texts, *refs):
        image_refs, (factor_all, flipped, image_all) = refs[:10], refs[10:]
        image_rows(image_refs, image_all)
        scale, bias = scale_ref[0], bias_ref[0]
        factor_rows(scale, bias, texts, image_all, factor_all, flipped, 512, False)
        match(scale, bias, texts, image_all, factor_all, flipped)

    outs = [shape(rows, rows), shape(rows, rows), shape(rows, width)]
    return pair_call("pairs_even", body, outs, scale, bias, (texts, *images), 2 * rows * rows * width, 24)


def pairs_odd(scale, bias, texts, image_all, after):
    count, own, width = texts.shape
    rows = count * own

    def body(scale_ref, bias_ref, texts, image_all, _, flipped, out, factor_all):
        factor_rows(scale_ref[0], bias_ref[0], texts, image_all, factor_all, flipped, 256, True)
        text_grads(factor_all, image_all, out, 256, True)

    outs = [shape(rows, rows), shape(count, own, width)]
    scratch = [pltpu.VMEM((rows, rows), BF16)]
    arrays = (texts, image_all, after)
    return pair_call("pairs_odd", body, outs, scale, bias, arrays, 4 * rows * rows * width, 24, scratch)


def pairs_image(name, flips, texts, start, stop, outs, after, tile, unroll):
    own, width = texts[0].shape[-2:]

    def body(flip_even, flip_odd, even, odd, *out_refs):
        def columns_at(here):
            factor = jnp.concatenate([flip_even[start:stop], flip_odd[start:stop]], axis=1)
            rows = jnp.concatenate([ref[:, :, here].reshape(-1, tile) for ref in (even, odd)], axis=0)
            total = product(factor, rows).astype(BF16)
            place = 0
            for ref in out_refs:
                size = ref.size // width
                ref[..., here] = total[place : place + size].reshape(*ref.shape[:-1], tile)
                place += size

        tiles(width // tile, tile, columns_at, unroll)

    flops = 2 * (stop - start) * 16 * own * width
    return call(name, body, outs, (*flips, *texts), flops, 24, after)


def weight_part(name, column, place, pieces, halves, feat, after, more=0):
    count, width = len(pieces), pieces[-1].shape[-1]
    rows, features = feat.shape
    own = rows // 8
    strip = width // 16
    tile = 256

    def body(column_ref, place_ref, *refs):
        feat_ref, same, other, flipped, moved, result = refs[count:]
        for n, part in enumerate(near_far_order(grouped(refs[:count], halves))):
            k = NEAR_FAR[n]
            flipped[:, k * own : (k + 1) * own] = part.T
        def features_at(here):
            for k in range(rows // own):
                start = pl.multiple_of((column_ref[0] ^ k) * own, own)
                moved[k * own : (k + 1) * own] = feat_ref[pl.ds(start, own), here]
            result[...] = product(flipped[...], moved[...]).astype(BF16)
            for j, k in enumerate((0, 2, 4, 6, 12, 14, 8, 10)):
                mine = pl.multiple_of((place_ref[0] ^ k) * strip, strip)
                theirs = pl.multiple_of((place_ref[0] ^ (k + 1)) * strip, strip)
                same[j, :, here] = result[pl.ds(mine, strip)]
                other[j, :, here] = result[pl.ds(theirs, strip)]

        tiles(features // tile, tile, features_at, True)

    smem, vmem = pl.BlockSpec(memory_space=pltpu.SMEM), pl.BlockSpec(memory_space=pltpu.VMEM)
    specs = [smem, smem] + [vmem] * (len(pieces) + 1)
    scratch = [
        pltpu.VMEM((width, rows), BF16),
        pltpu.VMEM((rows, tile), BF16),
        pltpu.VMEM((width, tile), BF16),
    ]
    outs = [shape(8, strip, features)] * 2
    flops = 2 * rows * width * features + more
    return call(name, body, outs, (column, place, *pieces, feat), flops, 16, after, specs, scratch)


def feature_grad(name, column, pieces, halves, weight):
    count, width = len(pieces), pieces[-1].shape[-1]
    features = weight.shape[0]
    own = pieces[0].shape[1] * halves
    rows = 8 * own
    tile = 256

    def body(column_ref, *refs):
        weight_ref, out = refs[count:]
        def features_at(here):
            egrad = jnp.concatenate(near_far_order(grouped(refs[:count], halves)), axis=0)
            result = lax.dot_general(
                egrad, weight_ref[here], (((1,), (1,)), ((), ())), preferred_element_type=F32
            ).astype(BF16)
            for n, k in enumerate(NEAR_FAR):
                start = pl.multiple_of((column_ref[0] ^ k) * own, own)
                out[pl.ds(start, own), here] = result[n * own : (n + 1) * own]

        tiles(features // tile, tile, features_at)

    smem, vmem = pl.BlockSpec(memory_space=pltpu.SMEM), pl.BlockSpec(memory_space=pltpu.VMEM)
    outs, ins = [shape(rows, features)], (column, *pieces, weight)
    return call(name, body, outs, ins, 2 * rows * width * features, 16, None, [smem] + [vmem] * (len(pieces) + 1))[0]


def chip_weight(name, same, other, after=None):
    strip, features = same.shape[1:]

    def body(same, got, *outs):
        for j, out in enumerate(outs):
            out[...] = (wide(same, slice(2 * j, 2 * j + 2)) + wide(got, slice(2 * j, 2 * j + 2))).astype(BF16)

    outs = [shape(2, strip, features)] * 4
    return call(name, body, outs, (same, swap(other, "blk", 1)), after=after)


def sum_weight(p02, p46, p1214, p810):
    strip, features = p02.shape[1:]

    def along_z(p02, p46, p1214, p810, p0_out, p2_out):
        total = wide(p02) + wide(p46) + wide(p1214) + wide(p810)
        p0_out[...] = total[0]
        p2_out[...] = total[1].astype(BF16)

    def along_y(p0, p2, out):
        out[...] = p0[...] + wide(p2)

    p46, p1214, p810 = swap(p46, "blk", 4), swap(p1214, "blk", 12), swap(p810, "blk", 8)
    outs = [shape(strip, features, dtype=F32), shape(strip, features)]
    p0, p2 = call("weight_z", along_z, outs, (p02, p46, p1214, p810))
    p2 = swap(p2, "blk", 2)
    return call("weight_y", along_y, outs[:1], (p0, p2))[0].T


def chip_weight_y(name, same, other, after=None):
    strip, features = same.shape[1:]

    def body(same, got, mine, theirs):
        for j in range(4):
            for k, out in enumerate((mine, theirs)):
                out[j] = (wide(same, 2 * j + k) + wide(got, 2 * j + k)).astype(BF16)

    outs = [shape(4, strip, features)] * 2
    return call(name, body, outs, (same, swap(other, "blk", 1)), after=after)


def sum_weight_y(mine, theirs):
    strip, features = mine.shape[1:]
    one = (strip, features)

    def along_y(mine, got, p0, p4, p12, p8):
        p0[...] = wide(mine, 0) + wide(got, 0)
        for j, out in ((1, p4), (2, p12), (3, p8)):
            out[...] = (wide(mine, j) + wide(got, j)).astype(BF16)

    def along_z(p0, p4, p12, p8, out):
        out[...] = p0[...] + wide(p4) + wide(p12) + wide(p8)

    outs = [shape(*one, dtype=F32)] + [shape(*one)] * 3
    p0, p4, p12, p8 = call("weight_image_y", along_y, outs, (mine, swap(theirs, "blk", 2)))
    p4, p12, p8 = swap(p4, "blk", 4), swap(p12, "blk", 12), swap(p8, "blk", 8)
    return call("weight_image_z", along_z, outs[:1], (p0, p4, p12, p8))[0].T, p0


def local(img_feat, txt_feat, img_weight, txt_weight, natural_exponent_multiplier, bias):
    scale = jnp.exp(natural_exponent_multiplier)
    blocks = lax.axis_size("mp")
    column = lax.axis_index("mp").astype(jnp.int32)[None]
    place = lax.axis_index("blk").astype(jnp.int32)[None]
    own = img_feat.shape[0] // blocks
    width = img_weight.shape[1]
    one, two = (own, width), (2, own, width)

    half = (2, own // 2, width)
    own_half = (own // 2, width)

    t01, t23, t67, t4, t5 = embed("embed_text", txt_feat, txt_weight, column, blocks)
    t4, t5 = swap(t4, "mp", 6), swap(t5, "mp", 2)
    i01, i23, i67, i4, i5 = embed("embed_image", img_feat, img_weight, column, blocks)
    t23, t67 = call("relay_text", relay_add, [shape(*two)] * 2, (t23, t67, t4, t5))
    t23, t67 = swap(t23, "mp", 2), swap(t67, "mp", 6)
    i4, i5 = swap(i4, "mp", 6), swap(i5, "mp", 2)

    def second(t01, t23, t67, t0_out, t1_out):
        t0_out[...] = wide(t01, 0) + wide(t23, 0) + wide(t67, 0)
        t1_out[...] = (wide(t01, 1) + wide(t23, 1) + wide(t67, 1)).astype(BF16)

    t0, t1 = call("sums_second", second, [shape(*one, dtype=F32), shape(*one)], (t01, t23, t67))
    t1_got = swap(t1, "mp", 1)
    sent = call("relay_image", relay_split, [shape(*half)] * 4, (i23, i67, i4, i5), after=t1)
    got = [(swap(sent[2 * h], "mp", 2), swap(sent[2 * h + 1], "mp", 6)) for h in range(2)]

    def third(t0, t1, text_out, unit_out):
        embedded = t0[...] + wide(t1)
        text_out[...] = embedded
        unit_out[...] = unit_of(embedded)[0].astype(BF16)

    txt_emb, a0 = call("sums_third", third, [shape(*one, dtype=F32), shape(*one)], (t0, t1_got), after=sent[0])
    a2 = swap(a0, "blk", 2)
    (x_a,) = call("image_x_a", add_half(0), [shape(*half)], (i01, *got[0]), after=a0)
    y_a = swap(x_a, "mp", 1)
    (a02,) = call("stack_text", stack, [shape(*two)], (a0, a2), after=x_a)
    a46, a1214 = swap(a02, "blk", 4), swap(a02, "blk", 12)
    (x_b,) = call("image_x_b", add_half(1), [shape(*half)], (i01, *got[1]), after=a02)
    y_b = swap(x_b, "mp", 1)
    outs = [shape(*half, dtype=F32), shape(*half)]
    emb_a, u01_a = call("image_unit_a", norm_half, outs, (x_a, y_a), after=x_b)
    u23_a, u67_a = swap(u01_a, "mp", 2), swap(u01_a, "mp", 6)
    emb_b, u01_b = call("image_unit_b", norm_half, outs, (x_b, y_b), after=u01_a)
    u23_b, u67_b = swap(u01_b, "mp", 2), swap(u01_b, "mp", 6)
    outs = [shape(*own_half)] * 2
    u2_a, u7_a = call("cut_image_a", cut, outs, (u23_a, u67_a), after=u01_b)
    u4_a, u5_a = swap(u2_a, "mp", 6), swap(u7_a, "mp", 2)
    a4, a14 = call("cut_text", cut, [shape(*one)] * 2, (a46, a1214), after=u2_a)
    a8, a10 = swap(a4, "blk", 12), swap(a14, "blk", 4)
    u2_b, u7_b = call("cut_image_b", cut, outs, (u23_b, u67_b), after=a4)
    u4_b, u5_b = swap(u2_b, "mp", 6), swap(u7_b, "mp", 2)

    def collect(a02, a46, a1214, a8, a10, out):
        for k, ref in enumerate((a02, a46, a1214)):
            out[2 * k : 2 * k + 2] = ref[...]
        out[6] = a8[...]
        out[7] = a10[...]

    (even,) = call("collect", collect, [shape(8, *one)], (a02, a46, a1214, a8, a10), after=(u4_a, u5_a, u4_b, u5_b))
    odd = swap(even, "blk", 1)
    images = (u01_a, u01_b, u23_a, u23_b, u67_a, u67_b, u4_a, u4_b, u5_a, u5_b)
    factor_even, flip_even, image_all = pairs_even(scale, bias, even, images)
    flip_odd, odd_sum = pairs_odd(scale, bias, odd, image_all, flip_even)
    odd_got = swap(odd_sum, "blk", 1)
    flips, texts = (flip_even, flip_odd), (even, odd)
    g4, g5 = pairs_image("pairs_far_images", flips, texts, 6 * own, 8 * own, [shape(*one)] * 2, odd_sum, 256, True)
    g4_got, g5_got = swap(g4, "mp", 6), swap(g5, "mp", 2)
    flops = 128 * own * own * width
    (even_sum,) = call("text_grads_even", text_grads, [shape(8, *one)], (factor_even, image_all), flops, 20, g4)

    def fifth(even, got, p8, p10):
        p8[...] = (wide(even, 6) + wide(got, 6)).astype(BF16)
        p10[...] = (wide(even, 7) + wide(got, 7)).astype(BF16)

    p8, p10 = call("sums_fifth", fifth, [shape(*one)] * 2, (even_sum, odd_got))
    g01, g23, g67 = pairs_image("pairs_near_images", flips, texts, 0, 6 * own, [shape(*two)] * 3, p8, 512, False)
    p8_got, p10_got = swap(p8, "blk", 12), swap(p10, "blk", 4)
    sent = call("relay_image_grads", relay_split, [shape(*half)] * 4, (g23, g67, g4_got, g5_got))
    got = [(swap(sent[2 * h], "mp", 2), swap(sent[2 * h + 1], "mp", 6)) for h in range(2)]

    def sixth(even, got, p8, p10, p02, p46, p1214):
        for k in range(2):
            p02[k] = (wide(even, k) + wide(got, k)).astype(BF16)
        p46[0] = (wide(even, 2) + wide(got, 2) + wide(p8)).astype(BF16)
        p46[1] = (wide(even, 3) + wide(got, 3)).astype(BF16)
        p1214[0] = (wide(even, 4) + wide(got, 4)).astype(BF16)
        p1214[1] = (wide(even, 5) + wide(got, 5) + wide(p10)).astype(BF16)

    outs = [shape(*two)] * 3
    p02, p46, p1214 = call("sums_sixth", sixth, outs, (even_sum, odd_got, p8_got, p10_got), after=sent[0])
    p46, p1214 = swap(p46, "blk", 4), swap(p1214, "blk", 12)
    (x_a,) = call("image_grads_x_a", add_half(0), [shape(*half)], (g01, *got[0]), ORDER_COST // 2, after=p02)
    y_a = swap(x_a, "mp", 1)
    (x_b,) = call("image_grads_x_b", add_half(1), [shape(*half)], (g01, *got[1]), after=x_a)
    y_b = swap(x_b, "mp", 1)
    def seventh(p02, p46, p1214, p0_out, p2_out):
        p0_out[...] = wide(p02, 0) + wide(p46, 0) + wide(p1214, 0)
        p2_out[...] = (wide(p02, 1) + wide(p46, 1) + wide(p1214, 1)).astype(BF16)

    outs = [shape(*one, dtype=F32), shape(*one)]
    p0, p2 = call("sums_seventh", seventh, outs, (p02, p46, p1214), after=x_b)
    p2_got = swap(p2, "blk", 2)
    (e01_a,) = call("image_back_a", back_half, [shape(*half)], (x_a, y_a, emb_a), after=p2)
    e23_a, e67_a, e45_a = swap(e01_a, "mp", 2), swap(e01_a, "mp", 6), swap(e01_a, "mp", 4)

    def text_back(p0, p2, txt_emb, out):
        out[...] = norm_back(p0[...] + wide(p2), txt_emb[...]).astype(BF16)

    (d0,) = call("text_back", text_back, [shape(*one)], (p0, p2_got, txt_emb), after=e01_a)
    d1 = swap(d0, "mp", 1)
    (e01_b,) = call("image_back_b", back_half, [shape(*half)], (x_b, y_b, emb_b), after=d0)
    e23_b, e67_b, e45_b = swap(e01_b, "mp", 2), swap(e01_b, "mp", 6), swap(e01_b, "mp", 4)

    (d01,) = call("stack_text_grads", stack, [shape(*two)], (d0, d1), after=(e01_b, e23_a, e67_a, e45_a))
    d23, d67 = swap(d01, "mp", 2), swap(d01, "mp", 6)

    e_all = (e01_a, e01_b, e23_a, e23_b, e67_a, e67_b, e45_a, e45_b)
    same, other = weight_part("weight_image", column, place, e_all, 2, img_feat, d01, ORDER_COST // 4)
    d2, d7 = call("cut_text_grads", cut, [shape(*one)] * 2, (d23, d67), ORDER_COST, after=same)
    d4, d5 = swap(d2, "mp", 6), swap(d7, "mp", 2)
    image_chip = chip_weight_y("weight_image_chip", same, other)
    img_weight_grad, image_y = sum_weight_y(*image_chip)
    d_all = (d01, d23, d67, d4, d5)
    same, other = weight_part("weight_text", column, place, d_all, 1, txt_feat, image_chip[0])
    txt_weight_grad = sum_weight(*chip_weight("weight_text_chip", same, other))
    return (
        feature_grad("feature_image", column, e_all, 2, img_weight),
        feature_grad("feature_text", column, d_all, 1, txt_weight),
        img_weight_grad,
        txt_weight_grad,
    )


def solution(mesh):
    return jax.shard_map(
        local,
        mesh=mesh,
        in_specs=(P("blk", "mp"), P("blk", "mp"), P("mp", None), P("mp", None), P(), P()),
        out_specs=(P("blk", "mp"), P("blk", "mp"), P("mp", "blk"), P("mp", "blk")),
        check_vma=False,
    )
```

```python
import jax
import jax.numpy as jnp
from jax import lax
from jax.experimental import pallas as pl
from jax.experimental.pallas import tpu as pltpu
from jax.sharding import PartitionSpec as P

EPS = 1e-06
BF16 = jnp.bfloat16
F32 = jnp.float32
MIB = 1024 * 1024
ORDER_COST = 10 * 10**9
NEAR_FAR = (0, 1, 2, 3, 6, 7, 4, 5)


def swap(value, axis, offset):
    count = lax.axis_size(axis)
    return lax.ppermute(value, axis, [(i, i ^ offset) for i in range(count)])


def shape(*dims, dtype=BF16):
    return jax.ShapeDtypeStruct(dims, dtype)


def call(name, body, outs, ins, flops=0, limit=10, after=None, in_specs=None, scratch=()):
    ins, specs = list(ins), in_specs or [pl.BlockSpec(memory_space=pltpu.VMEM)] * len(ins)
    run = body
    if after is not None:
        after = list(after) if isinstance(after, tuple) else [after]
        ins, specs = after + ins, [pl.BlockSpec(memory_space=pltpu.VMEM)] * len(after) + list(specs)

        def run(*refs):
            body(*refs[len(after) :])

    moved = sum(a.size * a.dtype.itemsize for a in ins + list(outs))
    return pl.pallas_call(
        run,
        out_shape=outs,
        in_specs=specs,
        scratch_shapes=list(scratch),
        compiler_params=pltpu.CompilerParams(vmem_limit_bytes=limit * MIB),
        cost_estimate=pl.CostEstimate(flops=flops, bytes_accessed=moved, transcendentals=0),
        name=name,
    )(*ins)


def tiles(count, size, body, unroll=False):
    if unroll:
        for index in range(count):
            body(slice(index * size, (index + 1) * size))
        return

    def step(index, carry):
        body(pl.ds(pl.multiple_of(index * size, size), size))
        return carry

    lax.fori_loop(0, count, step, 0)


def wide(ref, block=None):
    return (ref[...] if block is None else ref[block]).astype(F32)


def embed(name, feat, weight, column, blocks, tile=256):
    rows, width = feat.shape
    columns = weight.shape[1]
    own = rows // blocks

    def body(column_ref, feat_ref, weight_ref, p01, p23, p67, p4, p5, result):
        def part(k):
            return result[pl.ds(pl.multiple_of((column_ref[0] ^ k) * own, own), own)]

        def columns_at(here):
            result[...] = product(feat_ref[...], weight_ref[:, here]).astype(BF16)
            for k in range(2):
                p01[k, :, here] = part(k)
                p23[k, :, here] = part(2 + k)
                p67[k, :, here] = part(6 + k)
            p4[:, here] = part(4)
            p5[:, here] = part(5)

        tiles(columns // tile, tile, columns_at)

    outs = [shape(2, own, columns)] * 3 + [shape(own, columns)] * 2
    specs = [pl.BlockSpec(memory_space=pltpu.SMEM)] + [pl.BlockSpec(memory_space=pltpu.VMEM)] * 2
    scratch = [pltpu.VMEM((rows, tile), BF16)]
    return call(name, body, outs, (column, feat, weight), 2 * rows * width * columns, 16, None, specs, scratch)


def relay_add(p23, p67, r4, r5, out23, out67):
    out23[0] = (wide(p23, 0) + wide(r4)).astype(BF16)
    out23[1] = p23[1]
    out67[0] = p67[0]
    out67[1] = (wide(p67, 1) + wide(r5)).astype(BF16)


def relay_split(p23, p67, r4, r5, a23, a67, b23, b67):
    half = r4.shape[0] // 2
    for h, (out23, out67) in enumerate(((a23, a67), (b23, b67))):
        rows = slice(h * half, (h + 1) * half)
        out23[0] = (p23[0, rows].astype(F32) + wide(r4, rows)).astype(BF16)
        out23[1] = p23[1, rows]
        out67[0] = p67[0, rows]
        out67[1] = (p67[1, rows].astype(F32) + wide(r5, rows)).astype(BF16)


def add_half(h):
    def body(p01, r23, r67, out):
        half = out.shape[1]
        for k in range(2):
            own = p01[k, h * half : (h + 1) * half].astype(F32)
            out[k] = (own + wide(r23, k) + wide(r67, k)).astype(BF16)

    return body


def norm_half(p01, got01, emb_out, unit_out):
    for k in range(2):
        embedded = wide(p01, k) + wide(got01, 1 - k)
        emb_out[k] = embedded
        unit_out[k] = unit_of(embedded)[0].astype(BF16)


def back_half(g01, got01, emb, out):
    for k in range(2):
        out[k] = norm_back(wide(g01, k) + wide(got01, 1 - k), emb[k]).astype(BF16)


def cut(near, other, first_out, last_out):
    first_out[...] = near[0]
    last_out[...] = other[1]


def stack(first, second, out):
    out[0] = first[...]
    out[1] = second[...]


def grouped(refs, halves):
    return [refs[i : i + halves] for i in range(0, len(refs), halves)]


def block(group, k=None):
    parts = [ref[...] if k is None else ref[k] for ref in group]
    return parts[0] if len(parts) == 1 else jnp.concatenate(parts, axis=0)


def near_far_order(groups):
    pairs = [block(g, k) for g in groups[:3] for k in range(2)]
    if len(groups) == 4:
        return pairs + [block(groups[3], k) for k in range(2)]
    return pairs + [block(g) for g in groups[3:]]


def unit_of(embedded):
    inverse = lax.rsqrt(jnp.sum(embedded * embedded, axis=1, keepdims=True) + EPS)
    return embedded * inverse, inverse


def norm_back(unit_grad, embedded):
    unit, inverse = unit_of(embedded)
    return inverse * (unit_grad - unit * jnp.sum(unit * unit_grad, axis=1, keepdims=True))


def flat(ref):
    return ref[...].reshape(-1, ref.shape[-1])


def factors(scale, bias, txt, img):
    affinity = lax.dot_general(txt, img, (((1,), (1,)), ((), ())), preferred_element_type=F32)
    logits = scale * affinity + bias
    return logits, (scale / (1.0 + jnp.exp(-logits))).astype(BF16)


def product(first, second):
    return jnp.dot(first, second, preferred_element_type=F32)


def pair_call(name, body, outs, scale, bias, arrays, flops, limit, scratch=()):
    smem = pl.BlockSpec(memory_space=pltpu.SMEM)
    vmem = pl.BlockSpec(memory_space=pltpu.VMEM)
    moved = sum(a.size * a.dtype.itemsize for a in list(arrays) + outs)
    return pl.pallas_call(
        body,
        in_specs=[smem, smem] + [vmem] * len(arrays),
        out_shape=outs,
        scratch_shapes=list(scratch),
        compiler_params=pltpu.CompilerParams(vmem_limit_bytes=limit * MIB),
        cost_estimate=pl.CostEstimate(flops=flops, bytes_accessed=moved, transcendentals=0),
        name=name,
    )(scale, bias, *arrays)


def image_rows(image_refs, image_all):
    own = image_all.shape[0] // 8
    for k, part in enumerate(near_far_order(grouped(image_refs, 2))):
        image_all[k * own : (k + 1) * own] = part


def factor_rows(scale, bias, texts, image_all, factor_all, flipped, tile, unroll):
    def images_at(here):
        factor = factors(scale, bias, flat(texts), image_all[here])[1]
        factor_all[:, here] = factor
        flipped[here] = factor.T

    tiles(image_all.shape[0] // tile, tile, images_at, unroll)


def match(scale, bias, texts, image_all, factor_all, flipped):
    own = texts.shape[1]
    logits = factors(scale, bias, texts[0], image_all[:own])[0]
    row = lax.broadcasted_iota(jnp.int32, logits.shape, 0)
    column = lax.broadcasted_iota(jnp.int32, logits.shape, 1)
    pull = (-scale / (1.0 + jnp.exp(logits))).astype(BF16)
    factor = jnp.where(row == column, pull, factor_all[:own, :own])
    factor_all[:own, :own] = factor
    flipped[:own, :own] = factor.T


def text_grads(factor_all, image_all, out, tile=512, unroll=False):
    def columns_at(here):
        grads = product(factor_all[...], image_all[:, here]).astype(BF16)
        out[:, :, here] = grads.reshape(*out.shape[:2], tile)

    tiles(out.shape[-1] // tile, tile, columns_at, unroll)


def pairs_even(scale, bias, texts, images):
    count, own, width = texts.shape
    rows = count * own

    def body(scale_ref, bias_ref, texts, *refs):
        image_refs, (factor_all, flipped, image_all) = refs[:10], refs[10:]
        image_rows(image_refs, image_all)
        scale, bias = scale_ref[0], bias_ref[0]
        factor_rows(scale, bias, texts, image_all, factor_all, flipped, 512, False)
        match(scale, bias, texts, image_all, factor_all, flipped)

    outs = [shape(rows, rows), shape(rows, rows), shape(rows, width)]
    return pair_call("pairs_even", body, outs, scale, bias, (texts, *images), 2 * rows * rows * width, 24)


def pairs_odd(scale, bias, texts, image_all, after):
    count, own, width = texts.shape
    rows = count * own

    def body(scale_ref, bias_ref, texts, image_all, _, flipped, out, factor_all):
        factor_rows(scale_ref[0], bias_ref[0], texts, image_all, factor_all, flipped, 256, True)
        text_grads(factor_all, image_all, out, 256, True)

    outs = [shape(rows, rows), shape(count, own, width)]
    scratch = [pltpu.VMEM((rows, rows), BF16)]
    arrays = (texts, image_all, after)
    return pair_call("pairs_odd", body, outs, scale, bias, arrays, 4 * rows * rows * width, 24, scratch)


def pairs_image(name, flips, texts, start, stop, outs, after, tile, unroll):
    own, width = texts[0].shape[-2:]

    def body(flip_even, flip_odd, even, odd, *out_refs):
        def columns_at(here):
            factor = jnp.concatenate([flip_even[start:stop], flip_odd[start:stop]], axis=1)
            rows = jnp.concatenate([ref[:, :, here].reshape(-1, tile) for ref in (even, odd)], axis=0)
            total = product(factor, rows).astype(BF16)
            place = 0
            for ref in out_refs:
                size = ref.size // width
                ref[..., here] = total[place : place + size].reshape(*ref.shape[:-1], tile)
                place += size

        tiles(width // tile, tile, columns_at, unroll)

    flops = 2 * (stop - start) * 16 * own * width
    return call(name, body, outs, (*flips, *texts), flops, 24, after)


def weight_part(name, column, place, pieces, halves, feat, after, more=0):
    count, width = len(pieces), pieces[-1].shape[-1]
    rows, features = feat.shape
    own = rows // 8
    strip = width // 16
    tile = 256

    def body(column_ref, place_ref, *refs):
        feat_ref, same, other, flipped, moved, result = refs[count:]
        for n, part in enumerate(near_far_order(grouped(refs[:count], halves))):
            k = NEAR_FAR[n]
            flipped[:, k * own : (k + 1) * own] = part.T
        def features_at(here):
            for k in range(rows // own):
                start = pl.multiple_of((column_ref[0] ^ k) * own, own)
                moved[k * own : (k + 1) * own] = feat_ref[pl.ds(start, own), here]
            result[...] = product(flipped[...], moved[...]).astype(BF16)
            for j, k in enumerate((0, 2, 4, 6, 12, 14, 8, 10)):
                mine = pl.multiple_of((place_ref[0] ^ k) * strip, strip)
                theirs = pl.multiple_of((place_ref[0] ^ (k + 1)) * strip, strip)
                same[j, :, here] = result[pl.ds(mine, strip)]
                other[j, :, here] = result[pl.ds(theirs, strip)]

        tiles(features // tile, tile, features_at, True)

    smem, vmem = pl.BlockSpec(memory_space=pltpu.SMEM), pl.BlockSpec(memory_space=pltpu.VMEM)
    specs = [smem, smem] + [vmem] * (len(pieces) + 1)
    scratch = [
        pltpu.VMEM((width, rows), BF16),
        pltpu.VMEM((rows, tile), BF16),
        pltpu.VMEM((width, tile), BF16),
    ]
    outs = [shape(8, strip, features)] * 2
    flops = 2 * rows * width * features + more
    return call(name, body, outs, (column, place, *pieces, feat), flops, 16, after, specs, scratch)


def feature_grad(name, column, pieces, halves, weight, after=None):
    count, width = len(pieces), pieces[-1].shape[-1]
    features = weight.shape[0]
    own = pieces[0].shape[1] * halves
    rows = 8 * own
    tile = 256

    def body(column_ref, *refs):
        weight_ref, out, mark = refs[count:]
        mark[...] = jnp.zeros_like(mark)
        def features_at(here):
            egrad = jnp.concatenate(near_far_order(grouped(refs[:count], halves)), axis=0)
            result = lax.dot_general(
                egrad, weight_ref[here], (((1,), (1,)), ((), ())), preferred_element_type=F32
            ).astype(BF16)
            for n, k in enumerate(NEAR_FAR):
                start = pl.multiple_of((column_ref[0] ^ k) * own, own)
                out[pl.ds(start, own), here] = result[n * own : (n + 1) * own]

        tiles(features // tile, tile, features_at)

    smem, vmem = pl.BlockSpec(memory_space=pltpu.SMEM), pl.BlockSpec(memory_space=pltpu.VMEM)
    outs, ins = [shape(rows, features), shape(16, 128)], (column, *pieces, weight)
    return call(name, body, outs, ins, 2 * rows * width * features, 16, after, [smem] + [vmem] * (len(pieces) + 1))


def chip_weight(name, same, other, after=None):
    strip, features = same.shape[1:]

    def body(same, got, *outs):
        for j, out in enumerate(outs):
            out[...] = (wide(same, slice(2 * j, 2 * j + 2)) + wide(got, slice(2 * j, 2 * j + 2))).astype(BF16)

    outs = [shape(2, strip, features)] * 4
    return call(name, body, outs, (same, swap(other, "blk", 1)), after=after)


def sum_weight(p02, p46, p1214, p810):
    strip, features = p02.shape[1:]

    def along_z(p02, p46, p1214, p810, p0_out, p2_out):
        total = wide(p02) + wide(p46) + wide(p1214) + wide(p810)
        p0_out[...] = total[0]
        p2_out[...] = total[1].astype(BF16)

    def along_y(p0, p2, out):
        out[...] = p0[...] + wide(p2)

    p46, p1214, p810 = swap(p46, "blk", 4), swap(p1214, "blk", 12), swap(p810, "blk", 8)
    outs = [shape(strip, features, dtype=F32), shape(strip, features)]
    p0, p2 = call("weight_z", along_z, outs, (p02, p46, p1214, p810))
    p2 = swap(p2, "blk", 2)
    return call("weight_y", along_y, outs[:1], (p0, p2))[0].T


def chip_weight_y(name, same, other, after=None):
    strip, features = same.shape[1:]

    def body(same, got, mine, theirs):
        for j in range(4):
            for k, out in enumerate((mine, theirs)):
                out[j] = (wide(same, 2 * j + k) + wide(got, 2 * j + k)).astype(BF16)

    outs = [shape(4, strip, features)] * 2
    return call(name, body, outs, (same, swap(other, "blk", 1)), after=after)


def sum_weight_y(mine, theirs):
    strip, features = mine.shape[1:]
    one = (strip, features)

    def along_y(mine, got, p0, p4, p12, p8):
        p0[...] = wide(mine, 0) + wide(got, 0)
        for j, out in ((1, p4), (2, p12), (3, p8)):
            out[...] = (wide(mine, j) + wide(got, j)).astype(BF16)

    def along_z(p0, p4, p12, p8, out):
        out[...] = p0[...] + wide(p4) + wide(p12) + wide(p8)

    outs = [shape(*one, dtype=F32)] + [shape(*one)] * 3
    p0, p4, p12, p8 = call("weight_image_y", along_y, outs, (mine, swap(theirs, "blk", 2)), ORDER_COST * 2 // 5)
    p4, p12, p8 = swap(p4, "blk", 4), swap(p12, "blk", 12), swap(p8, "blk", 8)
    return call("weight_image_z", along_z, outs[:1], (p0, p4, p12, p8))[0].T, p0


def local(img_feat, txt_feat, img_weight, txt_weight, natural_exponent_multiplier, bias):
    scale = jnp.exp(natural_exponent_multiplier)
    blocks = lax.axis_size("mp")
    column = lax.axis_index("mp").astype(jnp.int32)[None]
    place = lax.axis_index("blk").astype(jnp.int32)[None]
    own = img_feat.shape[0] // blocks
    width = img_weight.shape[1]
    one, two = (own, width), (2, own, width)

    half = (2, own // 2, width)
    own_half = (own // 2, width)

    t01, t23, t67, t4, t5 = embed("embed_text", txt_feat, txt_weight, column, blocks)
    t4, t5 = swap(t4, "mp", 6), swap(t5, "mp", 2)
    i01, i23, i67, i4, i5 = embed("embed_image", img_feat, img_weight, column, blocks)
    t23, t67 = call("relay_text", relay_add, [shape(*two)] * 2, (t23, t67, t4, t5))
    t23, t67 = swap(t23, "mp", 2), swap(t67, "mp", 6)
    i4, i5 = swap(i4, "mp", 6), swap(i5, "mp", 2)

    def second(t01, t23, t67, t0_out, t1_out):
        t0_out[...] = wide(t01, 0) + wide(t23, 0) + wide(t67, 0)
        t1_out[...] = (wide(t01, 1) + wide(t23, 1) + wide(t67, 1)).astype(BF16)

    t0, t1 = call("sums_second", second, [shape(*one, dtype=F32), shape(*one)], (t01, t23, t67))
    t1_got = swap(t1, "mp", 1)
    sent = call("relay_image", relay_split, [shape(*half)] * 4, (i23, i67, i4, i5), after=t1)
    got = [(swap(sent[2 * h], "mp", 2), swap(sent[2 * h + 1], "mp", 6)) for h in range(2)]

    def third(t0, t1, text_out, unit_out):
        embedded = t0[...] + wide(t1)
        text_out[...] = embedded
        unit_out[...] = unit_of(embedded)[0].astype(BF16)

    txt_emb, a0 = call("sums_third", third, [shape(*one, dtype=F32), shape(*one)], (t0, t1_got), after=sent[0])
    a2 = swap(a0, "blk", 2)
    (x_a,) = call("image_x_a", add_half(0), [shape(*half)], (i01, *got[0]), after=a0)
    y_a = swap(x_a, "mp", 1)
    (a02,) = call("stack_text", stack, [shape(*two)], (a0, a2), after=x_a)
    a46, a1214 = swap(a02, "blk", 4), swap(a02, "blk", 12)
    (x_b,) = call("image_x_b", add_half(1), [shape(*half)], (i01, *got[1]), after=a02)
    y_b = swap(x_b, "mp", 1)
    outs = [shape(*half, dtype=F32), shape(*half)]
    emb_a, u01_a = call("image_unit_a", norm_half, outs, (x_a, y_a), after=x_b)
    u23_a, u67_a = swap(u01_a, "mp", 2), swap(u01_a, "mp", 6)
    emb_b, u01_b = call("image_unit_b", norm_half, outs, (x_b, y_b), after=u01_a)
    u23_b, u67_b = swap(u01_b, "mp", 2), swap(u01_b, "mp", 6)
    outs = [shape(*own_half)] * 2
    u2_a, u7_a = call("cut_image_a", cut, outs, (u23_a, u67_a), after=u01_b)
    u4_a, u5_a = swap(u2_a, "mp", 6), swap(u7_a, "mp", 2)
    a4, a14 = call("cut_text", cut, [shape(*one)] * 2, (a46, a1214), after=u2_a)
    a8, a10 = swap(a4, "blk", 12), swap(a14, "blk", 4)
    u2_b, u7_b = call("cut_image_b", cut, outs, (u23_b, u67_b), after=a4)
    u4_b, u5_b = swap(u2_b, "mp", 6), swap(u7_b, "mp", 2)

    def collect(a02, a46, a1214, a8, a10, out):
        for k, ref in enumerate((a02, a46, a1214)):
            out[2 * k : 2 * k + 2] = ref[...]
        out[6] = a8[...]
        out[7] = a10[...]

    (even,) = call("collect", collect, [shape(8, *one)], (a02, a46, a1214, a8, a10), after=(u4_a, u5_a, u4_b, u5_b))
    odd = swap(even, "blk", 1)
    images = (u01_a, u01_b, u23_a, u23_b, u67_a, u67_b, u4_a, u4_b, u5_a, u5_b)
    factor_even, flip_even, image_all = pairs_even(scale, bias, even, images)
    flip_odd, odd_sum = pairs_odd(scale, bias, odd, image_all, flip_even)
    odd_got = swap(odd_sum, "blk", 1)
    flips, texts = (flip_even, flip_odd), (even, odd)
    g4, g5 = pairs_image("pairs_far_images", flips, texts, 6 * own, 8 * own, [shape(*one)] * 2, odd_sum, 256, True)
    g4_got, g5_got = swap(g4, "mp", 6), swap(g5, "mp", 2)
    flops = 128 * own * own * width
    (even_sum,) = call("text_grads_even", text_grads, [shape(8, *one)], (factor_even, image_all), flops, 20, g4)

    def fifth(even, got, p8, p10):
        p8[...] = (wide(even, 6) + wide(got, 6)).astype(BF16)
        p10[...] = (wide(even, 7) + wide(got, 7)).astype(BF16)

    p8, p10 = call("sums_fifth", fifth, [shape(*one)] * 2, (even_sum, odd_got))
    g01, g23, g67 = pairs_image("pairs_near_images", flips, texts, 0, 6 * own, [shape(*two)] * 3, p8, 512, False)
    p8_got, p10_got = swap(p8, "blk", 12), swap(p10, "blk", 4)
    sent = call("relay_image_grads", relay_split, [shape(*half)] * 4, (g23, g67, g4_got, g5_got))
    got = [(swap(sent[2 * h], "mp", 2), swap(sent[2 * h + 1], "mp", 6)) for h in range(2)]

    def sixth(even, got, p8, p10, p02, p46, p1214):
        for k in range(2):
            p02[k] = (wide(even, k) + wide(got, k)).astype(BF16)
        p46[0] = (wide(even, 2) + wide(got, 2) + wide(p8)).astype(BF16)
        p46[1] = (wide(even, 3) + wide(got, 3)).astype(BF16)
        p1214[0] = (wide(even, 4) + wide(got, 4)).astype(BF16)
        p1214[1] = (wide(even, 5) + wide(got, 5) + wide(p10)).astype(BF16)

    outs = [shape(*two)] * 3
    p02, p46, p1214 = call("sums_sixth", sixth, outs, (even_sum, odd_got, p8_got, p10_got), after=sent[0])
    p46, p1214 = swap(p46, "blk", 4), swap(p1214, "blk", 12)
    (x_a,) = call("image_grads_x_a", add_half(0), [shape(*half)], (g01, *got[0]), ORDER_COST // 2, after=p02)
    y_a = swap(x_a, "mp", 1)
    (x_b,) = call("image_grads_x_b", add_half(1), [shape(*half)], (g01, *got[1]), after=x_a)
    y_b = swap(x_b, "mp", 1)
    def seventh(p02, p46, p1214, p0_out, p2_out):
        p0_out[...] = wide(p02, 0) + wide(p46, 0) + wide(p1214, 0)
        p2_out[...] = (wide(p02, 1) + wide(p46, 1) + wide(p1214, 1)).astype(BF16)

    outs = [shape(*one, dtype=F32), shape(*one)]
    p0, p2 = call("sums_seventh", seventh, outs, (p02, p46, p1214), after=x_b)
    p2_got = swap(p2, "blk", 2)
    (e01_a,) = call("image_back_a", back_half, [shape(*half)], (x_a, y_a, emb_a), after=p2)
    e23_a, e67_a, e45_a = swap(e01_a, "mp", 2), swap(e01_a, "mp", 6), swap(e01_a, "mp", 4)

    def text_back(p0, p2, txt_emb, out):
        out[...] = norm_back(p0[...] + wide(p2), txt_emb[...]).astype(BF16)

    (d0,) = call("text_back", text_back, [shape(*one)], (p0, p2_got, txt_emb), after=e01_a)
    d1 = swap(d0, "mp", 1)
    (e01_b,) = call("image_back_b", back_half, [shape(*half)], (x_b, y_b, emb_b), after=d0)
    e23_b, e67_b, e45_b = swap(e01_b, "mp", 2), swap(e01_b, "mp", 6), swap(e01_b, "mp", 4)

    (d01,) = call("stack_text_grads", stack, [shape(*two)], (d0, d1), after=(e01_b, e23_a, e67_a, e45_a))
    d23, d67 = swap(d01, "mp", 2), swap(d01, "mp", 6)

    e_all = (e01_a, e01_b, e23_a, e23_b, e67_a, e67_b, e45_a, e45_b)
    same, other = weight_part("weight_image", column, place, e_all, 2, img_feat, d01, ORDER_COST // 4)
    d2, d7 = call("cut_text_grads", cut, [shape(*one)] * 2, (d23, d67), ORDER_COST, after=same)
    d4, d5 = swap(d2, "mp", 6), swap(d7, "mp", 2)
    image_chip = chip_weight_y("weight_image_chip", same, other)
    img_feat_grad, image_done = feature_grad("feature_image", column, e_all, 2, img_weight, image_chip[0])
    img_weight_grad, image_y = sum_weight_y(*image_chip)
    d_all = (d01, d23, d67, d4, d5)
    same, other = weight_part("weight_text", column, place, d_all, 1, txt_feat, image_done)
    txt_weight_grad = sum_weight(*chip_weight("weight_text_chip", same, other, image_y))
    txt_feat_grad, _ = feature_grad("feature_text", column, d_all, 1, txt_weight)
    return (img_feat_grad, txt_feat_grad, img_weight_grad, txt_weight_grad)


def solution(mesh):
    return jax.shard_map(
        local,
        mesh=mesh,
        in_specs=(P("blk", "mp"), P("blk", "mp"), P("mp", None), P("mp", None), P(), P()),
        out_specs=(P("blk", "mp"), P("blk", "mp"), P("mp", "blk"), P("mp", "blk")),
        check_vma=False,
    )
```

```python
import jax
import jax.numpy as jnp
from jax import lax
from jax.experimental import pallas as pl
from jax.experimental.pallas import tpu as pltpu
from jax.sharding import PartitionSpec as P

EPS = 1e-06
BF16 = jnp.bfloat16
F32 = jnp.float32
MIB = 1024 * 1024
ORDER_COST = 10 * 10**9
NEAR_FAR = (0, 1, 2, 3, 6, 7, 4, 5)


def swap(value, axis, offset):
    count = lax.axis_size(axis)
    return lax.ppermute(value, axis, [(i, i ^ offset) for i in range(count)])


def shape(*dims, dtype=BF16):
    return jax.ShapeDtypeStruct(dims, dtype)


def call(name, body, outs, ins, flops=0, limit=10, after=None, in_specs=None, scratch=()):
    ins, specs = list(ins), in_specs or [pl.BlockSpec(memory_space=pltpu.VMEM)] * len(ins)
    run = body
    if after is not None:
        after = list(after) if isinstance(after, tuple) else [after]
        ins, specs = after + ins, [pl.BlockSpec(memory_space=pltpu.VMEM)] * len(after) + list(specs)

        def run(*refs):
            body(*refs[len(after) :])

    moved = sum(a.size * a.dtype.itemsize for a in ins + list(outs))
    return pl.pallas_call(
        run,
        out_shape=outs,
        in_specs=specs,
        scratch_shapes=list(scratch),
        compiler_params=pltpu.CompilerParams(vmem_limit_bytes=limit * MIB),
        cost_estimate=pl.CostEstimate(flops=flops, bytes_accessed=moved, transcendentals=0),
        name=name,
    )(*ins)


def tiles(count, size, body, unroll=False):
    if unroll:
        for index in range(count):
            body(slice(index * size, (index + 1) * size))
        return

    def step(index, carry):
        body(pl.ds(pl.multiple_of(index * size, size), size))
        return carry

    lax.fori_loop(0, count, step, 0)


def wide(ref, block=None):
    return (ref[...] if block is None else ref[block]).astype(F32)


def embed(name, feat, weight, column, blocks, tile=256):
    rows, width = feat.shape
    columns = weight.shape[1]
    own = rows // blocks

    def body(column_ref, feat_ref, weight_ref, p01, p23, p67, p4, p5, result):
        def part(k):
            return result[pl.ds(pl.multiple_of((column_ref[0] ^ k) * own, own), own)]

        def columns_at(here):
            result[...] = product(feat_ref[...], weight_ref[:, here]).astype(BF16)
            for k in range(2):
                p01[k, :, here] = part(k)
                p23[k, :, here] = part(2 + k)
                p67[k, :, here] = part(6 + k)
            p4[:, here] = part(4)
            p5[:, here] = part(5)

        tiles(columns // tile, tile, columns_at)

    outs = [shape(2, own, columns)] * 3 + [shape(own, columns)] * 2
    specs = [pl.BlockSpec(memory_space=pltpu.SMEM)] + [pl.BlockSpec(memory_space=pltpu.VMEM)] * 2
    scratch = [pltpu.VMEM((rows, tile), BF16)]
    return call(name, body, outs, (column, feat, weight), 2 * rows * width * columns, 16, None, specs, scratch)


def relay_add(p23, p67, r4, r5, out23, out67):
    out23[0] = (wide(p23, 0) + wide(r4)).astype(BF16)
    out23[1] = p23[1]
    out67[0] = p67[0]
    out67[1] = (wide(p67, 1) + wide(r5)).astype(BF16)


def relay_split(p23, p67, r4, r5, a23, a67, b23, b67):
    half = r4.shape[0] // 2
    for h, (out23, out67) in enumerate(((a23, a67), (b23, b67))):
        rows = slice(h * half, (h + 1) * half)
        out23[0] = (p23[0, rows].astype(F32) + wide(r4, rows)).astype(BF16)
        out23[1] = p23[1, rows]
        out67[0] = p67[0, rows]
        out67[1] = (p67[1, rows].astype(F32) + wide(r5, rows)).astype(BF16)


def add_half(h):
    def body(p01, r23, r67, out):
        half = out.shape[1]
        for k in range(2):
            own = p01[k, h * half : (h + 1) * half].astype(F32)
            out[k] = (own + wide(r23, k) + wide(r67, k)).astype(BF16)

    return body


def norm_half(p01, got01, emb_out, unit_out):
    for k in range(2):
        embedded = wide(p01, k) + wide(got01, 1 - k)
        emb_out[k] = embedded
        unit_out[k] = unit_of(embedded)[0].astype(BF16)


def back_half(g01, got01, emb, out):
    for k in range(2):
        out[k] = norm_back(wide(g01, k) + wide(got01, 1 - k), emb[k]).astype(BF16)


def cut(near, other, first_out, last_out):
    first_out[...] = near[0]
    last_out[...] = other[1]


def stack(first, second, out):
    out[0] = first[...]
    out[1] = second[...]


def grouped(refs, halves):
    return [refs[i : i + halves] for i in range(0, len(refs), halves)]


def block(group, k=None):
    parts = [ref[...] if k is None else ref[k] for ref in group]
    return parts[0] if len(parts) == 1 else jnp.concatenate(parts, axis=0)


def near_far_order(groups):
    pairs = [block(g, k) for g in groups[:3] for k in range(2)]
    if len(groups) == 4:
        return pairs + [block(groups[3], k) for k in range(2)]
    return pairs + [block(g) for g in groups[3:]]


def unit_of(embedded):
    inverse = lax.rsqrt(jnp.sum(embedded * embedded, axis=1, keepdims=True) + EPS)
    return embedded * inverse, inverse


def norm_back(unit_grad, embedded):
    unit, inverse = unit_of(embedded)
    return inverse * (unit_grad - unit * jnp.sum(unit * unit_grad, axis=1, keepdims=True))


def flat(ref):
    return ref[...].reshape(-1, ref.shape[-1])


def factors(scale, bias, txt, img):
    affinity = lax.dot_general(txt, img, (((1,), (1,)), ((), ())), preferred_element_type=F32)
    logits = scale * affinity + bias
    return logits, (scale / (1.0 + jnp.exp(-logits))).astype(BF16)


def product(first, second):
    return jnp.dot(first, second, preferred_element_type=F32)


def pair_call(name, body, outs, scale, bias, arrays, flops, limit, scratch=()):
    smem = pl.BlockSpec(memory_space=pltpu.SMEM)
    vmem = pl.BlockSpec(memory_space=pltpu.VMEM)
    moved = sum(a.size * a.dtype.itemsize for a in list(arrays) + outs)
    return pl.pallas_call(
        body,
        in_specs=[smem, smem] + [vmem] * len(arrays),
        out_shape=outs,
        scratch_shapes=list(scratch),
        compiler_params=pltpu.CompilerParams(vmem_limit_bytes=limit * MIB),
        cost_estimate=pl.CostEstimate(flops=flops, bytes_accessed=moved, transcendentals=0),
        name=name,
    )(scale, bias, *arrays)


def image_rows(image_refs, image_all):
    own = image_all.shape[0] // 8
    for k, part in enumerate(near_far_order(grouped(image_refs, 2))):
        image_all[k * own : (k + 1) * own] = part


def factor_rows(scale, bias, texts, image_all, factor_all, flipped, tile, unroll):
    def images_at(here):
        factor = factors(scale, bias, flat(texts), image_all[here])[1]
        factor_all[:, here] = factor
        flipped[here] = factor.T

    tiles(image_all.shape[0] // tile, tile, images_at, unroll)


def match(scale, bias, texts, image_all, factor_all, flipped):
    own = texts.shape[1]
    logits = factors(scale, bias, texts[0], image_all[:own])[0]
    row = lax.broadcasted_iota(jnp.int32, logits.shape, 0)
    column = lax.broadcasted_iota(jnp.int32, logits.shape, 1)
    pull = (-scale / (1.0 + jnp.exp(logits))).astype(BF16)
    factor = jnp.where(row == column, pull, factor_all[:own, :own])
    factor_all[:own, :own] = factor
    flipped[:own, :own] = factor.T


def text_grads(factor_all, image_all, out, tile=512, unroll=False):
    def columns_at(here):
        grads = product(factor_all[...], image_all[:, here]).astype(BF16)
        out[:, :, here] = grads.reshape(*out.shape[:2], tile)

    tiles(out.shape[-1] // tile, tile, columns_at, unroll)


def pairs_even(scale, bias, texts, images):
    count, own, width = texts.shape
    rows = count * own

    def body(scale_ref, bias_ref, texts, *refs):
        image_refs, (factor_all, flipped, image_all) = refs[:10], refs[10:]
        image_rows(image_refs, image_all)
        scale, bias = scale_ref[0], bias_ref[0]
        factor_rows(scale, bias, texts, image_all, factor_all, flipped, 512, False)
        match(scale, bias, texts, image_all, factor_all, flipped)

    outs = [shape(rows, rows), shape(rows, rows), shape(rows, width)]
    return pair_call("pairs_even", body, outs, scale, bias, (texts, *images), 2 * rows * rows * width, 24)


def pairs_odd(scale, bias, texts, image_all, after):
    count, own, width = texts.shape
    rows = count * own

    def body(scale_ref, bias_ref, texts, image_all, _, flipped, out, factor_all):
        factor_rows(scale_ref[0], bias_ref[0], texts, image_all, factor_all, flipped, 256, True)
        text_grads(factor_all, image_all, out, 256, True)

    outs = [shape(rows, rows), shape(count, own, width)]
    scratch = [pltpu.VMEM((rows, rows), BF16)]
    arrays = (texts, image_all, after)
    return pair_call("pairs_odd", body, outs, scale, bias, arrays, 4 * rows * rows * width, 24, scratch)


def pairs_image(name, flips, texts, start, stop, outs, after, tile, unroll):
    own, width = texts[0].shape[-2:]

    def body(flip_even, flip_odd, even, odd, *out_refs):
        def columns_at(here):
            factor = jnp.concatenate([flip_even[start:stop], flip_odd[start:stop]], axis=1)
            rows = jnp.concatenate([ref[:, :, here].reshape(-1, tile) for ref in (even, odd)], axis=0)
            total = product(factor, rows).astype(BF16)
            place = 0
            for ref in out_refs:
                size = ref.size // width
                ref[..., here] = total[place : place + size].reshape(*ref.shape[:-1], tile)
                place += size

        tiles(width // tile, tile, columns_at, unroll)

    flops = 2 * (stop - start) * 16 * own * width
    return call(name, body, outs, (*flips, *texts), flops, 24, after)


def weight_part(name, column, place, pieces, halves, feat, after, more=0):
    count, width = len(pieces), pieces[-1].shape[-1]
    rows, features = feat.shape
    own = rows // 8
    strip = width // 16
    tile = 256

    def body(column_ref, place_ref, *refs):
        feat_ref, same, other, flipped, moved, result = refs[count:]
        for n, part in enumerate(near_far_order(grouped(refs[:count], halves))):
            k = NEAR_FAR[n]
            flipped[:, k * own : (k + 1) * own] = part.T
        def features_at(here):
            for k in range(rows // own):
                start = pl.multiple_of((column_ref[0] ^ k) * own, own)
                moved[k * own : (k + 1) * own] = feat_ref[pl.ds(start, own), here]
            result[...] = product(flipped[...], moved[...]).astype(BF16)
            for j, k in enumerate((0, 2, 4, 6, 12, 14, 8, 10)):
                mine = pl.multiple_of((place_ref[0] ^ k) * strip, strip)
                theirs = pl.multiple_of((place_ref[0] ^ (k + 1)) * strip, strip)
                same[j, :, here] = result[pl.ds(mine, strip)]
                other[j, :, here] = result[pl.ds(theirs, strip)]

        tiles(features // tile, tile, features_at, True)

    smem, vmem = pl.BlockSpec(memory_space=pltpu.SMEM), pl.BlockSpec(memory_space=pltpu.VMEM)
    specs = [smem, smem] + [vmem] * (len(pieces) + 1)
    scratch = [
        pltpu.VMEM((width, rows), BF16),
        pltpu.VMEM((rows, tile), BF16),
        pltpu.VMEM((width, tile), BF16),
    ]
    outs = [shape(8, strip, features)] * 2
    flops = 2 * rows * width * features + more
    return call(name, body, outs, (column, place, *pieces, feat), flops, 16, after, specs, scratch)


def feature_grad(name, column, pieces, halves, weight):
    count, width = len(pieces), pieces[-1].shape[-1]
    features = weight.shape[0]
    own = pieces[0].shape[1] * halves
    rows = 8 * own
    tile = 256

    def body(column_ref, *refs):
        weight_ref, out = refs[count:]
        def features_at(here):
            egrad = jnp.concatenate(near_far_order(grouped(refs[:count], halves)), axis=0)
            result = lax.dot_general(
                egrad, weight_ref[here], (((1,), (1,)), ((), ())), preferred_element_type=F32
            ).astype(BF16)
            for n, k in enumerate(NEAR_FAR):
                start = pl.multiple_of((column_ref[0] ^ k) * own, own)
                out[pl.ds(start, own), here] = result[n * own : (n + 1) * own]

        tiles(features // tile, tile, features_at)

    smem, vmem = pl.BlockSpec(memory_space=pltpu.SMEM), pl.BlockSpec(memory_space=pltpu.VMEM)
    outs, ins = [shape(rows, features)], (column, *pieces, weight)
    return call(name, body, outs, ins, 2 * rows * width * features, 16, None, [smem] + [vmem] * (len(pieces) + 1))[0]


def chip_weight(name, same, other, after=None):
    strip, features = same.shape[1:]

    def body(same, got, *outs):
        for j, out in enumerate(outs):
            out[...] = (wide(same, slice(2 * j, 2 * j + 2)) + wide(got, slice(2 * j, 2 * j + 2))).astype(BF16)

    outs = [shape(2, strip, features)] * 4
    return call(name, body, outs, (same, swap(other, "blk", 1)), after=after)


def sum_weight(p02, p46, p1214, p810):
    strip, features = p02.shape[1:]

    def along_z(p02, p46, p1214, p810, p0_out, p2_out):
        total = wide(p02) + wide(p46) + wide(p1214) + wide(p810)
        p0_out[...] = total[0]
        p2_out[...] = total[1].astype(BF16)

    def along_y(p0, p2, out):
        out[...] = p0[...] + wide(p2)

    p46, p1214, p810 = swap(p46, "blk", 4), swap(p1214, "blk", 12), swap(p810, "blk", 8)
    outs = [shape(strip, features, dtype=F32), shape(strip, features)]
    p0, p2 = call("weight_z", along_z, outs, (p02, p46, p1214, p810))
    p2 = swap(p2, "blk", 2)
    return call("weight_y", along_y, outs[:1], (p0, p2))[0].T


def chip_weight_y(name, same, other, after=None):
    strip, features = same.shape[1:]

    def body(same, got, mine, theirs):
        for j in range(4):
            for k, out in enumerate((mine, theirs)):
                out[j] = (wide(same, 2 * j + k) + wide(got, 2 * j + k)).astype(BF16)

    outs = [shape(4, strip, features)] * 2
    return call(name, body, outs, (same, swap(other, "blk", 1)), after=after)


def sum_weight_y(mine, theirs):
    strip, features = mine.shape[1:]
    one = (strip, features)

    def along_y(mine, got, p0, p4, p12, p8):
        p0[...] = wide(mine, 0) + wide(got, 0)
        for j, out in ((1, p4), (2, p12), (3, p8)):
            out[...] = (wide(mine, j) + wide(got, j)).astype(BF16)

    def along_z(p0, p4, p12, p8, out):
        out[...] = p0[...] + wide(p4) + wide(p12) + wide(p8)

    outs = [shape(*one, dtype=F32)] + [shape(*one)] * 3
    p0, p4, p12, p8 = call("weight_image_y", along_y, outs, (mine, swap(theirs, "blk", 2)), ORDER_COST * 2 // 5)
    p4, p12, p8 = swap(p4, "blk", 4), swap(p12, "blk", 12), swap(p8, "blk", 8)
    return call("weight_image_z", along_z, outs[:1], (p0, p4, p12, p8))[0].T, p0


def local(img_feat, txt_feat, img_weight, txt_weight, natural_exponent_multiplier, bias):
    scale = jnp.exp(natural_exponent_multiplier)
    blocks = lax.axis_size("mp")
    column = lax.axis_index("mp").astype(jnp.int32)[None]
    place = lax.axis_index("blk").astype(jnp.int32)[None]
    own = img_feat.shape[0] // blocks
    width = img_weight.shape[1]
    one, two = (own, width), (2, own, width)

    half = (2, own // 2, width)
    own_half = (own // 2, width)

    t01, t23, t67, t4, t5 = embed("embed_text", txt_feat, txt_weight, column, blocks)
    t4, t5 = swap(t4, "mp", 6), swap(t5, "mp", 2)
    i01, i23, i67, i4, i5 = embed("embed_image", img_feat, img_weight, column, blocks)
    t23, t67 = call("relay_text", relay_add, [shape(*two)] * 2, (t23, t67, t4, t5))
    t23, t67 = swap(t23, "mp", 2), swap(t67, "mp", 6)
    i4, i5 = swap(i4, "mp", 6), swap(i5, "mp", 2)

    def second(t01, t23, t67, t0_out, t1_out):
        t0_out[...] = wide(t01, 0) + wide(t23, 0) + wide(t67, 0)
        t1_out[...] = (wide(t01, 1) + wide(t23, 1) + wide(t67, 1)).astype(BF16)

    t0, t1 = call("sums_second", second, [shape(*one, dtype=F32), shape(*one)], (t01, t23, t67))
    t1_got = swap(t1, "mp", 1)
    sent = call("relay_image", relay_split, [shape(*half)] * 4, (i23, i67, i4, i5), after=t1)
    got = [(swap(sent[2 * h], "mp", 2), swap(sent[2 * h + 1], "mp", 6)) for h in range(2)]

    def third(t0, t1, text_out, unit_out):
        embedded = t0[...] + wide(t1)
        text_out[...] = embedded
        unit_out[...] = unit_of(embedded)[0].astype(BF16)

    txt_emb, a0 = call("sums_third", third, [shape(*one, dtype=F32), shape(*one)], (t0, t1_got), after=sent[0])
    a2 = swap(a0, "blk", 2)
    (x_a,) = call("image_x_a", add_half(0), [shape(*half)], (i01, *got[0]), after=a0)
    y_a = swap(x_a, "mp", 1)
    (a02,) = call("stack_text", stack, [shape(*two)], (a0, a2), after=x_a)
    a46, a1214 = swap(a02, "blk", 4), swap(a02, "blk", 12)
    (x_b,) = call("image_x_b", add_half(1), [shape(*half)], (i01, *got[1]), after=a02)
    y_b = swap(x_b, "mp", 1)
    outs = [shape(*half, dtype=F32), shape(*half)]
    emb_a, u01_a = call("image_unit_a", norm_half, outs, (x_a, y_a), after=x_b)
    u23_a, u67_a = swap(u01_a, "mp", 2), swap(u01_a, "mp", 6)
    emb_b, u01_b = call("image_unit_b", norm_half, outs, (x_b, y_b), after=u01_a)
    u23_b, u67_b = swap(u01_b, "mp", 2), swap(u01_b, "mp", 6)
    outs = [shape(*own_half)] * 2
    u2_a, u7_a = call("cut_image_a", cut, outs, (u23_a, u67_a), after=u01_b)
    u4_a, u5_a = swap(u2_a, "mp", 6), swap(u7_a, "mp", 2)
    a4, a14 = call("cut_text", cut, [shape(*one)] * 2, (a46, a1214), after=u2_a)
    a8, a10 = swap(a4, "blk", 12), swap(a14, "blk", 4)
    u2_b, u7_b = call("cut_image_b", cut, outs, (u23_b, u67_b), after=a4)
    u4_b, u5_b = swap(u2_b, "mp", 6), swap(u7_b, "mp", 2)

    def collect(a02, a46, a1214, a8, a10, out):
        for k, ref in enumerate((a02, a46, a1214)):
            out[2 * k : 2 * k + 2] = ref[...]
        out[6] = a8[...]
        out[7] = a10[...]

    (even,) = call("collect", collect, [shape(8, *one)], (a02, a46, a1214, a8, a10), after=(u4_a, u5_a, u4_b, u5_b))
    odd = swap(even, "blk", 1)
    images = (u01_a, u01_b, u23_a, u23_b, u67_a, u67_b, u4_a, u4_b, u5_a, u5_b)
    factor_even, flip_even, image_all = pairs_even(scale, bias, even, images)
    flip_odd, odd_sum = pairs_odd(scale, bias, odd, image_all, flip_even)
    odd_got = swap(odd_sum, "blk", 1)
    flips, texts = (flip_even, flip_odd), (even, odd)
    g4, g5 = pairs_image("pairs_far_images", flips, texts, 6 * own, 8 * own, [shape(*one)] * 2, odd_sum, 256, True)
    g4_got, g5_got = swap(g4, "mp", 6), swap(g5, "mp", 2)
    flops = 128 * own * own * width
    (even_sum,) = call("text_grads_even", text_grads, [shape(8, *one)], (factor_even, image_all), flops, 20, g4)

    def fifth(even, got, p8, p10):
        p8[...] = (wide(even, 6) + wide(got, 6)).astype(BF16)
        p10[...] = (wide(even, 7) + wide(got, 7)).astype(BF16)

    p8, p10 = call("sums_fifth", fifth, [shape(*one)] * 2, (even_sum, odd_got))
    g01, g23, g67 = pairs_image("pairs_near_images", flips, texts, 0, 6 * own, [shape(*two)] * 3, p8, 512, False)
    p8_got, p10_got = swap(p8, "blk", 12), swap(p10, "blk", 4)
    sent = call("relay_image_grads", relay_split, [shape(*half)] * 4, (g23, g67, g4_got, g5_got))
    got = [(swap(sent[2 * h], "mp", 2), swap(sent[2 * h + 1], "mp", 6)) for h in range(2)]

    def sixth(even, got, p8, p10, p02, p46, p1214):
        for k in range(2):
            p02[k] = (wide(even, k) + wide(got, k)).astype(BF16)
        p46[0] = (wide(even, 2) + wide(got, 2) + wide(p8)).astype(BF16)
        p46[1] = (wide(even, 3) + wide(got, 3)).astype(BF16)
        p1214[0] = (wide(even, 4) + wide(got, 4)).astype(BF16)
        p1214[1] = (wide(even, 5) + wide(got, 5) + wide(p10)).astype(BF16)

    outs = [shape(*two)] * 3
    p02, p46, p1214 = call("sums_sixth", sixth, outs, (even_sum, odd_got, p8_got, p10_got), after=sent[0])
    p46, p1214 = swap(p46, "blk", 4), swap(p1214, "blk", 12)
    (x_a,) = call("image_grads_x_a", add_half(0), [shape(*half)], (g01, *got[0]), ORDER_COST * 3 // 10, after=p02)
    y_a = swap(x_a, "mp", 1)
    (x_b,) = call("image_grads_x_b", add_half(1), [shape(*half)], (g01, *got[1]), after=x_a)
    y_b = swap(x_b, "mp", 1)
    def seventh(p02, p46, p1214, p0_out, p2_out):
        p0_out[...] = wide(p02, 0) + wide(p46, 0) + wide(p1214, 0)
        p2_out[...] = (wide(p02, 1) + wide(p46, 1) + wide(p1214, 1)).astype(BF16)

    outs = [shape(*one, dtype=F32), shape(*one)]
    p0, p2 = call("sums_seventh", seventh, outs, (p02, p46, p1214), after=x_b)
    p2_got = swap(p2, "blk", 2)
    (e01_a,) = call("image_back_a", back_half, [shape(*half)], (x_a, y_a, emb_a), after=p2)
    e23_a, e67_a, e45_a = swap(e01_a, "mp", 2), swap(e01_a, "mp", 6), swap(e01_a, "mp", 4)

    def text_back(p0, p2, txt_emb, out):
        out[...] = norm_back(p0[...] + wide(p2), txt_emb[...]).astype(BF16)

    (d0,) = call("text_back", text_back, [shape(*one)], (p0, p2_got, txt_emb), after=e01_a)
    d1 = swap(d0, "mp", 1)
    (e01_b,) = call("image_back_b", back_half, [shape(*half)], (x_b, y_b, emb_b), after=d0)
    e23_b, e67_b, e45_b = swap(e01_b, "mp", 2), swap(e01_b, "mp", 6), swap(e01_b, "mp", 4)

    (d01,) = call("stack_text_grads", stack, [shape(*two)], (d0, d1), after=(e01_b, e23_a, e67_a, e45_a))
    d23, d67 = swap(d01, "mp", 2), swap(d01, "mp", 6)

    e_all = (e01_a, e01_b, e23_a, e23_b, e67_a, e67_b, e45_a, e45_b)
    same, other = weight_part("weight_image", column, place, e_all, 2, img_feat, d01, ORDER_COST // 4)
    d2, d7 = call("cut_text_grads", cut, [shape(*one)] * 2, (d23, d67), ORDER_COST, after=same)
    d4, d5 = swap(d2, "mp", 6), swap(d7, "mp", 2)
    image_chip = chip_weight_y("weight_image_chip", same, other)
    img_weight_grad, image_y = sum_weight_y(*image_chip)
    d_all = (d01, d23, d67, d4, d5)
    same, other = weight_part("weight_text", column, place, d_all, 1, txt_feat, image_chip[0])
    txt_weight_grad = sum_weight(*chip_weight("weight_text_chip", same, other, image_y))
    return (
        feature_grad("feature_image", column, e_all, 2, img_weight),
        feature_grad("feature_text", column, d_all, 1, txt_weight),
        img_weight_grad,
        txt_weight_grad,
    )


def solution(mesh):
    return jax.shard_map(
        local,
        mesh=mesh,
        in_specs=(P("blk", "mp"), P("blk", "mp"), P("mp", None), P("mp", None), P(), P()),
        out_specs=(P("blk", "mp"), P("blk", "mp"), P("mp", "blk"), P("mp", "blk")),
        check_vma=False,
    )
```

```python
import jax
import jax.numpy as jnp
from jax import lax
from jax.experimental import pallas as pl
from jax.experimental.pallas import tpu as pltpu
from jax.sharding import PartitionSpec as P

EPS = 1e-06
BF16 = jnp.bfloat16
F32 = jnp.float32
MIB = 1024 * 1024
ORDER_COST = 10 * 10**9
NEAR_FAR = (0, 1, 2, 3, 6, 7, 4, 5)


def swap(value, axis, offset):
    count = lax.axis_size(axis)
    return lax.ppermute(value, axis, [(i, i ^ offset) for i in range(count)])


def shape(*dims, dtype=BF16):
    return jax.ShapeDtypeStruct(dims, dtype)


def call(name, body, outs, ins, flops=0, limit=10, after=None, in_specs=None, scratch=()):
    ins, specs = list(ins), in_specs or [pl.BlockSpec(memory_space=pltpu.VMEM)] * len(ins)
    run = body
    if after is not None:
        after = list(after) if isinstance(after, tuple) else [after]
        ins, specs = after + ins, [pl.BlockSpec(memory_space=pltpu.VMEM)] * len(after) + list(specs)

        def run(*refs):
            body(*refs[len(after) :])

    moved = sum(a.size * a.dtype.itemsize for a in ins + list(outs))
    return pl.pallas_call(
        run,
        out_shape=outs,
        in_specs=specs,
        scratch_shapes=list(scratch),
        compiler_params=pltpu.CompilerParams(vmem_limit_bytes=limit * MIB),
        cost_estimate=pl.CostEstimate(flops=flops, bytes_accessed=moved, transcendentals=0),
        name=name,
    )(*ins)


def tiles(count, size, body, unroll=False):
    if unroll:
        for index in range(count):
            body(slice(index * size, (index + 1) * size))
        return

    def step(index, carry):
        body(pl.ds(pl.multiple_of(index * size, size), size))
        return carry

    lax.fori_loop(0, count, step, 0)


def wide(ref, block=None):
    return (ref[...] if block is None else ref[block]).astype(F32)


def embed(name, feat, weight, column, blocks, tile=256):
    rows, width = feat.shape
    columns = weight.shape[1]
    own = rows // blocks

    def body(column_ref, feat_ref, weight_ref, p01, p23, p67, p4, p5, result):
        def part(k):
            return result[pl.ds(pl.multiple_of((column_ref[0] ^ k) * own, own), own)]

        def columns_at(here):
            result[...] = product(feat_ref[...], weight_ref[:, here]).astype(BF16)
            for k in range(2):
                p01[k, :, here] = part(k)
                p23[k, :, here] = part(2 + k)
                p67[k, :, here] = part(6 + k)
            p4[:, here] = part(4)
            p5[:, here] = part(5)

        tiles(columns // tile, tile, columns_at)

    outs = [shape(2, own, columns)] * 3 + [shape(own, columns)] * 2
    specs = [pl.BlockSpec(memory_space=pltpu.SMEM)] + [pl.BlockSpec(memory_space=pltpu.VMEM)] * 2
    scratch = [pltpu.VMEM((rows, tile), BF16)]
    return call(name, body, outs, (column, feat, weight), 2 * rows * width * columns, 16, None, specs, scratch)


def relay_add(p23, p67, r4, r5, out23, out67):
    out23[0] = (wide(p23, 0) + wide(r4)).astype(BF16)
    out23[1] = p23[1]
    out67[0] = p67[0]
    out67[1] = (wide(p67, 1) + wide(r5)).astype(BF16)


def relay_split(p23, p67, r4, r5, a23, a67, b23, b67):
    half = r4.shape[0] // 2
    for h, (out23, out67) in enumerate(((a23, a67), (b23, b67))):
        rows = slice(h * half, (h + 1) * half)
        out23[0] = (p23[0, rows].astype(F32) + wide(r4, rows)).astype(BF16)
        out23[1] = p23[1, rows]
        out67[0] = p67[0, rows]
        out67[1] = (p67[1, rows].astype(F32) + wide(r5, rows)).astype(BF16)


def add_half(h):
    def body(p01, r23, r67, out):
        half = out.shape[1]
        for k in range(2):
            own = p01[k, h * half : (h + 1) * half].astype(F32)
            out[k] = (own + wide(r23, k) + wide(r67, k)).astype(BF16)

    return body


def norm_half(p01, got01, emb_out, unit_out):
    for k in range(2):
        embedded = wide(p01, k) + wide(got01, 1 - k)
        emb_out[k] = embedded
        unit_out[k] = unit_of(embedded)[0].astype(BF16)


def back_half(g01, got01, emb, out):
    for k in range(2):
        out[k] = norm_back(wide(g01, k) + wide(got01, 1 - k), emb[k]).astype(BF16)


def cut(near, other, first_out, last_out):
    first_out[...] = near[0]
    last_out[...] = other[1]


def stack(first, second, out):
    out[0] = first[...]
    out[1] = second[...]


def grouped(refs, halves):
    return [refs[i : i + halves] for i in range(0, len(refs), halves)]


def block(group, k=None):
    parts = [ref[...] if k is None else ref[k] for ref in group]
    return parts[0] if len(parts) == 1 else jnp.concatenate(parts, axis=0)


def near_far_order(groups):
    pairs = [block(g, k) for g in groups[:3] for k in range(2)]
    if len(groups) == 4:
        return pairs + [block(groups[3], k) for k in range(2)]
    return pairs + [block(g) for g in groups[3:]]


def unit_of(embedded):
    inverse = lax.rsqrt(jnp.sum(embedded * embedded, axis=1, keepdims=True) + EPS)
    return embedded * inverse, inverse


def norm_back(unit_grad, embedded):
    unit, inverse = unit_of(embedded)
    return inverse * (unit_grad - unit * jnp.sum(unit * unit_grad, axis=1, keepdims=True))


def flat(ref):
    return ref[...].reshape(-1, ref.shape[-1])


def factors(scale, bias, txt, img):
    affinity = lax.dot_general(txt, img, (((1,), (1,)), ((), ())), preferred_element_type=F32)
    logits = scale * affinity + bias
    return logits, (scale / (1.0 + jnp.exp(-logits))).astype(BF16)


def product(first, second):
    return jnp.dot(first, second, preferred_element_type=F32)


def pair_call(name, body, outs, scale, bias, arrays, flops, limit, scratch=()):
    smem = pl.BlockSpec(memory_space=pltpu.SMEM)
    vmem = pl.BlockSpec(memory_space=pltpu.VMEM)
    moved = sum(a.size * a.dtype.itemsize for a in list(arrays) + outs)
    return pl.pallas_call(
        body,
        in_specs=[smem, smem] + [vmem] * len(arrays),
        out_shape=outs,
        scratch_shapes=list(scratch),
        compiler_params=pltpu.CompilerParams(vmem_limit_bytes=limit * MIB),
        cost_estimate=pl.CostEstimate(flops=flops, bytes_accessed=moved, transcendentals=0),
        name=name,
    )(scale, bias, *arrays)


def image_rows(image_refs, image_all):
    own = image_all.shape[0] // 8
    for k, part in enumerate(near_far_order(grouped(image_refs, 2))):
        image_all[k * own : (k + 1) * own] = part


def factor_rows(scale, bias, texts, image_all, factor_all, flipped, tile, unroll):
    def images_at(here):
        factor = factors(scale, bias, flat(texts), image_all[here])[1]
        factor_all[:, here] = factor
        flipped[here] = factor.T

    tiles(image_all.shape[0] // tile, tile, images_at, unroll)


def match(scale, bias, texts, image_all, factor_all, flipped):
    own = texts.shape[1]
    logits = factors(scale, bias, texts[0], image_all[:own])[0]
    row = lax.broadcasted_iota(jnp.int32, logits.shape, 0)
    column = lax.broadcasted_iota(jnp.int32, logits.shape, 1)
    pull = (-scale / (1.0 + jnp.exp(logits))).astype(BF16)
    factor = jnp.where(row == column, pull, factor_all[:own, :own])
    factor_all[:own, :own] = factor
    flipped[:own, :own] = factor.T


def text_grads(factor_all, image_all, out, tile=512, unroll=False):
    def columns_at(here):
        grads = product(factor_all[...], image_all[:, here]).astype(BF16)
        out[:, :, here] = grads.reshape(*out.shape[:2], tile)

    tiles(out.shape[-1] // tile, tile, columns_at, unroll)


def pairs_even(scale, bias, texts, images):
    count, own, width = texts.shape
    rows = count * own

    def body(scale_ref, bias_ref, texts, *refs):
        image_refs, (factor_all, flipped, image_all) = refs[:10], refs[10:]
        image_rows(image_refs, image_all)
        scale, bias = scale_ref[0], bias_ref[0]
        factor_rows(scale, bias, texts, image_all, factor_all, flipped, 512, False)
        match(scale, bias, texts, image_all, factor_all, flipped)

    outs = [shape(rows, rows), shape(rows, rows), shape(rows, width)]
    return pair_call("pairs_even", body, outs, scale, bias, (texts, *images), 2 * rows * rows * width, 24)


def pairs_odd(scale, bias, texts, image_all, after):
    count, own, width = texts.shape
    rows = count * own

    def body(scale_ref, bias_ref, texts, image_all, _, flipped, out, factor_all):
        factor_rows(scale_ref[0], bias_ref[0], texts, image_all, factor_all, flipped, 256, True)
        text_grads(factor_all, image_all, out, 256, True)

    outs = [shape(rows, rows), shape(count, own, width)]
    scratch = [pltpu.VMEM((rows, rows), BF16)]
    arrays = (texts, image_all, after)
    return pair_call("pairs_odd", body, outs, scale, bias, arrays, 4 * rows * rows * width, 24, scratch)


def pairs_image(name, flips, texts, start, stop, outs, after, tile, unroll):
    own, width = texts[0].shape[-2:]

    def body(flip_even, flip_odd, even, odd, *out_refs):
        def columns_at(here):
            factor = jnp.concatenate([flip_even[start:stop], flip_odd[start:stop]], axis=1)
            rows = jnp.concatenate([ref[:, :, here].reshape(-1, tile) for ref in (even, odd)], axis=0)
            total = product(factor, rows).astype(BF16)
            place = 0
            for ref in out_refs:
                size = ref.size // width
                ref[..., here] = total[place : place + size].reshape(*ref.shape[:-1], tile)
                place += size

        tiles(width // tile, tile, columns_at, unroll)

    flops = 2 * (stop - start) * 16 * own * width
    return call(name, body, outs, (*flips, *texts), flops, 24, after)


def weight_part(name, column, place, pieces, halves, feat, after, more=0):
    count, width = len(pieces), pieces[-1].shape[-1]
    rows, features = feat.shape
    own = rows // 8
    strip = width // 16
    tile = 256

    def body(column_ref, place_ref, *refs):
        feat_ref, same, other, flipped, moved, result = refs[count:]
        for n, part in enumerate(near_far_order(grouped(refs[:count], halves))):
            k = NEAR_FAR[n]
            flipped[:, k * own : (k + 1) * own] = part.T
        def features_at(here):
            for k in range(rows // own):
                start = pl.multiple_of((column_ref[0] ^ k) * own, own)
                moved[k * own : (k + 1) * own] = feat_ref[pl.ds(start, own), here]
            result[...] = product(flipped[...], moved[...]).astype(BF16)
            for j, k in enumerate((0, 2, 4, 6, 12, 14, 8, 10)):
                mine = pl.multiple_of((place_ref[0] ^ k) * strip, strip)
                theirs = pl.multiple_of((place_ref[0] ^ (k + 1)) * strip, strip)
                same[j, :, here] = result[pl.ds(mine, strip)]
                other[j, :, here] = result[pl.ds(theirs, strip)]

        tiles(features // tile, tile, features_at, True)

    smem, vmem = pl.BlockSpec(memory_space=pltpu.SMEM), pl.BlockSpec(memory_space=pltpu.VMEM)
    specs = [smem, smem] + [vmem] * (len(pieces) + 1)
    scratch = [
        pltpu.VMEM((width, rows), BF16),
        pltpu.VMEM((rows, tile), BF16),
        pltpu.VMEM((width, tile), BF16),
    ]
    outs = [shape(8, strip, features)] * 2
    flops = 2 * rows * width * features + more
    return call(name, body, outs, (column, place, *pieces, feat), flops, 16, after, specs, scratch)


def feature_grad(name, column, pieces, halves, weight):
    count, width = len(pieces), pieces[-1].shape[-1]
    features = weight.shape[0]
    own = pieces[0].shape[1] * halves
    rows = 8 * own
    tile = 256

    def body(column_ref, *refs):
        weight_ref, out = refs[count:]
        def features_at(here):
            egrad = jnp.concatenate(near_far_order(grouped(refs[:count], halves)), axis=0)
            result = lax.dot_general(
                egrad, weight_ref[here], (((1,), (1,)), ((), ())), preferred_element_type=F32
            ).astype(BF16)
            for n, k in enumerate(NEAR_FAR):
                start = pl.multiple_of((column_ref[0] ^ k) * own, own)
                out[pl.ds(start, own), here] = result[n * own : (n + 1) * own]

        tiles(features // tile, tile, features_at)

    smem, vmem = pl.BlockSpec(memory_space=pltpu.SMEM), pl.BlockSpec(memory_space=pltpu.VMEM)
    outs, ins = [shape(rows, features)], (column, *pieces, weight)
    return call(name, body, outs, ins, 2 * rows * width * features, 16, None, [smem] + [vmem] * (len(pieces) + 1))[0]


def chip_weight(name, same, other, after=None):
    strip, features = same.shape[1:]

    def body(same, got, *outs):
        for j, out in enumerate(outs):
            out[...] = (wide(same, slice(2 * j, 2 * j + 2)) + wide(got, slice(2 * j, 2 * j + 2))).astype(BF16)

    outs = [shape(2, strip, features)] * 4
    return call(name, body, outs, (same, swap(other, "blk", 1)), after=after)


def sum_weight(p02, p46, p1214, p810):
    strip, features = p02.shape[1:]

    def along_z(p02, p46, p1214, p810, p0_out, p2_out):
        total = wide(p02) + wide(p46) + wide(p1214) + wide(p810)
        p0_out[...] = total[0]
        p2_out[...] = total[1].astype(BF16)

    def along_y(p0, p2, out):
        out[...] = p0[...] + wide(p2)

    p46, p1214, p810 = swap(p46, "blk", 4), swap(p1214, "blk", 12), swap(p810, "blk", 8)
    outs = [shape(strip, features, dtype=F32), shape(strip, features)]
    p0, p2 = call("weight_z", along_z, outs, (p02, p46, p1214, p810))
    p2 = swap(p2, "blk", 2)
    return call("weight_y", along_y, outs[:1], (p0, p2))[0].T


def chip_weight_y(name, same, other, after=None):
    strip, features = same.shape[1:]

    def body(same, got, mine, theirs):
        for j in range(4):
            for k, out in enumerate((mine, theirs)):
                out[j] = (wide(same, 2 * j + k) + wide(got, 2 * j + k)).astype(BF16)

    outs = [shape(4, strip, features)] * 2
    return call(name, body, outs, (same, swap(other, "blk", 1)), after=after)


def sum_weight_y(mine, theirs):
    strip, features = mine.shape[1:]
    one = (strip, features)

    def along_y(mine, got, p0, p4, p12, p8):
        p0[...] = wide(mine, 0) + wide(got, 0)
        for j, out in ((1, p4), (2, p12), (3, p8)):
            out[...] = (wide(mine, j) + wide(got, j)).astype(BF16)

    def along_z(p0, p4, p12, p8, out):
        out[...] = p0[...] + wide(p4) + wide(p12) + wide(p8)

    outs = [shape(*one, dtype=F32)] + [shape(*one)] * 3
    p0, p4, p12, p8 = call("weight_image_y", along_y, outs, (mine, swap(theirs, "blk", 2)), ORDER_COST * 2 // 5)
    p4, p12, p8 = swap(p4, "blk", 4), swap(p12, "blk", 12), swap(p8, "blk", 8)
    return call("weight_image_z", along_z, outs[:1], (p0, p4, p12, p8))[0].T, p0


def local(img_feat, txt_feat, img_weight, txt_weight, natural_exponent_multiplier, bias):
    scale = jnp.exp(natural_exponent_multiplier)
    blocks = lax.axis_size("mp")
    column = lax.axis_index("mp").astype(jnp.int32)[None]
    place = lax.axis_index("blk").astype(jnp.int32)[None]
    own = img_feat.shape[0] // blocks
    width = img_weight.shape[1]
    one, two = (own, width), (2, own, width)

    half = (2, own // 2, width)
    own_half = (own // 2, width)

    t01, t23, t67, t4, t5 = embed("embed_text", txt_feat, txt_weight, column, blocks)
    t4, t5 = swap(t4, "mp", 6), swap(t5, "mp", 2)
    i01, i23, i67, i4, i5 = embed("embed_image", img_feat, img_weight, column, blocks)
    t23, t67 = call("relay_text", relay_add, [shape(*two)] * 2, (t23, t67, t4, t5))
    t23, t67 = swap(t23, "mp", 2), swap(t67, "mp", 6)
    i4, i5 = swap(i4, "mp", 6), swap(i5, "mp", 2)

    def second(t01, t23, t67, t0_out, t1_out):
        t0_out[...] = wide(t01, 0) + wide(t23, 0) + wide(t67, 0)
        t1_out[...] = (wide(t01, 1) + wide(t23, 1) + wide(t67, 1)).astype(BF16)

    t0, t1 = call("sums_second", second, [shape(*one, dtype=F32), shape(*one)], (t01, t23, t67))
    t1_got = swap(t1, "mp", 1)
    sent = call("relay_image", relay_split, [shape(*half)] * 4, (i23, i67, i4, i5), after=t1)
    got = [(swap(sent[2 * h], "mp", 2), swap(sent[2 * h + 1], "mp", 6)) for h in range(2)]

    def third(t0, t1, text_out, unit_out):
        embedded = t0[...] + wide(t1)
        text_out[...] = embedded
        unit_out[...] = unit_of(embedded)[0].astype(BF16)

    txt_emb, a0 = call("sums_third", third, [shape(*one, dtype=F32), shape(*one)], (t0, t1_got), after=sent[0])
    a2 = swap(a0, "blk", 2)
    (x_a,) = call("image_x_a", add_half(0), [shape(*half)], (i01, *got[0]), after=a0)
    y_a = swap(x_a, "mp", 1)
    (a02,) = call("stack_text", stack, [shape(*two)], (a0, a2), after=x_a)
    a46, a1214 = swap(a02, "blk", 4), swap(a02, "blk", 12)
    (x_b,) = call("image_x_b", add_half(1), [shape(*half)], (i01, *got[1]), after=a02)
    y_b = swap(x_b, "mp", 1)
    outs = [shape(*half, dtype=F32), shape(*half)]
    emb_a, u01_a = call("image_unit_a", norm_half, outs, (x_a, y_a), after=x_b)
    u23_a, u67_a = swap(u01_a, "mp", 2), swap(u01_a, "mp", 6)
    emb_b, u01_b = call("image_unit_b", norm_half, outs, (x_b, y_b), after=u01_a)
    u23_b, u67_b = swap(u01_b, "mp", 2), swap(u01_b, "mp", 6)
    outs = [shape(*own_half)] * 2
    u2_a, u7_a = call("cut_image_a", cut, outs, (u23_a, u67_a), after=u01_b)
    u4_a, u5_a = swap(u2_a, "mp", 6), swap(u7_a, "mp", 2)
    a4, a14 = call("cut_text", cut, [shape(*one)] * 2, (a46, a1214), after=u2_a)
    a8, a10 = swap(a4, "blk", 12), swap(a14, "blk", 4)
    u2_b, u7_b = call("cut_image_b", cut, outs, (u23_b, u67_b), after=a4)
    u4_b, u5_b = swap(u2_b, "mp", 6), swap(u7_b, "mp", 2)

    def collect(a02, a46, a1214, a8, a10, out):
        for k, ref in enumerate((a02, a46, a1214)):
            out[2 * k : 2 * k + 2] = ref[...]
        out[6] = a8[...]
        out[7] = a10[...]

    (even,) = call("collect", collect, [shape(8, *one)], (a02, a46, a1214, a8, a10), after=(u4_a, u5_a, u4_b, u5_b))
    odd = swap(even, "blk", 1)
    images = (u01_a, u01_b, u23_a, u23_b, u67_a, u67_b, u4_a, u4_b, u5_a, u5_b)
    factor_even, flip_even, image_all = pairs_even(scale, bias, even, images)
    flip_odd, odd_sum = pairs_odd(scale, bias, odd, image_all, flip_even)
    odd_got = swap(odd_sum, "blk", 1)
    flips, texts = (flip_even, flip_odd), (even, odd)
    g4, g5 = pairs_image("pairs_far_images", flips, texts, 6 * own, 8 * own, [shape(*one)] * 2, odd_sum, 256, True)
    g4_got, g5_got = swap(g4, "mp", 6), swap(g5, "mp", 2)
    flops = 128 * own * own * width
    (even_sum,) = call("text_grads_even", text_grads, [shape(8, *one)], (factor_even, image_all), flops, 20, g4)

    def fifth(even, got, p8, p10):
        p8[...] = (wide(even, 6) + wide(got, 6)).astype(BF16)
        p10[...] = (wide(even, 7) + wide(got, 7)).astype(BF16)

    p8, p10 = call("sums_fifth", fifth, [shape(*one)] * 2, (even_sum, odd_got))
    g01, g23, g67 = pairs_image("pairs_near_images", flips, texts, 0, 6 * own, [shape(*two)] * 3, p8, 512, False)
    p8_got, p10_got = swap(p8, "blk", 12), swap(p10, "blk", 4)
    sent = call("relay_image_grads", relay_split, [shape(*half)] * 4, (g23, g67, g4_got, g5_got))
    got = [(swap(sent[2 * h], "mp", 2), swap(sent[2 * h + 1], "mp", 6)) for h in range(2)]

    def sixth(even, got, p8, p10, p02, p46, p1214):
        for k in range(2):
            p02[k] = (wide(even, k) + wide(got, k)).astype(BF16)
        p46[0] = (wide(even, 2) + wide(got, 2) + wide(p8)).astype(BF16)
        p46[1] = (wide(even, 3) + wide(got, 3)).astype(BF16)
        p1214[0] = (wide(even, 4) + wide(got, 4)).astype(BF16)
        p1214[1] = (wide(even, 5) + wide(got, 5) + wide(p10)).astype(BF16)

    outs = [shape(*two)] * 3
    p02, p46, p1214 = call("sums_sixth", sixth, outs, (even_sum, odd_got, p8_got, p10_got), after=sent[0])
    p46, p1214 = swap(p46, "blk", 4), swap(p1214, "blk", 12)
    (x_a,) = call("image_grads_x_a", add_half(0), [shape(*half)], (g01, *got[0]), ORDER_COST * 3 // 10, after=p02)
    y_a = swap(x_a, "mp", 1)
    (x_b,) = call("image_grads_x_b", add_half(1), [shape(*half)], (g01, *got[1]), after=x_a)
    y_b = swap(x_b, "mp", 1)
    def seventh(p02, p46, p1214, p0_out, p2_out):
        p0_out[...] = wide(p02, 0) + wide(p46, 0) + wide(p1214, 0)
        p2_out[...] = (wide(p02, 1) + wide(p46, 1) + wide(p1214, 1)).astype(BF16)

    outs = [shape(*one, dtype=F32), shape(*one)]
    p0, p2 = call("sums_seventh", seventh, outs, (p02, p46, p1214), after=x_b)
    p2_got = swap(p2, "blk", 2)
    (e01_a,) = call("image_back_a", back_half, [shape(*half)], (x_a, y_a, emb_a), after=p2)
    e23_a, e67_a, e45_a = swap(e01_a, "mp", 2), swap(e01_a, "mp", 6), swap(e01_a, "mp", 4)

    def text_back(p0, p2, txt_emb, out):
        out[...] = norm_back(p0[...] + wide(p2), txt_emb[...]).astype(BF16)

    (d0,) = call("text_back", text_back, [shape(*one)], (p0, p2_got, txt_emb), after=e01_a)
    d1 = swap(d0, "mp", 1)
    (e01_b,) = call("image_back_b", back_half, [shape(*half)], (x_b, y_b, emb_b), after=d0)
    e23_b, e67_b = swap(e01_b, "mp", 2), swap(e01_b, "mp", 6)
    e2_b, e7_b = call("cut_image_grads", cut, [shape(*own_half)] * 2, (e23_b, e67_b))
    e4_b, e5_b = swap(e2_b, "mp", 6), swap(e7_b, "mp", 2)
    (e45_b,) = call("stack_image_grads", stack, [shape(*half)], (e4_b, e5_b))

    (d01,) = call("stack_text_grads", stack, [shape(*two)], (d0, d1), after=(e01_b, e23_a, e67_a, e45_a))
    d23, d67 = swap(d01, "mp", 2), swap(d01, "mp", 6)

    e_all = (e01_a, e01_b, e23_a, e23_b, e67_a, e67_b, e45_a, e45_b)
    same, other = weight_part("weight_image", column, place, e_all, 2, img_feat, d01)
    d2, d7 = call("cut_text_grads", cut, [shape(*one)] * 2, (d23, d67), ORDER_COST, after=same)
    d4, d5 = swap(d2, "mp", 6), swap(d7, "mp", 2)
    image_chip = chip_weight_y("weight_image_chip", same, other)
    img_weight_grad, image_y = sum_weight_y(*image_chip)
    d_all = (d01, d23, d67, d4, d5)
    same, other = weight_part("weight_text", column, place, d_all, 1, txt_feat, image_chip[0])
    txt_weight_grad = sum_weight(*chip_weight("weight_text_chip", same, other, image_y))
    return (
        feature_grad("feature_image", column, e_all, 2, img_weight),
        feature_grad("feature_text", column, d_all, 1, txt_weight),
        img_weight_grad,
        txt_weight_grad,
    )


def solution(mesh):
    return jax.shard_map(
        local,
        mesh=mesh,
        in_specs=(P("blk", "mp"), P("blk", "mp"), P("mp", None), P("mp", None), P(), P()),
        out_specs=(P("blk", "mp"), P("blk", "mp"), P("mp", "blk"), P("mp", "blk")),
        check_vma=False,
    )
```
